32 devices in a mesh: narrow: 4 (over y, x), wide: 8 (over z, core).
Axes of the slice: x: 2, y: 2, z: 4, core: 2. Of those that a mesh axis runs over, the one named last changes fastest.
Arguments:
- tokens: bfloat16 [8192, 768], P(('narrow', 'wide')), may hold values from -6 to 6
- cotangent: bfloat16 [8192, 768], P(('narrow', 'wide')), may hold values from -6 to 6
- w_query: bfloat16 [768, 768], replicated, may hold values from -0.21875 to 0.21875
- w_key: bfloat16 [768, 768], replicated, may hold values from -0.21875 to 0.21875
- w_value: bfloat16 [768, 768], replicated, may hold values from -0.21875 to 0.21875
- w_output: bfloat16 [768, 768], replicated, may hold values from -1.25 to 1.25
- gain_attn: float32 [768], replicated, may hold values from 0.5 to 1.5
- gain_ffn: float32 [768], replicated, may hold values from 0.5 to 1.5
- w_router: bfloat16 [768, 8], replicated, may hold values from -0.109375 to 0.109375
- bias_table: float32 [32, 12], replicated, may hold values from -4 to 4
- expert_in: bfloat16 [8, 768, 3072], P('wide', None, 'narrow'), may hold values from -0.21875 to 0.21875
- expert_out: bfloat16 [8, 3072, 768], P('wide', 'narrow'), may hold values from -1.75 to 1.75
- choices: int32 [8192, 1], P(('narrow', 'wide')), may hold values from 0 to 7
- router_levels: int32 [8], replicated, may hold values from 0 to 3
- buckets: int32 [511], replicated, may hold values from 0 to 31
Outputs:
- layer_output: bfloat16 [8192, 768], P(('narrow', 'wide'))
- input_grad: bfloat16 [8192, 768], P(('narrow', 'wide'))
- grad_w_query: float32 [768, 768], replicated
- grad_w_key: float32 [768, 768], replicated
- grad_w_value: float32 [768, 768], replicated
- grad_w_output: float32 [768, 768], replicated
- grad_gain_attn: float32 [768], replicated
- grad_gain_ffn: float32 [768], replicated
- grad_w_router: float32 [768, 8], replicated
- grad_bias_table: float32 [32, 12], replicated
- grad_expert_in: float32 [8, 768, 3072], P('wide', None, 'narrow')
- grad_expert_out: float32 [8, 3072, 768], P('wide', 'narrow')
The draws below stay inside these ranges and needn't reach their ends.
All inputs are finite; a program needn't handle non-finite values.
Results may differ from the reference program's by a relative error of at most 0.018.
Values may be sent and summed in bfloat16 or wider, within the bound.
No kernel may reach another device: no remote copies, remote signals or barrier semaphores. Data moves between devices by JAX's collectives and lax.ppermute only.
A program may use at most 128 MiB of HBM per device.

```python
import jax
import jax.numpy as jnp
from jax import lax

D = 768
HEADS = 12
HEAD = 64
FF = 3072
NB = 32
TOK_DEV = 256
EXPERTS = 8
CAP = 40
TOKENS = 8192
N_NARROW = 4
N_WIDE = 8


def set_ends(array, own_key, low, high):
    place = [jax.random.randint(jax.random.fold_in(own_key, axis), (), 0, length) for axis, length in enumerate(array.shape)]
    longest = array.shape.index(max(array.shape))
    neighbour = place[:longest] + [(place[longest] + 1) % array.shape[longest]] + place[longest + 1:]
    return array.at[tuple(place)].set(low).at[tuple(neighbour)].set(high)


def shard_levels(stream_key, dims, cuts, smallest, largest):
    level = 1.0
    for axis_at, shards_of in cuts:
        draws = jax.random.uniform(jax.random.fold_in(jax.random.fold_in(stream_key, 6), axis_at), (shards_of,), jnp.float32, smallest / len(cuts), largest / len(cuts))
        level = level * jnp.repeat(jnp.exp(draws), dims[axis_at] // shards_of).reshape((-1,) + (1,) * (len(dims) - 1 - axis_at))
    return level


def choose_distinct(own_key, rows, amount, top, lift):
    ranking = jax.random.permutation(jax.random.fold_in(own_key, 1), amount)
    favour = ranking
    for power in range(3):
        favour = favour * favour // amount
    favour = favour * lift // amount
    lots = jax.random.randint(jax.random.fold_in(own_key, 2), (rows, amount), 0, 4096) + favour
    holders = jax.random.permutation(jax.random.fold_in(own_key, 3), rows)[jnp.arange(amount) % rows]
    lots = jnp.where(jnp.arange(rows)[:, None] == holders[None, :], 1 << 14, lots)
    score = lots * amount + jnp.arange(amount)
    return lax.top_k(score.astype(jnp.int32), top)[1].astype(jnp.int32)


def normal_values(stream_key, extent, scale, limit, split=(), kind=jnp.bfloat16):
    level = shard_levels(stream_key, extent, split, -0.22, 0.18) if split else 1.0
    array = jax.random.normal(stream_key, extent, jnp.float32) * scale * level
    return jnp.minimum(jnp.maximum(array, -limit), limit).astype(kind)


def setup_inputs(seed: int = 0) -> dict:
    key_of = jax.random.split(jax.random.key(seed), 16)
    return {
        "tokens": normal_values(key_of[0], (TOKENS, D), 1.0, 6.0, ((0, 32),)),
        "cotangent": normal_values(key_of[1], (TOKENS, D), 1.0, 6.0, ((0, 32),)),
        "w_query": normal_values(key_of[2], (D, D), D ** -0.5, 0.21875),
        "w_key": normal_values(key_of[3], (D, D), D ** -0.5, 0.21875),
        "w_value": normal_values(key_of[4], (D, D), D ** -0.5, 0.21875),
        "w_output": normal_values(key_of[5], (D, D), (D // 32) ** -0.5, 1.25),
        "gain_attn": jnp.clip(1.0 + 0.1 * jax.random.normal(key_of[6], (D,), jnp.float32), 0.5, 1.5),
        "gain_ffn": jnp.clip(1.0 + 0.1 * jax.random.normal(key_of[7], (D,), jnp.float32), 0.5, 1.5),
        "w_router": normal_values(key_of[8], (D, EXPERTS), (4 * D) ** -0.5, 0.109375),
        "bias_table": normal_values(key_of[9], (NB, HEADS), 1.0, 4.0, (), jnp.float32),
        "expert_in": normal_values(key_of[10], (EXPERTS, D, FF), D ** -0.5, 0.21875, ((0, 8), (2, 4))),
        "expert_out": normal_values(key_of[11], (EXPERTS, FF, D), (2 * EXPERTS * FF ** -0.5), 1.75, ((0, 8), (1, 4))),
        "choices": choose_distinct(key_of[12], TOKENS, EXPERTS, 1, 2048),
        "router_levels": set_ends(jax.random.randint(key_of[13], (EXPERTS,), 0, 4), jax.random.fold_in(key_of[13], 1), 0, 3).astype(jnp.int32),
        "buckets": set_ends(jax.random.randint(key_of[14], (2 * TOK_DEV - 1,), 0, NB), jax.random.fold_in(key_of[14], 1), 0, NB - 1).astype(jnp.int32),
    }


epsilon = 1e-06

@jax.custom_vjp
def low(v):
    return lax.optimization_barrier(v.astype(jnp.bfloat16)).astype(jnp.float32)

@jax.custom_vjp
def low_back(v):
    return v

def low_keep(v):
    return (low(v), None)

def low_pass(kept, grad):
    return (grad,)

def back_keep(v):
    return (v, None)

def back_low(kept, grad):
    return (low(grad),)
low.defvjp(low_keep, low_pass)
low_back.defvjp(back_keep, back_low)

def high_dot(left, right):
    return jnp.dot(left, right, precision=lax.Precision.HIGHEST)

def rms_norm(rows, gain):
    return rows * lax.rsqrt(lax.optimization_barrier(jnp.mean(rows * rows, axis=-1, keepdims=True)) + epsilon) * gain

def reference(tokens, cotangent, w_query, w_key, w_value, w_output, gain_attn, gain_ffn, w_router, bias_table, expert_in, expert_out, choices, router_levels, buckets):
    devices = N_NARROW * N_WIDE
    chosen = choices[:, 0].reshape(devices, TOK_DEV)
    chosen_mask = chosen[:, :, None] == jnp.arange(EXPERTS, dtype=jnp.int32)[None, None, :]
    counts = jnp.cumsum(chosen_mask.astype(jnp.int32), axis=1)
    position = lax.optimization_barrier(jnp.sum(jnp.where(chosen_mask, counts, 0), axis=2)) - 1
    kept_mask = position < CAP
    device_ids = jnp.arange(devices, dtype=jnp.int32)[:, None]
    slot_of = (chosen * devices + device_ids) * CAP + jnp.minimum(position, CAP - 1)
    flat_slots = EXPERTS * devices * CAP
    target = jnp.where(kept_mask, slot_of, flat_slots).reshape(-1)
    token_of = jnp.zeros((flat_slots,), jnp.int32).at[target].set(jnp.arange(TOKENS, dtype=jnp.int32), mode='drop')
    filled = jnp.zeros((flat_slots,), jnp.float32).at[target].set(1.0, mode='drop')
    slot_of = slot_of.reshape(-1)
    kept_value = kept_mask.reshape(-1).astype(jnp.float32)
    chosen_flat = chosen_mask.reshape(TOKENS, EXPERTS)
    offsets = jnp.arange(TOK_DEV, dtype=jnp.int32)[None, :] - jnp.arange(TOK_DEV, dtype=jnp.int32)[:, None] + (TOK_DEV - 1)
    bucket_grid = buckets[offsets]
    levels = 0.25 * router_levels.astype(jnp.float32)
    scale = HEAD ** (-0.5)

    def forward(inputs, wq, wk, wv, wo, gone, gtwo, wr, table, w_in, w_out):
        score_bias = jnp.transpose(table[bucket_grid], (2, 0, 1))

        def attend(rows):
            normed = low(rms_norm(rows, gone))
            query_rows = low_back(low(high_dot(normed, wq))).reshape(TOK_DEV, HEADS, HEAD)
            key_rows = low_back(low(high_dot(normed, wk))).reshape(TOK_DEV, HEADS, HEAD)
            value_rows = low_back(low(high_dot(normed, wv))).reshape(TOK_DEV, HEADS, HEAD)
            scores = jnp.einsum('ihd,jhd->hij', query_rows, key_rows, precision=lax.Precision.HIGHEST) * scale + score_bias
            scores = low_back(scores)
            shifted = scores - lax.optimization_barrier(jnp.max(scores, axis=-1, keepdims=True))
            exp_scores = jnp.exp(shifted)
            probs = exp_scores / lax.optimization_barrier(jnp.sum(exp_scores, axis=-1, keepdims=True))
            mixed = jnp.einsum('hij,jhd->ihd', low(probs), value_rows, precision=lax.Precision.HIGHEST).reshape(TOK_DEV, D)
            mixed = low_back(low(mixed))
            return rows + low_back(high_dot(mixed, wo))
        residual = lax.map(jax.checkpoint(attend), inputs.reshape(devices, TOK_DEV, D)).reshape(TOKENS, D)
        normed_two = low(rms_norm(residual, gtwo))
        logits = low_back(high_dot(normed_two, wr)) + levels[None, :]
        logit_shift = logits - lax.optimization_barrier(jnp.max(logits, axis=1, keepdims=True))
        logit_exp = jnp.exp(logit_shift)
        router_probs = logit_exp / lax.optimization_barrier(jnp.sum(logit_exp, axis=1, keepdims=True))
        gate_value = lax.optimization_barrier(jnp.sum(jnp.where(chosen_flat, router_probs, 0.0), axis=1))
        sent = low_back(jnp.take(normed_two, token_of, axis=0) * filled[:, None]).reshape(EXPERTS, devices * CAP, D)

        def expert(pieces):
            rows, weight_in, weight_out = pieces
            pre_act = low_back(high_dot(rows, weight_in))
            hidden = low(jax.nn.gelu(pre_act, approximate=True))
            return low_back(low(high_dot(hidden, weight_out)))
        result = lax.map(jax.checkpoint(expert), (sent, w_in, w_out)).reshape(flat_slots, D)
        picked = jnp.take(result, slot_of, axis=0)
        return residual + (gate_value * kept_value)[:, None] * picked
    floats = (tokens, w_query, w_key, w_value, w_output, gain_attn, gain_ffn, w_router, bias_table, expert_in, expert_out)
    floats = tuple((item.astype(jnp.float32) for item in floats))
    result, pull = jax.vjp(forward, *floats)
    grads = pull(cotangent.astype(jnp.float32))
    return (result.astype(jnp.bfloat16), grads[0].astype(jnp.bfloat16), grads[1], grads[2], grads[3], grads[4], grads[5], grads[6], grads[7], grads[8], grads[9], grads[10])
```

```python
import functools

import jax
import jax.numpy as jnp
from jax import lax
from jax.experimental import pallas as pl
from jax.experimental.pallas import tpu as pltpu
from jax.sharding import PartitionSpec as P

epsilon = 1e-06
BF = jnp.bfloat16
F32 = jnp.float32
VMEM_LIMIT = 56 * 2**20


def mm(a, b):
    return lax.dot_general(a, b, (((1,), (0,)), ((), ())), preferred_element_type=F32)


def mm_nt(a, b):
    return lax.dot_general(a, b, (((1,), (1,)), ((), ())), preferred_element_type=F32)


def mm_tn(a, b):
    return lax.dot_general(a, b, (((0,), (0,)), ((), ())), preferred_element_type=F32)


def rms_scale(rows):
    return lax.rsqrt(jnp.mean(rows * rows, axis=-1, keepdims=True) + epsilon)


def half_masks(rows, width):
    lane = lax.broadcasted_iota(jnp.int32, (rows, width), 1)
    low = (lane < width // 2).astype(F32)
    return low.astype(BF), (1.0 - low).astype(BF)


def call(kernel, outs, *args, flops=0, transcendentals=0, scratch=(), smem=0):
    out_bytes = sum(o.size * o.dtype.itemsize for o in outs)
    in_bytes = sum(a.size * a.dtype.itemsize for a in args)
    specs = [pl.BlockSpec(memory_space=pltpu.SMEM)] * smem
    specs += [pl.BlockSpec(memory_space=pltpu.VMEM)] * (len(args) - smem)
    return pl.pallas_call(
        kernel,
        out_shape=tuple(outs),
        in_specs=specs,
        out_specs=tuple(pl.BlockSpec(memory_space=pltpu.VMEM) for _ in outs),
        scratch_shapes=list(scratch),
        compiler_params=pltpu.CompilerParams(vmem_limit_bytes=VMEM_LIMIT),
        cost_estimate=pl.CostEstimate(
            flops=flops, transcendentals=transcendentals, bytes_accessed=in_bytes + out_bytes
        ),
    )(*args)


def shaped(shape, dtype=BF):
    return jax.ShapeDtypeStruct(shape, dtype)


def front_kernel(
    heads,
    cap,
    tokens,
    cotangent,
    w_query,
    w_key,
    w_value,
    w_output,
    gain_attn,
    gain_ffn,
    w_router,
    table,
    spread,
    choices,
    levels,
    normed_one_out,
    query_out,
    key_out,
    value_out,
    probs_out,
    mixed_out,
    residual_out,
    normed_two_out,
    router_out,
    target_out,
    slots_out,
    grads_out,
):
    length, width = tokens.shape
    scale = (width // heads) ** (-0.5)
    experts = w_router.shape[1]
    flat_slots = slots_out.shape[0]
    inputs = tokens[...].astype(F32)
    normed = (inputs * rms_scale(inputs) * gain_attn[...]).astype(BF)
    normed_one_out[...] = normed
    query_out[...] = mm(normed, w_query[...]).astype(BF)
    key_out[...] = mm(normed, w_key[...]).astype(BF)
    value_out[...] = mm(normed, w_value[...]).astype(BF)
    buckets_n = table.shape[0]
    onehot = (
        lax.broadcasted_iota(jnp.int32, (buckets_n, 2 * length), 0) == spread[...]
    ).astype(F32)
    by_offset = lax.dot_general(
        table[...],
        onehot,
        (((0,), (0,)), ((), ())),
        precision=lax.Precision.HIGHEST,
        preferred_element_type=F32,
    )
    pair = 2 * width // heads
    masks = half_masks(length, pair)
    for p in range(heads // 2):
        at = slice(p * pair, (p + 1) * pair)
        q2, k2, v2 = query_out[:, at], key_out[:, at], value_out[:, at]
        probs = []
        for half in (0, 1):
            h = 2 * p + half
            base = jnp.broadcast_to(by_offset[h : h + 1, :], (length, 2 * length))
            bias = pltpu.roll(base, 0, 1, stride=1, stride_axis=0)[:, :length]
            scores = mm_nt(q2, k2 * masks[half]) * scale + bias
            e = jnp.exp(scores - jnp.max(scores, axis=-1, keepdims=True))
            e = (e / jnp.sum(e, axis=-1, keepdims=True)).astype(BF)
            probs_out[h] = e
            probs.append(e)
        mixed_out[:, at] = mm(
            jnp.concatenate(probs, axis=1),
            jnp.concatenate([v2 * masks[0], v2 * masks[1]], axis=0),
        ).astype(BF)
    residual = inputs + mm(mixed_out[...], w_output[...])
    residual_out[...] = residual
    normed_two = (residual * rms_scale(residual) * gain_ffn[...]).astype(BF)
    normed_two_out[...] = normed_two
    logits = mm(normed_two, w_router[...]) + 0.25 * levels[...].astype(F32)
    logit_exp = jnp.exp(logits - jnp.max(logits, axis=1, keepdims=True))
    router = logit_exp / jnp.sum(logit_exp, axis=1, keepdims=True)
    router_out[...] = router
    chosen = choices[...]
    mask = chosen == lax.broadcasted_iota(jnp.int32, (length, experts), 1)
    mask_f = mask.astype(F32)
    earlier = (
        lax.broadcasted_iota(jnp.int32, (length, length), 1)
        < lax.broadcasted_iota(jnp.int32, (length, length), 0)
    ).astype(F32)
    counts = mm(earlier.astype(BF), mask_f.astype(BF))
    position = jnp.sum(mask_f * counts, axis=1, keepdims=True).astype(jnp.int32)
    target = jnp.where(position < cap, chosen * cap + position, -1)
    target_out[...] = target
    gate = jnp.sum(mask_f * router, axis=1, keepdims=True)
    place = (target == lax.broadcasted_iota(jnp.int32, (length, flat_slots), 1)).astype(F32)
    place = place.astype(BF)
    slots_out[...] = mm_tn(place, normed_two).astype(BF)
    sent = (gate * cotangent[...].astype(F32)).astype(BF)
    grads_out[...] = mm_tn(place, sent).astype(BF)


def expert_forward_kernel(r0, r1a, r1b, r2a, r2b, r3a, r3b, w_in, w_out, hidden, slope, *outs):
    keep_a, send_a, keep_b, send_b = outs
    half = r1a.shape[0]
    c = 0.7978845608028654
    pieces = (
        (r0[:half], keep_a, 0),
        (r0[half:], keep_b, 0),
        (r1a[...], send_a, 0),
        (r1b[...], keep_b, 1),
        (r2a[...], keep_a, 1),
        (r2b[...], send_b, 0),
        (r3a[...], send_a, 1),
        (r3b[...], send_b, 1),
    )
    for i, (rows, out, slot) in enumerate(pieces):
        pre = mm(rows, w_in[...])
        square = pre * pre
        t = jnp.tanh(c * pre * (1.0 + 0.044715 * square))
        act = (0.5 * pre * (1.0 + t)).astype(BF)
        hidden[i] = act
        slope[i] = (
            0.5 * (1.0 + t) + 0.5 * c * pre * (1.0 - t * t) * (1.0 + 3 * 0.044715 * square)
        ).astype(BF)
        out[slot] = mm(act, w_out[...]).astype(BF)


def expert_backward_kernel(r0, r1a, r1b, r2a, r2b, r3a, r3b, w_in, w_out, slope, grad_pre, *outs):
    keep_a, send_a, keep_b, send_b = outs
    half = r1a.shape[0]
    pieces = (
        (r0[:half], keep_a, 0),
        (r0[half:], keep_b, 0),
        (r1a[...], send_a, 0),
        (r1b[...], keep_b, 1),
        (r2a[...], keep_a, 1),
        (r2b[...], send_b, 0),
        (r3a[...], send_a, 1),
        (r3b[...], send_b, 1),
    )
    for i, (rows, out, slot) in enumerate(pieces):
        g = (mm_nt(rows, w_out[...]) * slope[i].astype(F32)).astype(BF)
        grad_pre[i] = g
        out[slot] = mm_nt(g, w_in[...]).astype(BF)


def expert_weights_kernel(x0, x1, x2, x3, x4, x5, x6, g0, g1, g2, g3, g4, g5, g6, hidden, grad_pre, grad_in, grad_out):
    half = x1.shape[0]
    xs = jnp.concatenate([x0[...], x1[...], x2[...], x3[...], x4[...], x5[...], x6[...]], axis=0)
    gs = jnp.concatenate([g0[...], g1[...], g2[...], g3[...], g4[...], g5[...], g6[...]], axis=0)
    width = grad_in.shape[1]
    act = hidden[...].reshape(8 * half, -1)
    pre = grad_pre[...].reshape(8 * half, -1)
    step = 256
    for i in range(width // step):
        grad_in[0, i * step : (i + 1) * step, :] = mm_tn(xs[:, i * step : (i + 1) * step], pre)
    for i in range(act.shape[1] // step):
        grad_out[0, i * step : (i + 1) * step, :] = mm_tn(act[:, i * step : (i + 1) * step], gs)


def store_halves(core, h, value, keep, send):
    @pl.when(core == h)
    def _():
        keep[...] = value

    @pl.when(core != h)
    def _():
        send[...] = value


def middle_kernel(
    core_ref,
    target,
    choices,
    router,
    normed_two,
    residual_ref,
    cotangent,
    returned,
    returned_grad,
    gain_ffn,
    w_router,
    mixed,
    w_output,
    layer_output,
    grad_residual_out,
    grad_mixed_out,
    keep,
    send,
    grad_gain_out,
    grad_router_out,
):
    core = core_ref[0]
    length, width = residual_ref.shape
    experts = router.shape[1]
    residual = residual_ref[...]
    upstream = cotangent[...].astype(F32)
    goal = target[...]
    place = (
        goal == lax.broadcasted_iota(jnp.int32, (length, returned.shape[0]), 1)
    ).astype(F32)
    place = place.astype(BF)
    picked = mm(place, returned[...])
    kept = (goal >= 0).astype(F32)
    mask = (choices[...] == lax.broadcasted_iota(jnp.int32, (length, experts), 1)).astype(F32)
    probs = router[...]
    gate = jnp.sum(mask * probs, axis=1, keepdims=True)
    layer_output[...] = (residual + gate * kept * picked).astype(BF)
    grad_gate = jnp.sum(upstream * picked, axis=1, keepdims=True) * kept
    grad_logits = ((grad_gate * gate) * (mask - probs)).astype(BF)
    grad_router_out[...] = mm_tn(grad_logits, normed_two[...])
    grad_two = mm(place, returned_grad[...]) + mm_nt(grad_logits, w_router[...])
    scale_two = rms_scale(residual)
    grad_gain_out[...] = jnp.sum(grad_two * residual * scale_two, axis=0, keepdims=True)
    weighted = grad_two * gain_ffn[...]
    grad_residual = (
        upstream
        + scale_two * weighted
        - residual * (scale_two**3 * jnp.mean(weighted * residual, axis=1, keepdims=True))
    )
    grad_residual_out[...] = grad_residual
    grad_attn = grad_residual.astype(BF)
    half = width // 2
    for h in (0, 1):
        value = mm_tn(mixed[:, h * half : (h + 1) * half], grad_attn).astype(BF)
        store_halves(core, h, value, keep, send)
    grad_mixed_out[...] = mm_nt(grad_attn, w_output[...]).astype(BF)


def attention_backward_kernel(
    heads,
    core_ref,
    normed_one,
    query,
    key,
    value,
    probs,
    grad_mixed,
    spread,
    grad_all,
    keep,
    send,
    grad_table,
    stack,
):
    core = core_ref[0]
    length, width = query.shape
    scale = (width // heads) ** (-0.5)
    pair = 2 * width // heads
    masks = half_masks(length, pair)
    for p in range(heads // 2):
        at = slice(p * pair, (p + 1) * pair)
        q2, k2, v2, g2 = query[:, at], key[:, at], value[:, at], grad_mixed[:, at]
        attn, grads = [], []
        for half in (0, 1):
            h = 2 * p + half
            e = probs[h]
            attn.append(e)
            e = e.astype(F32)
            grad_probs = mm_nt(g2, v2 * masks[half])
            gs = e * (grad_probs - jnp.sum(e * grad_probs, axis=-1, keepdims=True))
            stack[h] = gs
            grads.append(gs.astype(BF))
        grad_q = mm(
            jnp.concatenate(grads, axis=1),
            jnp.concatenate([k2 * masks[0], k2 * masks[1]], axis=0),
        )
        grad_k = mm_tn(
            jnp.concatenate(grads, axis=0),
            jnp.concatenate([q2 * masks[0], q2 * masks[1]], axis=0),
        )
        grad_v = mm_tn(
            jnp.concatenate(attn, axis=0),
            jnp.concatenate([g2 * masks[0], g2 * masks[1]], axis=0),
        )
        grad_all[:, p * pair : (p + 1) * pair] = (grad_q * scale).astype(BF)
        grad_all[:, width + p * pair : width + (p + 1) * pair] = (grad_k * scale).astype(BF)
        grad_all[:, 2 * width + p * pair : 2 * width + (p + 1) * pair] = grad_v.astype(BF)
    half = width // 2
    for h in (0, 1):
        value_h = mm_tn(normed_one[:, h * half : (h + 1) * half], grad_all[...]).astype(BF)
        store_halves(core, h, value_h, keep, send)

    blocks = length // 8
    zeros = jnp.zeros((heads * 8, length), F32)

    def block(a):
        rows = stack[:, pl.ds(pl.multiple_of(a * 8, 8), 8), :].reshape(heads * 8, length)
        return jnp.concatenate([rows, zeros], axis=1)

    def step(i, total):
        return block(blocks - 2 - i) + pltpu.roll(total, 2 * length - 8, 1)

    total = lax.fori_loop(0, blocks - 1, step, block(blocks - 1))
    row = lax.broadcasted_iota(jnp.int32, total.shape, 0) % 8
    for bit in (1, 2, 4):
        total = jnp.where((row & bit) != 0, pltpu.roll(total, 2 * length - bit, 1), total)
    by_offset = jnp.sum(total.reshape(heads, 8, 2 * length), axis=1)
    onehot = (
        lax.broadcasted_iota(jnp.int32, (grad_table.shape[1], 2 * length), 0) == spread[...]
    ).astype(F32)
    grad_table[...] = lax.dot_general(
        by_offset,
        onehot,
        (((1,), (1,)), ((), ())),
        precision=lax.Precision.HIGHEST,
        preferred_element_type=F32,
    )


def input_kernel(
    grad_all,
    w_query,
    w_key,
    w_value,
    tokens,
    gain_attn,
    grad_residual,
    grad_gain_ffn,
    grad_router,
    grad_table,
    input_grad,
    small,
):
    width = tokens.shape[1]
    grad = mm_nt(grad_all[:, :width], w_query[...])
    grad = grad + mm_nt(grad_all[:, width : 2 * width], w_key[...])
    grad = grad + mm_nt(grad_all[:, 2 * width :], w_value[...])
    inputs = tokens[...].astype(F32)
    scale_one = rms_scale(inputs)
    gain_row = jnp.sum(grad * inputs * scale_one, axis=0, keepdims=True)
    weighted = grad * gain_attn[...]
    input_grad[...] = (
        grad_residual[...]
        + scale_one * weighted
        - inputs * (scale_one**3 * jnp.mean(weighted * inputs, axis=1, keepdims=True))
    ).astype(BF)
    experts = grad_router.shape[0]
    heads, buckets_n = grad_table.shape
    small[...] = jnp.zeros_like(small)
    small[0:1, :] = gain_row
    small[8:9, :] = grad_gain_ffn[...]
    small[16 : 16 + experts, :] = grad_router[...]
    small[16 + experts : 16 + experts + heads, :buckets_n] = grad_table[...]


def finish_kernel(place_ref, own_a, own_b, far_a, far_b, *outs):
    core, bit_x, bit_y = place_ref[0], place_ref[1], place_ref[2]
    block = own_a.shape[0] // 4
    columns = own_a.shape[1]
    width = outs[0].shape[1]
    for far, (a, b) in enumerate(((own_a, own_b), (far_a, far_b))):
        for first in (0, 1):
            for second in (0, 1):
                rows = slice((2 * first + second) * block, (2 * first + second + 1) * block)
                top = (core ^ far) * 4
                at_a = (top + (bit_x ^ first) * 2 + (bit_y ^ second)) * block
                at_b = (top + (bit_y ^ first) * 2 + (bit_x ^ second)) * block
                for m, out in enumerate(outs):
                    for source, at, left in ((a, at_a, 0), (b, at_b, columns)):
                        low = max(m * width, left)
                        high = min((m + 1) * width, left + columns)
                        if low < high:
                            out[
                                pl.ds(pl.multiple_of(at, block), block),
                                low - m * width : high - m * width,
                            ] = source[rows, low - left : high - left].astype(F32)


def pairs(size, k):
    return [(i, i ^ k) for i in range(size)]


def local(
    n_narrow,
    n_wide,
    tokens,
    cotangent,
    w_query,
    w_key,
    w_value,
    w_output,
    gain_attn,
    gain_ffn,
    w_router,
    bias_table,
    expert_in,
    expert_out,
    choices,
    router_levels,
    buckets,
):
    length, width = tokens.shape
    heads = bias_table.shape[1]
    buckets_n = bias_table.shape[0]
    experts = w_router.shape[1]
    cap = (5 * length + 4 * experts - 1) // (4 * experts)
    flat_slots = experts * cap
    half = flat_slots // 2
    core = lax.axis_index("wide") % 2
    bit_x = lax.axis_index("narrow") % 2
    bit_y = lax.axis_index("narrow") // 2
    core_ref = core.astype(jnp.int32).reshape(1)
    gain_attn = gain_attn.reshape(1, width)
    gain_ffn = gain_ffn.reshape(1, width)
    spread = jnp.concatenate(
        [buckets[length - 1 :], jnp.zeros((1,), jnp.int32), buckets[: length - 1]]
    ).reshape(1, 2 * length)
    rows_bf = shaped((length, width))
    attn_flops = 4 * length * length * width

    def across(x, k):
        return lax.ppermute(x, "narrow", pairs(n_narrow, k))

    def along(x, k):
        return lax.ppermute(x, "wide", pairs(n_wide, k))

    (
        normed_one,
        query,
        key,
        value,
        probs,
        mixed,
        residual,
        normed_two,
        router,
        target,
        slots,
        slot_grads,
    ) = call(
        functools.partial(front_kernel, heads, cap),
        [
            rows_bf,
            rows_bf,
            rows_bf,
            rows_bf,
            shaped((heads, length, length)),
            rows_bf,
            shaped((length, width), F32),
            rows_bf,
            shaped((length, experts), F32),
            shaped((length, 1), jnp.int32),
            shaped((flat_slots, width)),
            shaped((flat_slots, width)),
        ],
        tokens,
        cotangent,
        w_query,
        w_key,
        w_value,
        w_output,
        gain_attn,
        gain_ffn,
        w_router,
        bias_table,
        spread,
        choices,
        router_levels.reshape(1, experts),
        flops=8 * length * width * width + attn_flops,
        transcendentals=heads * length * length,
    )

    def exchange(x):
        return lax.all_to_all(x, "wide", split_axis=0, concat_axis=0, tiled=True)

    def gather(x):
        a, b = x[:half], x[half:]
        r1a, r2b = across(a, 1), across(b, 2)
        r2a, r1b = across(a, 2), across(b, 1)
        r3a, r3b = across(r1a, 2), across(r2b, 1)
        return (x, r1a, r1b, r2a, r2b, r3a, r3b)

    def reduce(keep_a, send_a, keep_b, send_b):
        got_a, got_b = across(send_a, 1), across(send_b, 2)
        next_a = (keep_a[1].astype(F32) + got_a[1].astype(F32)).astype(BF)
        next_b = (keep_b[1].astype(F32) + got_b[1].astype(F32)).astype(BF)
        last_a, last_b = across(next_a, 2), across(next_b, 1)
        sum_a = keep_a[0].astype(F32) + got_a[0].astype(F32) + last_a.astype(F32)
        sum_b = keep_b[0].astype(F32) + got_b[0].astype(F32) + last_b.astype(F32)
        return jnp.concatenate([sum_a.astype(BF), sum_b.astype(BF)], axis=0)

    w_in = expert_in.reshape(width, -1)
    w_out = expert_out.reshape(-1, width)
    units = w_in.shape[1]
    rows = gather(exchange(slots))
    row_grads = gather(exchange(slot_grads))
    piece = shaped((2, half, width))
    eight = shaped((8, half, units))
    expert_flops = 2 * 8 * half * width * units
    hidden, slope, *partial = call(
        expert_forward_kernel,
        [eight, eight, piece, piece, piece, piece],
        *rows,
        w_in,
        w_out,
        flops=2 * expert_flops,
        transcendentals=8 * half * units,
    )
    returned = exchange(reduce(*partial))
    grad_pre, *partial = call(
        expert_backward_kernel,
        [eight, piece, piece, piece, piece],
        *row_grads,
        w_in,
        w_out,
        slope,
        flops=2 * expert_flops,
    )
    returned_grad = exchange(reduce(*partial))
    grad_expert_in, grad_expert_out = call(
        expert_weights_kernel,
        [shaped(expert_in.shape, F32), shaped(expert_out.shape, F32)],
        *rows,
        *row_grads,
        hidden,
        grad_pre,
        flops=2 * expert_flops,
    )

    (
        layer_output,
        grad_residual,
        grad_mixed,
        output_keep,
        output_send,
        grad_gain_ffn,
        grad_router,
    ) = call(
        middle_kernel,
        [
            rows_bf,
            shaped((length, width), F32),
            rows_bf,
            shaped((width // 2, width)),
            shaped((width // 2, width)),
            shaped((1, width), F32),
            shaped((experts, width), F32),
        ],
        core_ref,
        target,
        choices,
        router,
        normed_two,
        residual,
        cotangent,
        returned,
        returned_grad,
        gain_ffn,
        w_router,
        mixed,
        w_output,
        smem=1,
        flops=4 * length * width * width,
    )
    grad_all, keep, send, grad_table = call(
        functools.partial(attention_backward_kernel, heads),
        [
            shaped((length, 3 * width)),
            shaped((width // 2, 3 * width)),
            shaped((width // 2, 3 * width)),
            shaped((heads, buckets_n), F32),
        ],
        core_ref,
        normed_one,
        query,
        key,
        value,
        probs,
        grad_mixed,
        spread,
        smem=1,
        scratch=[pltpu.VMEM((heads, length, length), F32)],
        flops=6 * length * width * width + 2 * attn_flops,
    )
    small_rows = -(-(16 + experts + heads) // 16) * 16
    input_grad, small = call(
        input_kernel,
        [rows_bf, shaped((small_rows, width), F32)],
        grad_all,
        w_query,
        w_key,
        w_value,
        tokens,
        gain_attn,
        grad_residual,
        grad_gain_ffn,
        grad_router,
        grad_table,
        flops=6 * length * width * width,
    )

    def split(x, bit):
        size = x.shape[0] // 2
        kept = lax.dynamic_slice_in_dim(x, bit * size, size, 0)
        other = lax.dynamic_slice_in_dim(x, (1 - bit) * size, size, 0)
        return kept, other

    def fold(x, bit, move, k):
        kept, other = split(x, bit)
        return (kept.astype(F32) + move(other, k).astype(F32)).astype(BF)

    depth_bits = [k for k in (2**i for i in range(1, 20)) if k < n_wide]
    place = jnp.stack([core, bit_x, bit_y]).astype(jnp.int32)

    def total(keep, send, count):
        x = (keep.astype(F32) + along(send, 1).astype(F32)).astype(BF)
        columns = x.shape[1] // 2
        a, b = x[:, :columns], x[:, columns:]
        a, b = fold(a, bit_x, across, 1), fold(b, bit_y, across, 2)
        a, b = fold(a, bit_y, across, 2), fold(b, bit_x, across, 1)
        x = jnp.concatenate([a, b], axis=1)
        for k in depth_bits:
            x = fold(x, (lax.axis_index("wide") // k) % 2, along, k)
        for k in reversed(depth_bits):
            far = along(x, k)
            bit = (lax.axis_index("wide") // k) % 2
            x = jnp.concatenate(
                [jnp.where(bit == 0, x, far), jnp.where(bit == 0, far, x)], axis=0
            )
        a, b = x[:, :columns], x[:, columns:]
        a = jnp.concatenate([a, across(a, 2)], axis=0)
        b = jnp.concatenate([b, across(b, 1)], axis=0)
        a = jnp.concatenate([a, across(a, 1)], axis=0)
        b = jnp.concatenate([b, across(b, 2)], axis=0)
        far_a, far_b = along(a, 1), along(b, 1)
        return call(
            finish_kernel,
            [shaped((width, width), F32)] * count,
            place,
            a,
            b,
            far_a,
            far_b,
            smem=1,
        )

    (grad_w_output,) = total(output_keep, output_send, 1)
    grad_w_query, grad_w_key, grad_w_value = total(keep, send, 3)
    if n_wide <= 8:
        every = lax.all_gather(small.astype(BF), ("narrow", "wide"), axis=0, tiled=False)
        small = jnp.sum(every.astype(F32), axis=0)
    else:
        small = lax.psum(small, ("narrow", "wide"))
    return (
        layer_output,
        input_grad,
        grad_w_query,
        grad_w_key,
        grad_w_value,
        grad_w_output,
        small[0],
        small[8],
        small[16 : 16 + experts].T,
        small[16 + experts : 16 + experts + heads, :buckets_n].T,
        grad_expert_in,
        grad_expert_out,
    )


def solution(mesh):
    tokens_spec = P(("narrow", "wide"), None)
    experts_in_spec = P("wide", None, "narrow")
    experts_out_spec = P("wide", "narrow", None)
    in_specs = (
        (tokens_spec, tokens_spec)
        + (P(),) * 8
        + (experts_in_spec, experts_out_spec, tokens_spec, P(), P())
    )
    out_specs = (tokens_spec, tokens_spec) + (P(),) * 8 + (experts_in_spec, experts_out_spec)
    body = functools.partial(local, mesh.shape["narrow"], mesh.shape["wide"])
    return jax.shard_map(body, mesh=mesh, in_specs=in_specs, out_specs=out_specs, check_vma=False)
```

```python
import functools

import jax
import jax.numpy as jnp
from jax import lax
from jax.experimental import pallas as pl
from jax.experimental.pallas import tpu as pltpu
from jax.sharding import PartitionSpec as P

epsilon = 1e-06
BF = jnp.bfloat16
F32 = jnp.float32
HIGH = 60 * 2**20
LOW = 12 * 2**20


def mm(a, b):
    return lax.dot_general(a, b, (((1,), (0,)), ((), ())), preferred_element_type=F32)


def mm_nt(a, b):
    return lax.dot_general(a, b, (((1,), (1,)), ((), ())), preferred_element_type=F32)


def mm_tn(a, b):
    return lax.dot_general(a, b, (((0,), (0,)), ((), ())), preferred_element_type=F32)


def rms_scale(rows):
    return lax.rsqrt(jnp.mean(rows * rows, axis=-1, keepdims=True) + epsilon)


def half_masks(rows, width):
    lane = lax.broadcasted_iota(jnp.int32, (rows, width), 1)
    low = (lane < width // 2).astype(F32)
    return low.astype(BF), (1.0 - low).astype(BF)


def as_row(ref):
    return ref[...].reshape(1, -1)


def as_column(ref):
    return ref[...].reshape(-1, 1)


def bucket_mask(count, spread):
    shape = (count, spread.shape[1])
    return (lax.broadcasted_iota(jnp.int32, shape, 0) == spread[...]).astype(F32)


class Fetched:
    def __init__(self, source, buffer, semaphore):
        self.buffer, self.copy = buffer, pltpu.make_async_copy(source, buffer, semaphore)
        self.copy.start()
        self.waiting = True

    @property
    def shape(self):
        return self.buffer.shape

    def wait(self):
        if self.waiting:
            self.copy.wait()
            self.waiting = False

    def __getitem__(self, index):
        self.wait()
        return self.buffer[index]


class Stored:
    def __init__(self, target, buffer, semaphore):
        self.buffer, self.copy = buffer, pltpu.make_async_copy(buffer, target, semaphore)
        self.sent = False
        self.dtype = buffer.dtype

    @property
    def shape(self):
        return self.buffer.shape

    def __getitem__(self, index):
        return self.buffer[index]

    def __setitem__(self, index, value):
        self.buffer[index] = value

    def send(self):
        if not self.sent:
            self.copy.start()
            self.sent = True


def large(x):
    return (
        len(x.shape) >= 2
        and x.shape[-2] % 16 == 0
        and x.shape[-1] % 128 == 0
        and x.size * x.dtype.itemsize >= 2**16
    )


def call(kernel, outs, *args, flops=0, transcendentals=0, scratch=(), smem=0, stream=True):
    out_bytes = sum(o.size * o.dtype.itemsize for o in outs)
    in_bytes = sum(a.size * a.dtype.itemsize for a in args)
    large_in = [stream and i >= smem and large(x) for i, x in enumerate(args)]
    large_out = [stream and large(x) for x in outs]
    moved = [x for x, flag in zip(args + tuple(outs), large_in + large_out) if flag]

    def body(*refs):
        operands, results = refs[: len(args)], refs[len(args) : len(args) + len(outs)]
        rest = refs[len(args) + len(outs) :]
        buffers = iter(rest[: len(moved)])
        semaphores = rest[len(moved)] if moved else None
        count = iter(range(len(moved)))
        operands = [
            Fetched(ref, next(buffers), semaphores.at[next(count)]) if flag else ref
            for ref, flag in zip(operands, large_in)
        ]
        results = [
            Stored(ref, next(buffers), semaphores.at[next(count)]) if flag else ref
            for ref, flag in zip(results, large_out)
        ]
        kernel(*operands, *results, *rest[len(moved) + bool(moved) :])
        for x in operands:
            if isinstance(x, Fetched):
                x.wait()
        for x in results:
            if isinstance(x, Stored):
                x.send()
        for x in results:
            if isinstance(x, Stored):
                x.copy.wait()

    def spec(flag):
        return pl.BlockSpec(memory_space=pl.ANY if flag else pltpu.VMEM)

    scratches = [pltpu.VMEM(x.shape, x.dtype) for x in moved]
    if moved:
        scratches.append(pltpu.SemaphoreType.DMA((len(moved),)))
    return pl.pallas_call(
        body,
        out_shape=tuple(outs),
        in_specs=[
            pl.BlockSpec(memory_space=pltpu.SMEM) if i < smem else spec(flag)
            for i, flag in enumerate(large_in)
        ],
        out_specs=tuple(spec(flag) for flag in large_out),
        scratch_shapes=scratches + list(scratch),
        compiler_params=pltpu.CompilerParams(vmem_limit_bytes=HIGH if stream else LOW),
        cost_estimate=pl.CostEstimate(
            flops=flops, transcendentals=transcendentals, bytes_accessed=in_bytes + out_bytes
        ),
    )(*args)


def shaped(shape, dtype=BF):
    return jax.ShapeDtypeStruct(shape, dtype)


def front_kernel(
    heads,
    cap,
    shift_ref,
    tokens,
    cotangent,
    w_query,
    w_key,
    w_value,
    w_output,
    gain_attn,
    gain_ffn,
    w_router,
    table,
    spread,
    choices,
    levels,
    normed_one_out,
    query_out,
    key_out,
    value_out,
    probs_out,
    mixed_out,
    residual_out,
    normed_two_out,
    router_out,
    target_out,
    *slots_out,
):
    length, width = tokens.shape
    scale = (width // heads) ** (-0.5)
    experts = w_router.shape[0]
    slot_rows = slots_out[0].shape[0]
    flat_slots = slot_rows * len(slots_out)
    inputs = tokens[...].astype(F32)
    normed = (inputs * rms_scale(inputs) * as_row(gain_attn)).astype(BF)
    normed_one_out[...] = normed
    normed_one_out.send()
    query_out[...] = mm(normed, w_query[...]).astype(BF)
    key_out[...] = mm(normed, w_key[...]).astype(BF)
    value_out[...] = mm(normed, w_value[...]).astype(BF)
    for out in (query_out, key_out, value_out):
        out.send()
    by_offset = lax.dot_general(
        table[...],
        bucket_mask(table.shape[1], spread),
        (((1,), (0,)), ((), ())),
        precision=lax.Precision.HIGHEST,
        preferred_element_type=F32,
    )
    pair = 2 * width // heads
    masks = half_masks(length, pair)
    for p in range(heads // 2):
        at = slice(p * pair, (p + 1) * pair)
        q2, k2, v2 = query_out[:, at], key_out[:, at], value_out[:, at]
        probs = []
        for half in (0, 1):
            h = 2 * p + half
            base = jnp.broadcast_to(by_offset[h : h + 1, :], (length, 2 * length))
            bias = pltpu.roll(base, 0, 1, stride=1, stride_axis=0)[:, :length]
            scores = mm_nt(q2, k2 * masks[half]) * scale + bias
            e = jnp.exp(scores - jnp.max(scores, axis=-1, keepdims=True))
            e = (e / jnp.sum(e, axis=-1, keepdims=True)).astype(BF)
            probs_out[h] = e
            probs.append(e)
        mixed_out[:, at] = mm(
            jnp.concatenate(probs, axis=1),
            jnp.concatenate([v2 * masks[0], v2 * masks[1]], axis=0),
        ).astype(BF)
    probs_out.send()
    mixed_out.send()
    residual = inputs + mm(mixed_out[...], w_output[...])
    residual_out[...] = residual
    residual_out.send()
    normed_two = (residual * rms_scale(residual) * as_row(gain_ffn)).astype(BF)
    normed_two_out[...] = normed_two
    normed_two_out.send()
    logits = mm_nt(w_router[...], normed_two) + 0.25 * as_column(levels).astype(F32)
    logit_exp = jnp.exp(logits - jnp.max(logits, axis=0, keepdims=True))
    router = logit_exp / jnp.sum(logit_exp, axis=0, keepdims=True)
    router_out[...] = router.T
    chosen = choices[...]
    mask = (chosen == lax.broadcasted_iota(jnp.int32, (experts, length), 0)).astype(F32)
    earlier = (
        lax.broadcasted_iota(jnp.int32, (length, length), 0)
        < lax.broadcasted_iota(jnp.int32, (length, length), 1)
    ).astype(F32)
    counts = mm(mask.astype(BF), earlier.astype(BF))
    position = jnp.sum(mask * counts, axis=0, keepdims=True).astype(jnp.int32)
    target = jnp.where(position < cap, (chosen ^ shift_ref[0]) * cap + position, -1)
    gate = jnp.sum(mask * router, axis=0, keepdims=True)
    row = lax.broadcasted_iota(jnp.int32, (8, length), 0)
    packed = jnp.where(
        row == 0, gate, jnp.where(row == 1, target.astype(F32), chosen.astype(F32))
    ).T
    target_out[...] = packed
    place = (target == lax.broadcasted_iota(jnp.int32, (flat_slots, length), 0)).astype(F32)
    place = place.astype(BF)
    sent = (packed[:, :1] * cotangent[...].astype(F32)).astype(BF)
    normed_slots, grad_slots = mm(place, normed_two), mm(place, sent)
    for i, out in enumerate(slots_out):
        rows = slice(i * slot_rows, (i + 1) * slot_rows)
        out[:, :width] = normed_slots[rows].astype(BF)
        out[:, width:] = grad_slots[rows].astype(BF)


def expert_kernel(*refs):
    w_in, first, w_out, second = refs[0], refs[1:5], refs[5], refs[6:10]
    hidden, grad_pre = refs[10:12], refs[12:14]
    keep_a0, keep_b0, send_a, send_b, keep_b1, keep_a1 = refs[14:]
    rows, double = first[0].shape
    width = double // 2
    c = 0.7978845608028654
    places = (
        ((keep_a0, ()), (keep_b0, ()), (send_a, (0,)), (keep_b1, ())),
        ((keep_a1, ()), (send_b, (0,)), (send_a, (1,)), (send_b, (1,))),
    )
    for i, (pieces, outs) in enumerate(zip((first, second), places)):
        both = jnp.concatenate([p[...] for p in pieces], axis=0)
        pre = mm(both[:, :width], w_in[...])
        square = pre * pre
        t = jnp.tanh(c * pre * (1.0 + 0.044715 * square))
        act = (0.5 * pre * (1.0 + t)).astype(BF)
        slope = 0.5 * (1.0 + t) + 0.5 * c * pre * (1.0 - t * t) * (1.0 + 3 * 0.044715 * square)
        grad = (mm_nt(both[:, width:], w_out[...]) * slope).astype(BF)
        hidden[i][...] = act
        hidden[i].send()
        grad_pre[i][...] = grad
        grad_pre[i].send()
        result = mm(act, w_out[...]).astype(BF)
        back = mm_nt(grad, w_in[...]).astype(BF)
        for j, (out, slot) in enumerate(outs):
            out[(*slot, slice(None), slice(0, width))] = result[j * rows : (j + 1) * rows]
            out[(*slot, slice(None), slice(width, double))] = back[j * rows : (j + 1) * rows]
            if slot != (0,):
                out.send()


def expert_weights_kernel(*refs):
    pieces, units, (grad_in, grad_out) = refs[:16], refs[16:24], refs[24:]
    width = grad_in.shape[1]
    both = jnp.concatenate([p[...] for p in pieces], axis=0)
    act = jnp.concatenate([units[i][...] for i in (0, 1, 4, 5)], axis=0)
    pre = jnp.concatenate([units[i][...] for i in (2, 3, 6, 7)], axis=0)
    step = 256
    for i in range(width // step):
        grad_in[0, i * step : (i + 1) * step, :] = mm_tn(both[:, i * step : (i + 1) * step], pre)
    grad_in.send()
    for i in range(act.shape[1] // step):
        grad_out[0, i * step : (i + 1) * step, :] = mm_tn(
            act[:, i * step : (i + 1) * step], both[:, width:]
        )


def store_halves(core, h, left, right, keep, send):
    columns = left.shape[1]

    @pl.when(core == h)
    def _():
        keep[:, :columns] = left
        keep[:, columns:] = right

    @pl.when(core != h)
    def _():
        send[:, :columns] = left
        send[:, columns:] = right


def diagonal_sums(scores):
    length = scores.shape[0]
    half = length // 2
    low, high = scores[:half], scores[half:]
    total = jnp.concatenate(
        [low[:, :half] + high[:, half:], low[:, half:], jnp.zeros_like(low[:, :half]), high[:, :half]],
        axis=1,
    )
    while total.shape[0] > 8:
        half = total.shape[0] // 2
        total = total[:half] + pltpu.roll(total[half:], 2 * length - half, 1)
    return total


def backward_kernel(
    heads,
    buckets_n,
    core_ref,
    packed,
    router,
    gain_ffn,
    w_router,
    spread,
    cotangent,
    residual_ref,
    w_output,
    value,
    probs_ref,
    normed_two,
    key,
    query,
    mixed,
    normed_one,
    w_value,
    w_query,
    w_key,
    tokens,
    gain_attn,
    *refs,
):
    returned, outs = refs[:-12], refs[-12:]
    layer_output, input_grad, keep_1, send_1, keep_2, send_2, small_out = outs[:7]
    small, grad_mixed_out, grad_value, grad_query, grad_key = outs[7:]
    core = core_ref[0]
    length, width = residual_ref.shape
    scale = (width // heads) ** (-0.5)
    experts = router.shape[1]
    slot_rows = returned[0].shape[0]
    gate, goal, chosen = packed[:, 0:1], packed[:, 1:2], packed[:, 2:3]
    if len(returned) > 1:
        back = jnp.concatenate([r[...].astype(F32) for r in returned], axis=0).astype(BF)
    else:
        back = returned[0][...]
    place = (
        goal.astype(jnp.int32)
        == lax.broadcasted_iota(jnp.int32, (length, slot_rows * len(returned)), 1)
    ).astype(F32)
    back = mm(place.astype(BF), back)
    picked = back[:, :width]
    kept = (goal >= 0).astype(F32)
    mask = (
        chosen.astype(jnp.int32) == lax.broadcasted_iota(jnp.int32, (length, experts), 1)
    ).astype(F32)
    probs = router[...]
    upstream = cotangent[...].astype(F32)
    residual = residual_ref[...]
    grad_gate = jnp.sum(upstream * picked, axis=1, keepdims=True) * kept
    grad_logits = ((grad_gate * gate) * (mask - probs)).astype(BF)
    grad_two = back[:, width:] + mm(grad_logits, w_router[...])
    scale_two = rms_scale(residual)
    weighted = grad_two * as_row(gain_ffn)
    grad_residual = (
        upstream
        + scale_two * weighted
        - residual * (scale_two**3 * jnp.mean(weighted * residual, axis=1, keepdims=True))
    )
    layer_output[...] = (residual + gate * kept * picked).astype(BF)
    layer_output.send()
    small[...] = jnp.zeros_like(small)
    small[1:2, :] = jnp.sum(grad_two * residual * scale_two, axis=0, keepdims=True)
    grad_attn = grad_residual.astype(BF)
    grad_mixed_out[...] = mm_nt(grad_attn, w_output[...]).astype(BF)
    small[2 : 2 + experts, :] = mm_tn(grad_logits, normed_two[...])
    pair = 2 * width // heads
    masks = half_masks(length, pair)
    sums = []
    for p in range(heads // 2):
        at = slice(p * pair, (p + 1) * pair)
        q2, k2, v2, g2 = query[:, at], key[:, at], value[:, at], grad_mixed_out[:, at]
        attn = probs_ref[2 * p], probs_ref[2 * p + 1]
        grads = []
        for half in (0, 1):
            e = attn[half].astype(F32)
            grad_probs = mm_nt(g2, v2 * masks[half])
            gs = e * (grad_probs - jnp.sum(e * grad_probs, axis=-1, keepdims=True))
            sums.append(diagonal_sums(gs))
            grads.append(gs.astype(BF))
        grad_v = mm_tn(
            jnp.concatenate(attn, axis=0),
            jnp.concatenate([g2 * masks[0], g2 * masks[1]], axis=0),
        )
        grad_q = mm(
            jnp.concatenate(grads, axis=1),
            jnp.concatenate([k2 * masks[0], k2 * masks[1]], axis=0),
        )
        grad_k = mm_tn(
            jnp.concatenate(grads, axis=0),
            jnp.concatenate([q2 * masks[0], q2 * masks[1]], axis=0),
        )
        grad_value[:, at] = grad_v.astype(BF)
        grad_query[:, at] = (grad_q * scale).astype(BF)
        grad_key[:, at] = (grad_k * scale).astype(BF)
    half = width // 2
    for h in (0, 1):
        at = slice(h * half, (h + 1) * half)
        left = mm_tn(mixed[:, at], grad_attn).astype(BF)
        right = mm_tn(normed_one[:, at], grad_value[...]).astype(BF)
        store_halves(core, h, left, right, keep_1, send_1)
    send_1.send()
    keep_1.send()
    for h in (0, 1):
        at = slice(h * half, (h + 1) * half)
        left = mm_tn(normed_one[:, at], grad_query[...]).astype(BF)
        right = mm_tn(normed_one[:, at], grad_key[...]).astype(BF)
        store_halves(core, h, left, right, keep_2, send_2)
    send_2.send()
    keep_2.send()
    grad_one = mm_nt(grad_value[...], w_value[...])
    grad_one = grad_one + mm_nt(grad_query[...], w_query[...])
    grad_one = grad_one + mm_nt(grad_key[...], w_key[...])
    inputs = tokens[...].astype(F32)
    scale_one = rms_scale(inputs)
    small[0:1, :] = jnp.sum(grad_one * inputs * scale_one, axis=0, keepdims=True)
    weighted = grad_one * as_row(gain_attn)
    input_grad[...] = (
        grad_residual
        + scale_one * weighted
        - inputs * (scale_one**3 * jnp.mean(weighted * inputs, axis=1, keepdims=True))
    ).astype(BF)
    input_grad.send()
    total = jnp.concatenate(sums, axis=0)
    row = lax.broadcasted_iota(jnp.int32, total.shape, 0) % 8
    for bit in (1, 2, 4):
        total = jnp.where((row & bit) != 0, pltpu.roll(total, 2 * length - bit, 1), total)
    by_offset = jnp.sum(total.reshape(heads, 8, 2 * length), axis=1)
    small[2 + experts : 2 + experts + heads, :buckets_n] = lax.dot_general(
        by_offset,
        bucket_mask(buckets_n, spread),
        (((1,), (1,)), ((), ())),
        precision=lax.Precision.HIGHEST,
        preferred_element_type=F32,
    )
    small_out[...] = small[...].astype(small_out.dtype)


def small_kernel(every, gain_attn, gain_ffn, router, table, small):
    small[...] = jnp.sum(every[...].astype(F32), axis=0)
    experts = router.shape[0]
    heads, buckets_n = table.shape
    gain_attn[...] = small[0:1, :].reshape(gain_attn.shape)
    gain_ffn[...] = small[1:2, :].reshape(gain_ffn.shape)
    router[...] = small[2 : 2 + experts, :]
    table[...] = small[2 + experts : 2 + experts + heads, :buckets_n]


def both(left, right, rows, columns):
    return left[rows, columns].astype(F32) + right[rows, columns].astype(F32)


def fold_kernel(bits, place_ref, *refs):
    count = len(refs) // 4 if len(refs) > 6 else 1
    for i, bit in enumerate(bits):
        own, got = refs[2 * i : 2 * i + 2] if count == 2 else refs[:2]
        keep, send = refs[-4 + 2 * i : len(refs) - 2 + 2 * i]
        half, columns = keep.shape
        left = 0 if count == 2 else i * columns
        for out, side in ((keep, place_ref[bit]), (send, 1 - place_ref[bit])):
            rows = pl.ds(pl.multiple_of(side * half, half), half)
            out[...] = both(own, got, rows, slice(left, left + columns)).astype(BF)


def join_kernel(bit, place_ref, own_a, got_a, own_b, got_b, keep, send):
    half = keep.shape[0]
    columns = own_a.shape[1]
    for out, side in ((keep, place_ref[bit]), (send, 1 - place_ref[bit])):
        rows = pl.ds(pl.multiple_of(side * half, half), half)
        out[:, :columns] = both(own_a, got_a, rows, slice(None)).astype(BF)
        out[:, columns:] = both(own_b, got_b, rows, slice(None)).astype(BF)


def columns_kernel(bit, place_ref, own, got, keep, send):
    columns = keep.shape[1]
    for out, side in ((keep, place_ref[bit]), (send, 1 - place_ref[bit])):
        at = pl.ds(pl.multiple_of(side * columns, columns), columns)
        out[...] = both(own, got, slice(None), at).astype(BF)


def beside_kernel(bit, place_ref, own, far, out):
    columns = own.shape[1]
    for source, side in ((own, place_ref[bit]), (far, 1 - place_ref[bit])):
        out[:, pl.ds(pl.multiple_of(side * columns, columns), columns)] = source[...]


def stack_kernel(bit, place_ref, own, far, out_a, out_b):
    rows, columns = own.shape[0], out_a.shape[1]
    for source, side in ((own, place_ref[bit]), (far, 1 - place_ref[bit])):
        at = pl.ds(pl.multiple_of(side * rows, rows), rows)
        out_a[at, :] = source[:, :columns]
        out_b[at, :] = source[:, columns:]


def double_kernel(own_a, far_a, own_b, far_b, out_a, out_b):
    rows = own_a.shape[0]
    for source, at, out in ((own_a, 0, out_a), (far_a, 1, out_a), (own_b, 0, out_b), (far_b, 1, out_b)):
        out[at * rows : (at + 1) * rows, :] = source[...]


def half_kernel(place_ref, own_a, far_a, own_b, far_b, out):
    block, columns = own_a.shape[0] // 2, own_a.shape[1]
    sources = ((own_a, 0, 0, 1, 2), (far_a, 0, 1, 1, 2), (own_b, 1, 0, 2, 1), (far_b, 1, 1, 2, 1))
    for source, side, far, bit_1, bit_2 in sources:
        for i in (0, 1):
            at = ((place_ref[bit_1] ^ far) * 2 + (place_ref[bit_2] ^ i)) * block
            out[
                pl.ds(pl.multiple_of(at, block), block), side * columns : (side + 1) * columns
            ] = source[i * block : (i + 1) * block, :]


def finish_kernel(other, count, place_ref, *refs):
    sources, outs, (buffer, semaphores) = refs[:count], refs[-2 - 2 * count : -2], refs[-2:]
    rows, width = sources[0].shape[0], outs[0].shape[1]
    side = (1 - place_ref[0]) if other else place_ref[0]
    at = pl.ds(pl.multiple_of(side * rows, rows), rows)
    copies = []
    for m, out in enumerate(outs):
        left = m % 2 * width
        buffer[m] = sources[m // 2][:, left : left + width].astype(F32)
        copies.append(pltpu.make_async_copy(buffer.at[m], out.at[at, :], semaphores.at[m]))
        copies[-1].start()
    for copy in copies:
        copy.wait()


def pairs(size, k):
    return [(i, i ^ k) for i in range(size)]


def local(
    n_narrow,
    n_wide,
    tokens,
    cotangent,
    w_query,
    w_key,
    w_value,
    w_output,
    gain_attn,
    gain_ffn,
    w_router,
    bias_table,
    expert_in,
    expert_out,
    choices,
    router_levels,
    buckets,
):
    length, width = tokens.shape
    buckets_n, heads = bias_table.shape
    experts = w_router.shape[1]
    cap = (5 * length + 4 * experts - 1) // (4 * experts)
    flat_slots = experts * cap
    direct = n_wide <= 8
    narrow_at, wide_at = lax.axis_index("narrow"), lax.axis_index("wide")
    core_ref = (wide_at % 2).reshape(1)
    shift_ref = (wide_at if direct else jnp.zeros((), jnp.int32)).reshape(1)
    w_router = w_router.T
    spread = jnp.roll(jnp.pad(buckets, (0, 1)), length + 1).reshape(1, 2 * length)
    rows_bf = shaped((length, width))
    attn_flops = 4 * length * length * width

    def across(x, k):
        return lax.ppermute(x, "narrow", pairs(n_narrow, k))

    def along(x, k):
        return lax.ppermute(x, "wide", pairs(n_wide, k))

    (
        normed_one,
        query,
        key,
        value,
        probs,
        mixed,
        residual,
        normed_two,
        router,
        packed,
        *slots,
    ) = call(
        functools.partial(front_kernel, heads, cap),
        [
            rows_bf,
            rows_bf,
            rows_bf,
            rows_bf,
            shaped((heads, length, length)),
            rows_bf,
            shaped((length, width), F32),
            rows_bf,
            shaped((length, experts), F32),
            shaped((length, 8), F32),
        ]
        + [shaped((cap if direct else flat_slots, 2 * width))] * (n_wide if direct else 1),
        shift_ref,
        tokens,
        cotangent,
        w_query,
        w_key,
        w_value,
        w_output,
        gain_attn,
        gain_ffn,
        w_router,
        bias_table.T,
        spread,
        choices.reshape(1, length),
        router_levels,
        smem=1,
        flops=8 * length * width * width + attn_flops,
        transcendentals=heads * length * length,
    )

    quarter = flat_slots // 4
    order = (0, 2, 1, 3)
    if direct:
        per = n_wide // 4
        moved = [slots[0]] + [along(slots[k], k) for k in range(1, n_wide)]
        parts = [moved[i * per : (i + 1) * per] for i in order]
    else:
        moved = lax.all_to_all(slots[0], "wide", split_axis=0, concat_axis=0, tiled=True)
        parts = [[moved[i * quarter : (i + 1) * quarter]] for i in range(4)]

    def gather(a, b):
        a1, b2 = across(a, 1), across(b, 2)
        a2, b1 = across(a, 2), across(b, 1)
        a3, b3 = across(a1, 2), across(b2, 1)
        return [a, b, a1, b1, a2, b2, a3, b3]

    quarters = [jnp.concatenate(part, axis=0) for part in parts]

    def reduce(keep_a, send_a, keep_b, send_b):
        got_a, got_b = across(send_a, 1), across(send_b, 2)
        next_a = (keep_a[1].astype(F32) + got_a[1].astype(F32)).astype(BF)
        next_b = (keep_b[1].astype(F32) + got_b[1].astype(F32)).astype(BF)
        last_a, last_b = across(next_a, 2), across(next_b, 1)
        sum_a = keep_a[0].astype(F32) + got_a[0].astype(F32) + last_a.astype(F32)
        sum_b = keep_b[0].astype(F32) + got_b[0].astype(F32) + last_b.astype(F32)
        return sum_a.astype(BF), sum_b.astype(BF)

    w_in = expert_in.reshape(width, -1)
    w_out = expert_out.reshape(-1, width)
    units = w_in.shape[1]
    piece = shaped((2, quarter, 2 * width))
    unit_rows = shaped((4 * quarter, units))
    slot_piece = shaped((quarter, 2 * width))
    expert_flops = 2 * 8 * quarter * width * units
    def experts_of(rows):
        return call(
            expert_kernel,
            [unit_rows] * 4 + [slot_piece, slot_piece, piece, piece, slot_piece, slot_piece],
            w_in,
            *rows[:4],
            w_out,
            *rows[4:],
            flops=4 * expert_flops,
            transcendentals=8 * quarter * units,
        )

    def reduced(keep_a0, keep_b0, send_a, send_b, keep_b1, keep_a1):
        return reduce((keep_a0, keep_a1), send_a, (keep_b0, keep_b1), send_b)

    first = gather(*quarters[:2])
    quarters[2], quarters[3], first[3], first[4] = lax.optimization_barrier(
        (quarters[2], quarters[3], first[3], first[4])
    )
    second = gather(*quarters[2:])
    done_1, done_2 = experts_of(first), experts_of(second)
    groups = [first, second]
    kept = done_1[:4] + done_2[:4]
    sums = [*reduced(*done_1[4:]), *reduced(*done_2[4:])]
    if direct:
        sums = [sums[i] for i in order]
        returned = [sums[k // per][k % per * cap : (k % per + 1) * cap] for k in range(n_wide)]
        returned = [returned[0]] + [along(returned[k], k) for k in range(1, n_wide)]
    else:
        returned = jnp.concatenate(sums, axis=0)
        returned = [lax.all_to_all(returned, "wide", split_axis=0, concat_axis=0, tiled=True)]
    grad_expert_in, grad_expert_out = call(
        expert_weights_kernel,
        [shaped(expert_in.shape, F32), shaped(expert_out.shape, F32)],
        *groups[0],
        *groups[1],
        *kept,
        flops=4 * expert_flops,
    )
    returned, grad_expert_in, grad_expert_out = lax.optimization_barrier(
        (returned, grad_expert_in, grad_expert_out)
    )

    half = width // 2
    small_rows = -(-(2 + experts + heads) // 16) * 16
    layer_output, input_grad, keep_1, send_1, keep_2, send_2, small = call(
        functools.partial(backward_kernel, heads, buckets_n),
        [rows_bf, rows_bf]
        + [shaped((half, 2 * width))] * 4
        + [shaped((small_rows, width), BF if direct else F32)],
        core_ref,
        packed,
        router,
        gain_ffn,
        w_router,
        spread,
        cotangent,
        residual,
        w_output,
        value,
        probs,
        normed_two,
        key,
        query,
        mixed,
        normed_one,
        w_value,
        w_query,
        w_key,
        tokens,
        gain_attn,
        *returned,
        smem=1,
        scratch=[pltpu.VMEM((small_rows, width), F32)] + [pltpu.VMEM((length, width), BF)] * 4,
        flops=16 * length * width * width + 3 * attn_flops,
    )

    place = jnp.stack(
        [wide_at % 2, narrow_at % 2, narrow_at // 2, wide_at // 2 % 2, wide_at // 4 % 2]
    ).astype(jnp.int32)
    deeper = [2**i for i in range(3, 20) if 2**i < n_wide]

    def hop(kernel, shapes, *args):
        return call(kernel, [shaped(x) for x in shapes], place, *args, smem=1, stream=False)

    def fold_first(keep, send):
        kernel = functools.partial(fold_kernel, (1, 2))
        return hop(kernel, [(half // 2, width)] * 4, keep, along(send, 1))

    def scatter(own_a, got_a, own_b, got_b):
        step = functools.partial
        own, other = hop(
            step(join_kernel, 3), [(half // 8, 2 * width)] * 2, own_a, got_a, own_b, got_b
        )
        own, other = hop(
            step(columns_kernel, 4), [(half // 8, width)] * 2, own, along(other, 2)
        )
        x = (own.astype(F32) + along(other, 4).astype(F32)).astype(BF)
        for k in deeper:
            bit, size = wide_at // k % 2, x.shape[0] // 2
            other = lax.dynamic_slice_in_dim(x, (1 - bit) * size, size, 0)
            own = lax.dynamic_slice_in_dim(x, bit * size, size, 0)
            x = (own.astype(F32) + along(other, k).astype(F32)).astype(BF)
        return x

    def spread_out(x):
        step = functools.partial
        for k in reversed(deeper):
            bit, far = wide_at // k % 2, along(x, k)
            x = jnp.concatenate([jnp.where(bit == 0, x, far), jnp.where(bit == 0, far, x)], axis=0)
        (x,) = hop(step(beside_kernel, 4), [(half // 8, 2 * width)], x, along(x, 4))
        a, b = hop(step(stack_kernel, 3), [(half // 4, width)] * 2, x, along(x, 2))
        a, b = call(
            double_kernel,
            [shaped((half // 2, width))] * 2,
            a,
            across(a, 2),
            b,
            across(b, 1),
            stream=False,
        )
        (x,) = hop(half_kernel, [(half, 2 * width)], a, across(a, 1), b, across(b, 2))
        return x

    def fold_second(own_a, send_a, own_b, send_b):
        own_a, send_a, own_b, send_b = hop(
            functools.partial(fold_kernel, (2, 1)),
            [(half // 4, width)] * 4,
            own_a,
            across(send_a, 1),
            own_b,
            across(send_b, 2),
        )
        return own_a, across(send_a, 2), own_b, across(send_b, 1)

    def finish(sources, outs=()):
        count = 2 * len(sources)
        return pl.pallas_call(
            functools.partial(finish_kernel, bool(outs), len(sources)),
            out_shape=(shaped((width, width), F32),) * count,
            in_specs=[pl.BlockSpec(memory_space=pltpu.SMEM)]
            + [pl.BlockSpec(memory_space=pltpu.VMEM)] * len(sources)
            + [pl.BlockSpec(memory_space=pl.ANY)] * len(outs),
            out_specs=(pl.BlockSpec(memory_space=pl.ANY),) * count,
            scratch_shapes=[
                pltpu.VMEM((count, half, width), F32),
                pltpu.SemaphoreType.DMA((count,)),
            ],
            input_output_aliases={1 + len(sources) + i: i for i in range(len(outs))},
            compiler_params=pltpu.CompilerParams(vmem_limit_bytes=LOW),
        )(place, *sources, *outs)

    after = lax.optimization_barrier
    first_1, first_2 = fold_first(keep_1, send_1), fold_first(keep_2, send_2)
    if direct:
        small = lax.all_gather(small, ("narrow", "wide"), axis=0, tiled=False)
    else:
        small = lax.psum(small, ("narrow", "wide"))[None]
    small = call(
        small_kernel,
        [
            shaped((width,), F32),
            shaped((width,), F32),
            shaped((experts, width), F32),
            shaped((heads, buckets_n), F32),
        ],
        small,
        scratch=[pltpu.VMEM((small_rows, width), F32)],
    )
    part_1 = spread_out(scatter(*fold_second(*first_1)))
    part_2 = spread_out(scatter(*fold_second(*first_2)))
    far_1, far_2 = along(part_1, 1), along(part_2, 1)
    near = finish((part_1, part_2))
    far_1, far_2, near, small = after((far_1, far_2, near, small))
    grad_w_output, grad_w_value, grad_w_query, grad_w_key = finish((far_1, far_2), near)
    return (
        layer_output,
        input_grad,
        grad_w_query,
        grad_w_key,
        grad_w_value,
        grad_w_output,
        small[0],
        small[1],
        small[2].T,
        small[3].T,
        grad_expert_in,
        grad_expert_out,
    )


def solution(mesh):
    tokens_spec = P(("narrow", "wide"), None)
    experts_in_spec = P("wide", None, "narrow")
    experts_out_spec = P("wide", "narrow", None)
    in_specs = (
        (tokens_spec, tokens_spec)
        + (P(),) * 8
        + (experts_in_spec, experts_out_spec, tokens_spec, P(), P())
    )
    out_specs = (tokens_spec, tokens_spec) + (P(),) * 8 + (experts_in_spec, experts_out_spec)
    body = functools.partial(local, mesh.shape["narrow"], mesh.shape["wide"])
    return jax.shard_map(body, mesh=mesh, in_specs=in_specs, out_specs=out_specs, check_vma=False)
```

```python
import functools

import jax
import jax.numpy as jnp
from jax import lax
from jax.experimental import pallas as pl
from jax.experimental.pallas import tpu as pltpu
from jax.sharding import PartitionSpec as P

epsilon = 1e-06
BF = jnp.bfloat16
F32 = jnp.float32
HIGH = 60 * 2**20
LOW = 12 * 2**20


def mm(a, b):
    return lax.dot_general(a, b, (((1,), (0,)), ((), ())), preferred_element_type=F32)


def mm_nt(a, b):
    return lax.dot_general(a, b, (((1,), (1,)), ((), ())), preferred_element_type=F32)


def mm_tn(a, b):
    return lax.dot_general(a, b, (((0,), (0,)), ((), ())), preferred_element_type=F32)


def rms_scale(rows):
    return lax.rsqrt(jnp.mean(rows * rows, axis=-1, keepdims=True) + epsilon)


def half_masks(rows, width):
    lane = lax.broadcasted_iota(jnp.int32, (rows, width), 1)
    low = (lane < width // 2).astype(F32)
    return low.astype(BF), (1.0 - low).astype(BF)


def as_row(ref):
    return ref[...].reshape(1, -1)


def as_column(ref):
    return ref[...].reshape(-1, 1)


def bucket_mask(count, buckets):
    span = buckets.shape[0] + 1
    row = jnp.concatenate([buckets[...].reshape(1, -1), jnp.zeros((1, 1), jnp.int32)], axis=1)
    rows = pltpu.roll(jnp.broadcast_to(row, (8, span)), span // 2 + 1, 1)
    index = lax.broadcasted_iota(jnp.int32, (count, span), 0)
    return (index == rows[:1]).astype(F32)


class Fetched:
    def __init__(self, source, buffer, semaphore, later):
        self.buffer, self.copy = buffer, pltpu.make_async_copy(source, buffer, semaphore)
        self.later, self.waiting = later, True

    @property
    def shape(self):
        return self.buffer.shape

    def wait(self):
        if self.waiting:
            self.copy.wait()
            self.waiting = False
            while self.later:
                self.later.pop(0).copy.start()

    def __getitem__(self, index):
        self.wait()
        return self.buffer[index]


class Stored:
    def __init__(self, target, buffer, semaphore):
        self.buffer, self.copy = buffer, pltpu.make_async_copy(buffer, target, semaphore)
        self.sent = False
        self.dtype = buffer.dtype

    @property
    def shape(self):
        return self.buffer.shape

    def __getitem__(self, index):
        return self.buffer[index]

    def __setitem__(self, index, value):
        self.buffer[index] = value

    def send(self):
        if not self.sent:
            self.copy.start()
            self.sent = True


def large(x):
    return (
        len(x.shape) >= 2
        and x.shape[-2] % 16 == 0
        and x.shape[-1] % 128 == 0
        and x.size * x.dtype.itemsize >= 2**16
    )


def call(kernel, outs, *args, flops=0, transcendentals=0, scratch=(), smem=0, stream=True, early=99):
    out_bytes = sum(o.size * o.dtype.itemsize for o in outs)
    in_bytes = sum(a.size * a.dtype.itemsize for a in args)
    large_in = [stream and i >= smem and large(x) for i, x in enumerate(args)]
    large_out = [stream and large(x) for x in outs]
    moved = [x for x, flag in zip(args + tuple(outs), large_in + large_out) if flag]

    def body(*refs):
        operands, results = refs[: len(args)], refs[len(args) : len(args) + len(outs)]
        rest = refs[len(args) + len(outs) :]
        buffers = iter(rest[: len(moved)])
        semaphores = rest[len(moved)] if moved else None
        count = iter(range(len(moved)))
        later = []
        operands = [
            Fetched(ref, next(buffers), semaphores.at[next(count)], later) if flag else ref
            for ref, flag in zip(operands, large_in)
        ]
        fetched = [x for x in operands if isinstance(x, Fetched)]
        later += fetched[early:]
        for x in fetched[:early]:
            x.copy.start()
        results = [
            Stored(ref, next(buffers), semaphores.at[next(count)]) if flag else ref
            for ref, flag in zip(results, large_out)
        ]
        kernel(*operands, *results, *rest[len(moved) + bool(moved) :])
        for x in operands:
            if isinstance(x, Fetched):
                x.wait()
        for x in results:
            if isinstance(x, Stored):
                x.send()
        for x in results:
            if isinstance(x, Stored):
                x.copy.wait()

    def spec(flag):
        return pl.BlockSpec(memory_space=pl.ANY if flag else pltpu.VMEM)

    scratches = [pltpu.VMEM(x.shape, x.dtype) for x in moved]
    if moved:
        scratches.append(pltpu.SemaphoreType.DMA((len(moved),)))
    return pl.pallas_call(
        body,
        out_shape=tuple(outs),
        in_specs=[
            pl.BlockSpec(memory_space=pltpu.SMEM) if i < smem else spec(flag)
            for i, flag in enumerate(large_in)
        ],
        out_specs=tuple(spec(flag) for flag in large_out),
        scratch_shapes=scratches + list(scratch),
        compiler_params=pltpu.CompilerParams(vmem_limit_bytes=HIGH if stream else LOW),
        cost_estimate=pl.CostEstimate(
            flops=flops, transcendentals=transcendentals, bytes_accessed=in_bytes + out_bytes
        ),
    )(*args)


def shaped(shape, dtype=BF):
    return jax.ShapeDtypeStruct(shape, dtype)


def front_kernel(
    heads,
    cap,
    shift_ref,
    tokens,
    w_query,
    w_key,
    w_value,
    w_output,
    cotangent,
    gain_attn,
    gain_ffn,
    w_router,
    table,
    buckets,
    choices,
    levels,
    normed_one_out,
    query_out,
    key_out,
    value_out,
    probs_out,
    mixed_out,
    residual_out,
    normed_two_out,
    packed_out,
    *slots_out,
):
    length, width = tokens.shape
    scale = (width // heads) ** (-0.5)
    experts = w_router.shape[0]
    slot_rows = slots_out[0].shape[0]
    flat_slots = slot_rows * len(slots_out)
    inputs = tokens[...].astype(F32)
    normed = (inputs * rms_scale(inputs) * as_row(gain_attn)).astype(BF)
    normed_one_out[...] = normed
    normed_one_out.send()
    query_out[...] = mm(normed, w_query[...]).astype(BF)
    key_out[...] = mm(normed, w_key[...]).astype(BF)
    value_out[...] = mm(normed, w_value[...]).astype(BF)
    for out in (query_out, key_out, value_out):
        out.send()
    by_offset = lax.dot_general(
        table[...],
        bucket_mask(table.shape[1], buckets),
        (((1,), (0,)), ((), ())),
        precision=lax.Precision.HIGHEST,
        preferred_element_type=F32,
    )
    pair = 2 * width // heads
    masks = half_masks(length, pair)
    for p in range(heads // 2):
        at = slice(p * pair, (p + 1) * pair)
        q2, k2, v2 = query_out[:, at], key_out[:, at], value_out[:, at]
        probs = []
        for half in (0, 1):
            h = 2 * p + half
            base = jnp.broadcast_to(by_offset[h : h + 1, :], (length, 2 * length))
            bias = pltpu.roll(base, 0, 1, stride=1, stride_axis=0)[:, :length]
            scores = mm_nt(q2, k2 * masks[half]) * scale + bias
            e = jnp.exp(scores - jnp.max(scores, axis=-1, keepdims=True))
            e = (e / jnp.sum(e, axis=-1, keepdims=True)).astype(BF)
            probs_out[h] = e
            probs.append(e)
        mixed_out[:, at] = mm(
            jnp.concatenate(probs, axis=1),
            jnp.concatenate([v2 * masks[0], v2 * masks[1]], axis=0),
        ).astype(BF)
    probs_out.send()
    mixed_out.send()
    residual = inputs + mm(mixed_out[...], w_output[...])
    residual_out[...] = residual
    residual_out.send()
    normed_two = (residual * rms_scale(residual) * as_row(gain_ffn)).astype(BF)
    normed_two_out[...] = normed_two
    normed_two_out.send()
    logits = mm_nt(w_router[...], normed_two) + 0.25 * as_column(levels).astype(F32)
    logit_exp = jnp.exp(logits - jnp.max(logits, axis=0, keepdims=True))
    router = logit_exp / jnp.sum(logit_exp, axis=0, keepdims=True)
    chosen = choices[...]
    mask = (chosen == lax.broadcasted_iota(jnp.int32, (experts, length), 0)).astype(F32)
    earlier = (
        lax.broadcasted_iota(jnp.int32, (length, length), 0)
        < lax.broadcasted_iota(jnp.int32, (length, length), 1)
    ).astype(F32)
    counts = mm(mask.astype(BF), earlier.astype(BF))
    position = jnp.sum(mask * counts, axis=0, keepdims=True).astype(jnp.int32)
    target = jnp.where(position < cap, (chosen ^ shift_ref[0]) * cap + position, -1)
    gate = jnp.sum(mask * router, axis=0, keepdims=True)
    row = lax.broadcasted_iota(jnp.int32, (8, length), 0)
    packed = jnp.where(
        row == 0, gate, jnp.where(row == 1, target.astype(F32), chosen.astype(F32))
    )
    packed_out[:8, :] = packed
    packed_out[8:, :] = router
    place = (target == lax.broadcasted_iota(jnp.int32, (flat_slots, length), 0)).astype(F32)
    place = place.astype(BF)
    sent = (packed.T[:, :1] * cotangent[...].astype(F32)).astype(BF)
    normed_slots, grad_slots = mm(place, normed_two), mm(place, sent)
    for i, out in enumerate(slots_out):
        rows = slice(i * slot_rows, (i + 1) * slot_rows)
        out[:, :width] = normed_slots[rows].astype(BF)
        out[:, width:] = grad_slots[rows].astype(BF)


def expert_kernel(*refs):
    w_in, first, w_out, second = refs[0], refs[1:5], refs[5], refs[6:10]
    hidden, grad_pre = refs[10:12], refs[12:14]
    keep_a0, keep_b0, send_a, send_b, keep_b1, keep_a1 = refs[14:]
    rows, double = first[0].shape
    width = double // 2
    c = 0.7978845608028654
    places = (
        ((keep_a0, ()), (keep_b0, ()), (send_a, (0,)), (keep_b1, ())),
        ((keep_a1, ()), (send_b, (0,)), (send_a, (1,)), (send_b, (1,))),
    )
    for i, (pieces, outs) in enumerate(zip((first, second), places)):
        both = jnp.concatenate([p[...] for p in pieces], axis=0)
        pre = mm(both[:, :width], w_in[...])
        square = pre * pre
        t = jnp.tanh(c * pre * (1.0 + 0.044715 * square))
        act = (0.5 * pre * (1.0 + t)).astype(BF)
        slope = 0.5 * (1.0 + t) + 0.5 * c * pre * (1.0 - t * t) * (1.0 + 3 * 0.044715 * square)
        grad = (mm_nt(both[:, width:], w_out[...]) * slope).astype(BF)
        hidden[i][...] = act
        hidden[i].send()
        grad_pre[i][...] = grad
        grad_pre[i].send()
        result = mm(act, w_out[...]).astype(BF)
        back = mm_nt(grad, w_in[...]).astype(BF)
        for j, (out, slot) in enumerate(outs):
            out[(*slot, slice(None), slice(0, width))] = result[j * rows : (j + 1) * rows]
            out[(*slot, slice(None), slice(width, double))] = back[j * rows : (j + 1) * rows]
            if slot != (0,):
                out.send()


def expert_weights_kernel(*refs):
    pieces, units, (grad_in, grad_out) = refs[:16], refs[16:24], refs[24:]
    width = grad_in.shape[1]
    both = jnp.concatenate([p[...] for p in pieces], axis=0)
    act = jnp.concatenate([units[i][...] for i in (0, 1, 4, 5)], axis=0)
    pre = jnp.concatenate([units[i][...] for i in (2, 3, 6, 7)], axis=0)
    step = 256
    for i in range(width // step):
        grad_in[0, i * step : (i + 1) * step, :] = mm_tn(both[:, i * step : (i + 1) * step], pre)
    grad_in.send()
    for i in range(act.shape[1] // step):
        grad_out[0, i * step : (i + 1) * step, :] = mm_tn(
            act[:, i * step : (i + 1) * step], both[:, width:]
        )


def store_halves(core, h, left, right, keep, send):
    columns = left.shape[1]

    rows = slice(0, left.shape[0])

    @pl.when(core == h)
    def _():
        keep[rows, :columns] = left
        keep[rows, columns:] = right

    @pl.when(core != h)
    def _():
        send[rows, :columns] = left
        send[rows, columns:] = right


def diagonal_sums(scores):
    length = scores.shape[0]
    half = length // 2
    low, high = scores[:half], scores[half:]
    total = jnp.concatenate(
        [low[:, :half] + high[:, half:], low[:, half:], jnp.zeros_like(low[:, :half]), high[:, :half]],
        axis=1,
    )
    while total.shape[0] > 8:
        half = total.shape[0] // 2
        total = total[:half] + pltpu.roll(total[half:], 2 * length - half, 1)
    return total


def backward_kernel(
    heads,
    buckets_n,
    core_ref,
    packed_ref,
    gain_ffn,
    w_router,
    buckets,
    cotangent,
    residual_ref,
    w_output,
    value,
    probs_ref,
    normed_two,
    key,
    query,
    mixed,
    normed_one,
    w_value,
    w_query,
    w_key,
    tokens,
    gain_attn,
    *refs,
):
    returned, outs = refs[:-12], refs[-12:]
    layer_output, input_grad, keep_1, send_1, keep_2, send_2, small_out = outs[:7]
    ride = keep_1.shape[0] > keep_2.shape[0]
    small, grad_mixed_out, grad_value, grad_query, grad_key = outs[7:]
    core = core_ref[0]
    length, width = residual_ref.shape
    scale = (width // heads) ** (-0.5)
    experts = packed_ref.shape[0] - 8
    slot_rows = returned[0].shape[0]
    packed = packed_ref[...].T
    gate, goal, chosen = packed[:, 0:1], packed[:, 1:2], packed[:, 2:3]
    if len(returned) > 1:
        back = jnp.concatenate([r[...].astype(F32) for r in returned], axis=0).astype(BF)
    else:
        back = returned[0][...]
    place = (
        goal.astype(jnp.int32)
        == lax.broadcasted_iota(jnp.int32, (length, slot_rows * len(returned)), 1)
    ).astype(F32)
    back = mm(place.astype(BF), back)
    picked = back[:, :width]
    kept = (goal >= 0).astype(F32)
    mask = (
        chosen.astype(jnp.int32) == lax.broadcasted_iota(jnp.int32, (length, experts), 1)
    ).astype(F32)
    probs = packed[:, 8:]
    upstream = cotangent[...].astype(F32)
    residual = residual_ref[...]
    grad_gate = jnp.sum(upstream * picked, axis=1, keepdims=True) * kept
    grad_logits = ((grad_gate * gate) * (mask - probs)).astype(BF)
    grad_two = back[:, width:] + mm(grad_logits, w_router[...])
    scale_two = rms_scale(residual)
    weighted = grad_two * as_row(gain_ffn)
    grad_residual = (
        upstream
        + scale_two * weighted
        - residual * (scale_two**3 * jnp.mean(weighted * residual, axis=1, keepdims=True))
    )
    layer_output[...] = (residual + gate * kept * picked).astype(BF)
    layer_output.send()
    small[...] = jnp.zeros_like(small)
    small[1:2, :] = jnp.sum(grad_two * residual * scale_two, axis=0, keepdims=True)
    grad_attn = grad_residual.astype(BF)
    grad_mixed_out[...] = mm_nt(grad_attn, w_output[...]).astype(BF)
    small[2 : 2 + experts, :] = mm_tn(grad_logits, normed_two[...])
    pair = 2 * width // heads
    masks = half_masks(length, pair)
    sums = []
    for p in range(heads // 2):
        at = slice(p * pair, (p + 1) * pair)
        q2, k2, v2, g2 = query[:, at], key[:, at], value[:, at], grad_mixed_out[:, at]
        attn = probs_ref[2 * p], probs_ref[2 * p + 1]
        grads = []
        for half in (0, 1):
            e = attn[half].astype(F32)
            grad_probs = mm_nt(g2, v2 * masks[half])
            gs = e * (grad_probs - jnp.sum(e * grad_probs, axis=-1, keepdims=True))
            sums.append(diagonal_sums(gs))
            grads.append(gs.astype(BF))
        grad_v = mm_tn(
            jnp.concatenate(attn, axis=0),
            jnp.concatenate([g2 * masks[0], g2 * masks[1]], axis=0),
        )
        grad_q = mm(
            jnp.concatenate(grads, axis=1),
            jnp.concatenate([k2 * masks[0], k2 * masks[1]], axis=0),
        )
        grad_k = mm_tn(
            jnp.concatenate(grads, axis=0),
            jnp.concatenate([q2 * masks[0], q2 * masks[1]], axis=0),
        )
        grad_value[:, at] = grad_v.astype(BF)
        grad_query[:, at] = (grad_q * scale).astype(BF)
        grad_key[:, at] = (grad_k * scale).astype(BF)
    half = width // 2
    for h in (0, 1):
        at = slice(h * half, (h + 1) * half)
        left = mm_tn(mixed[:, at], grad_attn).astype(BF)
        right = mm_tn(normed_one[:, at], grad_value[...]).astype(BF)
        store_halves(core, h, left, right, keep_1, send_1)
    for h in (0, 1):
        at = slice(h * half, (h + 1) * half)
        left = mm_tn(normed_one[:, at], grad_query[...]).astype(BF)
        right = mm_tn(normed_one[:, at], grad_key[...]).astype(BF)
        store_halves(core, h, left, right, keep_2, send_2)
    send_2.send()
    keep_2.send()
    grad_one = mm_nt(grad_value[...], w_value[...])
    grad_one = grad_one + mm_nt(grad_query[...], w_query[...])
    grad_one = grad_one + mm_nt(grad_key[...], w_key[...])
    inputs = tokens[...].astype(F32)
    scale_one = rms_scale(inputs)
    small[0:1, :] = jnp.sum(grad_one * inputs * scale_one, axis=0, keepdims=True)
    weighted = grad_one * as_row(gain_attn)
    input_grad[...] = (
        grad_residual
        + scale_one * weighted
        - inputs * (scale_one**3 * jnp.mean(weighted * inputs, axis=1, keepdims=True))
    ).astype(BF)
    input_grad.send()
    total = jnp.concatenate(sums, axis=0)
    row = lax.broadcasted_iota(jnp.int32, total.shape, 0) % 8
    for bit in (1, 2, 4):
        total = jnp.where((row & bit) != 0, pltpu.roll(total, 2 * length - bit, 1), total)
    by_offset = jnp.sum(total.reshape(heads, 8, 2 * length), axis=1)
    small[2 + experts : 2 + experts + heads, :buckets_n] = lax.dot_general(
        by_offset,
        bucket_mask(buckets_n, buckets),
        (((1,), (1,)), ((), ())),
        precision=lax.Precision.HIGHEST,
        preferred_element_type=F32,
    )
    if ride:
        top, count = keep_2.shape[0], small.shape[0] // 2
        for out in (keep_1, send_1):
            out[top:, :width] = small[:count].astype(BF)
            out[top:, width:] = small[count:].astype(BF)
    else:
        small_out[...] = small[...]


def both(left, right, rows, columns):
    return left[rows, columns].astype(F32) + right[rows, columns].astype(F32)


def small_kernel(rows, own, got, gain_attn, gain_ffn, router, table, small):
    small[...] = both(own, got, slice(rows, None), slice(None))
    experts = router.shape[0]
    heads, buckets_n = table.shape
    gain_attn[...] = small[0:1, :].reshape(gain_attn.shape)
    gain_ffn[...] = small[1:2, :].reshape(gain_ffn.shape)
    router[...] = small[2 : 2 + experts, :]
    table[...] = small[2 + experts : 2 + experts + heads, :buckets_n]


def side_by_side(rows):
    half = rows.shape[0] // 2
    return jnp.concatenate([rows[:half], rows[half:]], axis=1)


def one_over_other(rows):
    half = rows.shape[1] // 2
    return jnp.concatenate([rows[:, :half], rows[:, half:]], axis=0)


def first_kernel(place_ref, own, got, keep_a, send_a, keep_b, send_b):
    half, columns = keep_b.shape
    for i, (bit, keep, send) in enumerate(((1, keep_a, send_a), (2, keep_b, send_b))):
        at = slice(i * columns, (i + 1) * columns)
        for out, side in ((keep, place_ref[bit]), (send, 1 - place_ref[bit])):
            rows = pl.ds(pl.multiple_of(side * half, half), half)
            out[:half, :] = both(own, got, rows, at).astype(BF)
    if own.shape[0] > 2 * half:
        tail = both(own, got, slice(2 * half, None), slice(None))
        for out in (keep_a, send_a):
            out[half:, :] = one_over_other(tail).astype(BF)


def second_kernel(place_ref, own_a, got_a, own_b, got_b, keep_a, send_a, keep_b, send_b):
    half = keep_b.shape[0]
    for bit, own, got, keep, send in (
        (2, own_a, got_a, keep_a, send_a),
        (1, own_b, got_b, keep_b, send_b),
    ):
        for out, side in ((keep, place_ref[bit]), (send, 1 - place_ref[bit])):
            rows = pl.ds(pl.multiple_of(side * half, half), half)
            out[:half, :] = both(own, got, rows, slice(None)).astype(BF)
    if own_a.shape[0] > 2 * half:
        tail = both(own_a, got_a, slice(2 * half, None), slice(None))
        for out in (keep_a, send_a):
            out[half:, :] = tail.astype(BF)


def join_kernel(place_ref, own_a, got_a, own_b, got_b, keep, send):
    rows, columns = own_b.shape
    half = rows // 2
    for out, side in ((keep, place_ref[3]), (send, 1 - place_ref[3])):
        at = pl.ds(pl.multiple_of(side * half, half), half)
        out[:half, :columns] = both(own_a, got_a, at, slice(None)).astype(BF)
        out[:half, columns:] = both(own_b, got_b, at, slice(None)).astype(BF)
    if own_a.shape[0] > rows:
        tail = both(own_a, got_a, slice(rows, None), slice(None))
        for out in (keep, send):
            out[half:, :] = side_by_side(tail).astype(BF)


def columns_kernel(rows, place_ref, own, got, keep, send):
    columns = keep.shape[1]
    for out, side in ((keep, place_ref[4]), (send, 1 - place_ref[4])):
        at = pl.ds(pl.multiple_of(side * columns, columns), columns)
        out[:rows, :] = both(own, got, slice(0, rows), at).astype(BF)
    if own.shape[0] > rows:
        tail = both(own, got, slice(rows, None), slice(None))
        for out in (keep, send):
            out[rows:, :] = one_over_other(tail).astype(BF)


def beside_kernel(bit, place_ref, own, far, out):
    columns = own.shape[1]
    for source, side in ((own, place_ref[bit]), (far, 1 - place_ref[bit])):
        out[:, pl.ds(pl.multiple_of(side * columns, columns), columns)] = source[...]


def stack_kernel(bit, place_ref, own, far, out_a, out_b):
    rows, columns = own.shape[0], out_a.shape[1]
    for source, side in ((own, place_ref[bit]), (far, 1 - place_ref[bit])):
        at = pl.ds(pl.multiple_of(side * rows, rows), rows)
        out_a[at, :] = source[:, :columns]
        out_b[at, :] = source[:, columns:]


def double_kernel(own_a, far_a, own_b, far_b, out_a, out_b):
    rows = own_a.shape[0]
    for source, at, out in ((own_a, 0, out_a), (far_a, 1, out_a), (own_b, 0, out_b), (far_b, 1, out_b)):
        out[at * rows : (at + 1) * rows, :] = source[...]


def half_kernel(place_ref, own_a, far_a, own_b, far_b, out):
    block, columns = own_a.shape[0] // 2, own_a.shape[1]
    sources = ((own_a, 0, 0, 1, 2), (far_a, 0, 1, 1, 2), (own_b, 1, 0, 2, 1), (far_b, 1, 1, 2, 1))
    for source, side, far, bit_1, bit_2 in sources:
        for i in (0, 1):
            at = ((place_ref[bit_1] ^ far) * 2 + (place_ref[bit_2] ^ i)) * block
            out[
                pl.ds(pl.multiple_of(at, block), block), side * columns : (side + 1) * columns
            ] = source[i * block : (i + 1) * block, :]


def finish_kernel(other, count, place_ref, *refs):
    sources, outs, (buffer, semaphores) = refs[:count], refs[-2 - 2 * count : -2], refs[-2:]
    rows, width = sources[0].shape[0], outs[0].shape[1]
    side = (1 - place_ref[0]) if other else place_ref[0]
    at = pl.ds(pl.multiple_of(side * rows, rows), rows)
    copies = []
    for m, out in enumerate(outs):
        left = m % 2 * width
        buffer[m] = sources[m // 2][:, left : left + width].astype(F32)
        copies.append(pltpu.make_async_copy(buffer.at[m], out.at[at, :], semaphores.at[m]))
        copies[-1].start()
    for copy in copies:
        copy.wait()


def pairs(size, k):
    return [(i, i ^ k) for i in range(size)]


def local(
    n_narrow,
    n_wide,
    tokens,
    cotangent,
    w_query,
    w_key,
    w_value,
    w_output,
    gain_attn,
    gain_ffn,
    w_router,
    bias_table,
    expert_in,
    expert_out,
    choices,
    router_levels,
    buckets,
):
    length, width = tokens.shape
    buckets_n, heads = bias_table.shape
    experts = w_router.shape[1]
    cap = (5 * length + 4 * experts - 1) // (4 * experts)
    flat_slots = experts * cap
    direct = n_wide <= 8
    narrow_at, wide_at = lax.axis_index("narrow"), lax.axis_index("wide")
    core_ref = (wide_at % 2).reshape(1)
    shift_ref = (wide_at if direct else jnp.zeros((), jnp.int32)).reshape(1)
    w_router = w_router.T
    rows_bf = shaped((length, width))
    attn_flops = 4 * length * length * width

    def across(x, k):
        return lax.ppermute(x, "narrow", pairs(n_narrow, k))

    def along(x, k):
        return lax.ppermute(x, "wide", pairs(n_wide, k))

    (
        normed_one,
        query,
        key,
        value,
        probs,
        mixed,
        residual,
        normed_two,
        packed,
        *slots,
    ) = call(
        functools.partial(front_kernel, heads, cap),
        [
            rows_bf,
            rows_bf,
            rows_bf,
            rows_bf,
            shaped((heads, length, length)),
            rows_bf,
            shaped((length, width), F32),
            rows_bf,
            shaped((8 + experts, length), F32),
        ]
        + [shaped((cap if direct else flat_slots, 2 * width))] * (n_wide if direct else 1),
        shift_ref,
        tokens,
        w_query,
        w_key,
        w_value,
        w_output,
        cotangent,
        gain_attn,
        gain_ffn,
        w_router,
        bias_table.T,
        buckets,
        choices.reshape(1, length),
        router_levels,
        smem=1,
        early=2,
        flops=8 * length * width * width + attn_flops,
        transcendentals=heads * length * length,
    )

    quarter = flat_slots // 4
    order = (0, 3, 1, 2)
    if direct:
        per = n_wide // 4
        near = jnp.split(along(jnp.concatenate(slots[1::2], axis=0), 1), n_wide // 2)
        parts = [jnp.concatenate([slots[2 * i], near[i]], axis=0) for i in order]
        parts = [[along(p, 2 * i) if i else p] for i, p in zip(order, parts)]
    else:
        moved = lax.all_to_all(slots[0], "wide", split_axis=0, concat_axis=0, tiled=True)
        parts = [[moved[i * quarter : (i + 1) * quarter]] for i in range(4)]

    def gather(a, b):
        a1, b2 = across(a, 1), across(b, 2)
        a2, b1 = across(a, 2), across(b, 1)
        a3, b3 = across(a1, 2), across(b2, 1)
        return [a, b, a1, b1, a2, b2, a3, b3]

    quarters = [jnp.concatenate(part, axis=0) for part in parts]

    def reduce(keep_a, send_a, keep_b, send_b):
        got_a, got_b = across(send_a, 1), across(send_b, 2)
        next_a = (keep_a[1].astype(F32) + got_a[1].astype(F32)).astype(BF)
        next_b = (keep_b[1].astype(F32) + got_b[1].astype(F32)).astype(BF)
        last_a, last_b = across(next_a, 2), across(next_b, 1)
        sum_a = keep_a[0].astype(F32) + got_a[0].astype(F32) + last_a.astype(F32)
        sum_b = keep_b[0].astype(F32) + got_b[0].astype(F32) + last_b.astype(F32)
        return sum_a.astype(BF), sum_b.astype(BF)

    w_in = expert_in.reshape(width, -1)
    w_out = expert_out.reshape(-1, width)
    units = w_in.shape[1]
    piece = shaped((2, quarter, 2 * width))
    unit_rows = shaped((4 * quarter, units))
    slot_piece = shaped((quarter, 2 * width))
    expert_flops = 2 * 8 * quarter * width * units
    def experts_of(rows):
        return call(
            expert_kernel,
            [unit_rows] * 4 + [slot_piece, slot_piece, piece, piece, slot_piece, slot_piece],
            w_in,
            *rows[:4],
            w_out,
            *rows[4:],
            early=5,
            flops=4 * expert_flops,
            transcendentals=8 * quarter * units,
        )

    def reduced(keep_a0, keep_b0, send_a, send_b, keep_b1, keep_a1):
        return reduce((keep_a0, keep_a1), send_a, (keep_b0, keep_b1), send_b)

    first = gather(*quarters[:2])
    quarters[2], quarters[3], first[3], first[4] = lax.optimization_barrier(
        (quarters[2], quarters[3], first[3], first[4])
    )
    done_1 = experts_of(first)
    a, b = quarters[2:]
    a1, b2 = across(a, 1), across(b, 2)
    a2, b1 = across(a, 2), across(b, 1)
    a1, b2, done_1 = lax.optimization_barrier((a1, b2, done_1))
    a3, b3 = across(a1, 2), across(b2, 1)
    second = [a, b, a1, b1, a2, b2, a3, b3]
    done_2 = experts_of(second)
    groups = [first, second]
    kept = done_1[:4] + done_2[:4]
    sums = [*reduced(*done_1[4:]), *reduced(*done_2[4:])]
    if direct:
        sums = [sums[order.index(i)] for i in range(4)]
        returned = [sums[k // per][k % per * cap : (k % per + 1) * cap] for k in range(n_wide)]
        returned = [returned[0]] + [along(returned[k], k) for k in range(1, n_wide)]
    else:
        returned = jnp.concatenate(sums, axis=0)
        returned = [lax.all_to_all(returned, "wide", split_axis=0, concat_axis=0, tiled=True)]
    grad_expert_in, grad_expert_out = call(
        expert_weights_kernel,
        [shaped(expert_in.shape, F32), shaped(expert_out.shape, F32)],
        *groups[0],
        *groups[1],
        *kept,
        flops=4 * expert_flops,
    )
    returned, grad_expert_in, grad_expert_out = lax.optimization_barrier(
        (returned, grad_expert_in, grad_expert_out)
    )

    half = width // 2
    small_rows = -(-(2 + experts + heads) // 32) * 32
    ride = small_rows if direct else 0
    layer_output, input_grad, keep_1, send_1, keep_2, send_2, small = call(
        functools.partial(backward_kernel, heads, buckets_n),
        [rows_bf, rows_bf]
        + [shaped((half + ride // 2, 2 * width))] * 2
        + [shaped((half, 2 * width))] * 2
        + [shaped((8, 128) if direct else (small_rows, width), F32)],
        core_ref,
        packed,
        gain_ffn,
        w_router,
        buckets,
        cotangent,
        residual,
        w_output,
        value,
        probs,
        normed_two,
        key,
        query,
        mixed,
        normed_one,
        w_value,
        w_query,
        w_key,
        tokens,
        gain_attn,
        *returned,
        smem=1,
        early=4,
        scratch=[pltpu.VMEM((small_rows, width), F32)] + [pltpu.VMEM((length, width), BF)] * 4,
        flops=16 * length * width * width + 3 * attn_flops,
    )

    place = jnp.stack(
        [wide_at % 2, narrow_at % 2, narrow_at // 2, wide_at // 2 % 2, wide_at // 4 % 2]
    ).astype(jnp.int32)
    deeper = [2**i for i in range(3, 20) if 2**i < n_wide]

    def hop(kernel, shapes, *args):
        return call(kernel, [shaped(x) for x in shapes], place, *args, smem=1, stream=False)

    def scatter(keep, send, tail):
        own_a, send_a, own_b, send_b = hop(
            first_kernel,
            [(half // 2 + tail, width)] * 2 + [(half // 2, width)] * 2,
            keep,
            along(send, 1),
        )
        own_a, send_a, own_b, send_b = hop(
            second_kernel,
            [(half // 4 + tail, width)] * 2 + [(half // 4, width)] * 2,
            own_a,
            across(send_a, 1),
            own_b,
            across(send_b, 2),
        )
        rows = half // 8
        own, other = hop(
            join_kernel,
            [(rows + tail // 2, 2 * width)] * 2,
            own_a,
            across(send_a, 2),
            own_b,
            across(send_b, 1),
        )
        own, other = hop(
            functools.partial(columns_kernel, rows),
            [(rows + tail, width)] * 2,
            own,
            along(other, 2),
        )
        got = along(other, 4)
        x = (own[:rows].astype(F32) + got[:rows].astype(F32)).astype(BF)
        for k in deeper:
            bit, size = wide_at // k % 2, x.shape[0] // 2
            other = lax.dynamic_slice_in_dim(x, (1 - bit) * size, size, 0)
            mine = lax.dynamic_slice_in_dim(x, bit * size, size, 0)
            x = (mine.astype(F32) + along(other, k).astype(F32)).astype(BF)
        return x, own, got

    def spread_out(x):
        step = functools.partial
        for k in reversed(deeper):
            bit, far = wide_at // k % 2, along(x, k)
            x = jnp.concatenate([jnp.where(bit == 0, x, far), jnp.where(bit == 0, far, x)], axis=0)
        (x,) = hop(step(beside_kernel, 4), [(half // 8, 2 * width)], x, along(x, 4))
        a, b = hop(step(stack_kernel, 3), [(half // 4, width)] * 2, x, along(x, 2))
        a, b = call(
            double_kernel,
            [shaped((half // 2, width))] * 2,
            a,
            across(a, 2),
            b,
            across(b, 1),
            stream=False,
        )
        (x,) = hop(half_kernel, [(half, 2 * width)], a, across(a, 1), b, across(b, 2))
        return x

    def finish(sources, outs=()):
        count = 2 * len(sources)
        return pl.pallas_call(
            functools.partial(finish_kernel, bool(outs), len(sources)),
            out_shape=(shaped((width, width), F32),) * count,
            in_specs=[pl.BlockSpec(memory_space=pltpu.SMEM)]
            + [pl.BlockSpec(memory_space=pltpu.VMEM)] * len(sources)
            + [pl.BlockSpec(memory_space=pl.ANY)] * len(outs),
            out_specs=(pl.BlockSpec(memory_space=pl.ANY),) * count,
            scratch_shapes=[
                pltpu.VMEM((count, half, width), F32),
                pltpu.SemaphoreType.DMA((count,)),
            ],
            input_output_aliases={1 + len(sources) + i: i for i in range(len(outs))},
            compiler_params=pltpu.CompilerParams(vmem_limit_bytes=LOW),
        )(place, *sources, *outs)

    part_1, own, got = scatter(keep_1, send_1, ride)
    part_2, _, _ = scatter(keep_2, send_2, 0)
    if not direct:
        own = lax.psum(small, ("narrow", "wide"))
        got = jnp.zeros_like(own)
    small = call(
        functools.partial(small_kernel, half // 8 if direct else 0),
        [
            shaped((width,), F32),
            shaped((width,), F32),
            shaped((experts, width), F32),
            shaped((heads, buckets_n), F32),
        ],
        own,
        got,
        scratch=[pltpu.VMEM((small_rows, width), F32)],
        stream=False,
    )
    part_1, part_2 = spread_out(part_1), spread_out(part_2)
    far_1, far_2 = along(part_1, 1), along(part_2, 1)
    near = finish((part_1, part_2))
    far_1, far_2, near, small = lax.optimization_barrier((far_1, far_2, near, small))
    grad_w_output, grad_w_value, grad_w_query, grad_w_key = finish((far_1, far_2), near)
    return (
        layer_output,
        input_grad,
        grad_w_query,
        grad_w_key,
        grad_w_value,
        grad_w_output,
        small[0],
        small[1],
        small[2].T,
        small[3].T,
        grad_expert_in,
        grad_expert_out,
    )


def solution(mesh):
    tokens_spec = P(("narrow", "wide"), None)
    experts_in_spec = P("wide", None, "narrow")
    experts_out_spec = P("wide", "narrow", None)
    in_specs = (
        (tokens_spec, tokens_spec)
        + (P(),) * 8
        + (experts_in_spec, experts_out_spec, tokens_spec, P(), P())
    )
    out_specs = (tokens_spec, tokens_spec) + (P(),) * 8 + (experts_in_spec, experts_out_spec)
    body = functools.partial(local, mesh.shape["narrow"], mesh.shape["wide"])
    return jax.shard_map(body, mesh=mesh, in_specs=in_specs, out_specs=out_specs, check_vma=False)
```

```python
import functools

import jax
import jax.numpy as jnp
from jax import lax
from jax.experimental import pallas as pl
from jax.experimental.pallas import tpu as pltpu
from jax.sharding import PartitionSpec as P

epsilon = 1e-06
BF = jnp.bfloat16
F32 = jnp.float32
HIGH = 60 * 2**20
LOW = 12 * 2**20


def mm(a, b):
    return lax.dot_general(a, b, (((1,), (0,)), ((), ())), preferred_element_type=F32)


def mm_nt(a, b):
    return lax.dot_general(a, b, (((1,), (1,)), ((), ())), preferred_element_type=F32)


def mm_tn(a, b):
    return lax.dot_general(a, b, (((0,), (0,)), ((), ())), preferred_element_type=F32)


def rms_scale(rows):
    return lax.rsqrt(jnp.mean(rows * rows, axis=-1, keepdims=True) + epsilon)


def half_masks(rows, width):
    lane = lax.broadcasted_iota(jnp.int32, (rows, width), 1)
    low = (lane < width // 2).astype(F32)
    return low.astype(BF), (1.0 - low).astype(BF)


def as_row(ref):
    return ref[...].reshape(1, -1)


def as_column(ref):
    return ref[...].reshape(-1, 1)


def bucket_mask(count, buckets):
    span = buckets.shape[0] + 1
    row = jnp.concatenate([buckets[...].reshape(1, -1), jnp.zeros((1, 1), jnp.int32)], axis=1)
    rows = pltpu.roll(jnp.broadcast_to(row, (8, span)), span // 2 + 1, 1)
    index = lax.broadcasted_iota(jnp.int32, (count, span), 0)
    return (index == rows[:1]).astype(F32)


class Fetched:
    def __init__(self, source, buffer, semaphore, later):
        self.buffer, self.copy = buffer, pltpu.make_async_copy(source, buffer, semaphore)
        self.later, self.waiting = later, True

    @property
    def shape(self):
        return self.buffer.shape

    def wait(self):
        if self.waiting:
            self.copy.wait()
            self.waiting = False
            while self.later:
                self.later.pop(0).copy.start()

    def __getitem__(self, index):
        self.wait()
        return self.buffer[index]


class Stored:
    def __init__(self, target, buffer, semaphore):
        self.buffer, self.copy = buffer, pltpu.make_async_copy(buffer, target, semaphore)
        self.sent = False
        self.dtype = buffer.dtype

    @property
    def shape(self):
        return self.buffer.shape

    def __getitem__(self, index):
        return self.buffer[index]

    def __setitem__(self, index, value):
        self.buffer[index] = value

    def send(self):
        if not self.sent:
            self.copy.start()
            self.sent = True


def large(x):
    return (
        len(x.shape) >= 2
        and x.shape[-2] % 16 == 0
        and x.shape[-1] % 128 == 0
        and x.size * x.dtype.itemsize >= 2**16
    )


def call(kernel, outs, *args, flops=0, transcendentals=0, scratch=(), smem=0, stream=True, early=99):
    out_bytes = sum(o.size * o.dtype.itemsize for o in outs)
    in_bytes = sum(a.size * a.dtype.itemsize for a in args)
    large_in = [stream and i >= smem and large(x) for i, x in enumerate(args)]
    large_out = [stream and large(x) for x in outs]
    moved = [x for x, flag in zip(args + tuple(outs), large_in + large_out) if flag]

    def body(*refs):
        operands, results = refs[: len(args)], refs[len(args) : len(args) + len(outs)]
        rest = refs[len(args) + len(outs) :]
        buffers = iter(rest[: len(moved)])
        semaphores = rest[len(moved)] if moved else None
        count = iter(range(len(moved)))
        later = []
        operands = [
            Fetched(ref, next(buffers), semaphores.at[next(count)], later) if flag else ref
            for ref, flag in zip(operands, large_in)
        ]
        fetched = [x for x in operands if isinstance(x, Fetched)]
        later += fetched[early:]
        for x in fetched[:early]:
            x.copy.start()
        results = [
            Stored(ref, next(buffers), semaphores.at[next(count)]) if flag else ref
            for ref, flag in zip(results, large_out)
        ]
        kernel(*operands, *results, *rest[len(moved) + bool(moved) :])
        for x in operands:
            if isinstance(x, Fetched):
                x.wait()
        for x in results:
            if isinstance(x, Stored):
                x.send()
        for x in results:
            if isinstance(x, Stored):
                x.copy.wait()

    def spec(flag):
        return pl.BlockSpec(memory_space=pl.ANY if flag else pltpu.VMEM)

    scratches = [pltpu.VMEM(x.shape, x.dtype) for x in moved]
    if moved:
        scratches.append(pltpu.SemaphoreType.DMA((len(moved),)))
    return pl.pallas_call(
        body,
        out_shape=tuple(outs),
        in_specs=[
            pl.BlockSpec(memory_space=pltpu.SMEM) if i < smem else spec(flag)
            for i, flag in enumerate(large_in)
        ],
        out_specs=tuple(spec(flag) for flag in large_out),
        scratch_shapes=scratches + list(scratch),
        compiler_params=pltpu.CompilerParams(vmem_limit_bytes=HIGH if stream else LOW),
        cost_estimate=pl.CostEstimate(
            flops=flops, transcendentals=transcendentals, bytes_accessed=in_bytes + out_bytes
        ),
    )(*args)


def shaped(shape, dtype=BF):
    return jax.ShapeDtypeStruct(shape, dtype)


def spread_diagonals(rows, length):
    while rows.shape[0] < length // 2:
        rows = jnp.concatenate([rows, pltpu.roll(rows, rows.shape[0], 1)], axis=0)
    half = length // 2
    high = jnp.concatenate([rows[:, 3 * half :], rows[:, :half]], axis=1)
    return jnp.concatenate([rows[:, :length], high], axis=0)


def front_kernel(
    heads,
    cap,
    shift_ref,
    tokens,
    w_query,
    w_key,
    w_value,
    w_output,
    cotangent,
    gain_attn,
    gain_ffn,
    w_router,
    table,
    buckets,
    choices,
    levels,
    normed_one_out,
    query_out,
    key_out,
    value_out,
    probs_out,
    mixed_out,
    residual_out,
    normed_two_out,
    packed_out,
    *slots_out,
):
    length, width = tokens.shape
    scale = (width // heads) ** (-0.5)
    experts = w_router.shape[0]
    flat_slots = sum(out.shape[0] for out in slots_out)
    inputs = tokens[...].astype(F32)
    normed = (inputs * rms_scale(inputs) * as_row(gain_attn)).astype(BF)
    normed_one_out[...] = normed
    normed_one_out.send()
    query_out[...] = mm(normed, w_query[...]).astype(BF)
    key_out[...] = mm(normed, w_key[...]).astype(BF)
    value_out[...] = mm(normed, w_value[...]).astype(BF)
    for out in (query_out, key_out, value_out):
        out.send()
    by_offset = lax.dot_general(
        table[...],
        bucket_mask(table.shape[1], buckets),
        (((1,), (0,)), ((), ())),
        precision=lax.Precision.HIGHEST,
        preferred_element_type=F32,
    )
    rolled = jnp.broadcast_to(by_offset[:, None, :], (heads, 8, 2 * length))
    rolled = rolled.reshape(8 * heads, 2 * length)
    row = lax.broadcasted_iota(jnp.int32, rolled.shape, 0) % 8
    for bit in (1, 2, 4):
        rolled = jnp.where((row & bit) != 0, pltpu.roll(rolled, bit, 1), rolled)
    pair = 2 * width // heads
    masks = half_masks(length, pair)
    for p in range(heads // 2):
        at = slice(p * pair, (p + 1) * pair)
        q2, k2, v2 = query_out[:, at], key_out[:, at], value_out[:, at]
        probs = []
        for half in (0, 1):
            h = 2 * p + half
            bias = spread_diagonals(rolled[8 * h : 8 * h + 8], length)
            scores = mm_nt(q2, k2 * masks[half]) * scale + bias
            e = jnp.exp(scores - jnp.max(scores, axis=-1, keepdims=True))
            e = (e * (1.0 / jnp.sum(e, axis=-1, keepdims=True))).astype(BF)
            probs_out[h] = e
            probs.append(e)
        mixed_out[:, at] = mm(
            jnp.concatenate(probs, axis=1),
            jnp.concatenate([v2 * masks[0], v2 * masks[1]], axis=0),
        ).astype(BF)
    probs_out.send()
    mixed_out.send()
    residual = inputs + mm(mixed_out[...], w_output[...])
    residual_out[...] = residual
    residual_out.send()
    normed_two = (residual * rms_scale(residual) * as_row(gain_ffn)).astype(BF)
    normed_two_out[...] = normed_two
    normed_two_out.send()
    logits = mm_nt(w_router[...], normed_two) + 0.25 * as_column(levels).astype(F32)
    logit_exp = jnp.exp(logits - jnp.max(logits, axis=0, keepdims=True))
    router = logit_exp / jnp.sum(logit_exp, axis=0, keepdims=True)
    chosen = choices[...]
    mask = (chosen == lax.broadcasted_iota(jnp.int32, (experts, length), 0)).astype(F32)
    earlier = (
        lax.broadcasted_iota(jnp.int32, (length, length), 0)
        < lax.broadcasted_iota(jnp.int32, (length, length), 1)
    ).astype(F32)
    counts = mm(mask.astype(BF), earlier.astype(BF))
    position = jnp.sum(mask * counts, axis=0, keepdims=True).astype(jnp.int32)
    slot = chosen ^ shift_ref[0]
    if len(slots_out) > 1:
        slot = (slot & 1) * (experts // 2) + (slot >> 1)
    target = jnp.where(position < cap, slot * cap + position, -1)
    gate = jnp.sum(mask * router, axis=0, keepdims=True)
    row = lax.broadcasted_iota(jnp.int32, (8, length), 0)
    packed = jnp.where(
        row == 0, gate, jnp.where(row == 1, target.astype(F32), chosen.astype(F32))
    )
    packed_out[:8, :] = packed
    packed_out[8:, :] = router
    place = (target == lax.broadcasted_iota(jnp.int32, (flat_slots, length), 0)).astype(F32)
    place = place.astype(BF)
    sent = (packed.T[:, :1] * cotangent[...].astype(F32)).astype(BF)
    normed_slots, grad_slots = mm(place, normed_two), mm(place, sent)
    first = 0
    for out in slots_out:
        rows = slice(first, first + out.shape[0])
        first += out.shape[0]
        out[:, :width] = normed_slots[rows].astype(BF)
        out[:, width:] = grad_slots[rows].astype(BF)


def expert_kernel(*refs):
    w_in, first, w_out, second = refs[0], refs[1:5], refs[5], refs[6:10]
    hidden, grad_pre = refs[10:12], refs[12:14]
    keep_a0, keep_b0, send_a, send_b, keep_b1, keep_a1 = refs[14:]
    rows, double = first[0].shape
    width = double // 2
    c = 0.7978845608028654
    places = (
        ((keep_a0, ()), (keep_b0, ()), (send_a, (0,)), (keep_b1, ())),
        ((keep_a1, ()), (send_b, (0,)), (send_a, (1,)), (send_b, (1,))),
    )
    for i, (pieces, outs) in enumerate(zip((first, second), places)):
        both = jnp.concatenate([p[...] for p in pieces], axis=0)
        pre = mm(both[:, :width], w_in[...])
        square = pre * pre
        t = jnp.tanh(c * pre * (1.0 + 0.044715 * square))
        act = (0.5 * pre * (1.0 + t)).astype(BF)
        slope = 0.5 * (1.0 + t) + 0.5 * c * pre * (1.0 - t * t) * (1.0 + 3 * 0.044715 * square)
        grad = (mm_nt(both[:, width:], w_out[...]) * slope).astype(BF)
        hidden[i][...] = act
        hidden[i].send()
        grad_pre[i][...] = grad
        grad_pre[i].send()
        result = mm(act, w_out[...]).astype(BF)
        back = mm_nt(grad, w_in[...]).astype(BF)
        for j, (out, slot) in enumerate(outs):
            out[(*slot, slice(None), slice(0, width))] = result[j * rows : (j + 1) * rows]
            out[(*slot, slice(None), slice(width, double))] = back[j * rows : (j + 1) * rows]
            if slot != (0,):
                out.send()


def expert_weights_kernel(*refs):
    pieces, units, (grad_in, grad_out) = refs[:16], refs[16:24], refs[24:]
    width = grad_in.shape[1]
    both = jnp.concatenate([p[...] for p in pieces], axis=0)
    act = jnp.concatenate([units[i][...] for i in (0, 1, 4, 5)], axis=0)
    pre = jnp.concatenate([units[i][...] for i in (2, 3, 6, 7)], axis=0)
    step = 256
    for i in range(width // step):
        grad_in[0, i * step : (i + 1) * step, :] = mm_tn(both[:, i * step : (i + 1) * step], pre)
    grad_in.send()
    for i in range(act.shape[1] // step):
        grad_out[0, i * step : (i + 1) * step, :] = mm_tn(
            act[:, i * step : (i + 1) * step], both[:, width:]
        )


def store_halves(core, h, left, right, keep, send):
    columns = left.shape[1]

    rows = slice(0, left.shape[0])

    @pl.when(core == h)
    def _():
        keep[rows, :columns] = left
        keep[rows, columns:] = right

    @pl.when(core != h)
    def _():
        send[rows, :columns] = left
        send[rows, columns:] = right


def diagonal_sums(scores):
    length = scores.shape[0]
    half = length // 2
    low, high = scores[:half], scores[half:]
    total = jnp.concatenate(
        [low[:, :half] + high[:, half:], low[:, half:], jnp.zeros_like(low[:, :half]), high[:, :half]],
        axis=1,
    )
    while total.shape[0] > 8:
        half = total.shape[0] // 2
        total = total[:half] + pltpu.roll(total[half:], 2 * length - half, 1)
    return total


def backward_kernel(
    heads,
    buckets_n,
    core_ref,
    packed_ref,
    gain_ffn,
    w_router,
    buckets,
    cotangent,
    residual_ref,
    w_output,
    value,
    probs_ref,
    normed_two,
    key,
    query,
    mixed,
    normed_one,
    w_value,
    w_query,
    w_key,
    tokens,
    gain_attn,
    *refs,
):
    returned, outs = refs[:-12], refs[-12:]
    layer_output, input_grad, keep_1, send_1, keep_2, send_2, small_out = outs[:7]
    ride = keep_1.shape[0] > keep_2.shape[0]
    small, grad_mixed_out, grad_value, grad_query, grad_key = outs[7:]
    core = core_ref[0]
    length, width = residual_ref.shape
    scale = (width // heads) ** (-0.5)
    experts = packed_ref.shape[0] - 8
    slot_rows = returned[0].shape[0]
    packed = packed_ref[...].T
    gate, goal, chosen = packed[:, 0:1], packed[:, 1:2], packed[:, 2:3]
    if len(returned) > 1:
        back = jnp.concatenate([r[...].astype(F32) for r in returned], axis=0).astype(BF)
    else:
        back = returned[0][...]
    place = (
        goal.astype(jnp.int32)
        == lax.broadcasted_iota(jnp.int32, (length, slot_rows * len(returned)), 1)
    ).astype(F32)
    back = mm(place.astype(BF), back)
    picked = back[:, :width]
    kept = (goal >= 0).astype(F32)
    mask = (
        chosen.astype(jnp.int32) == lax.broadcasted_iota(jnp.int32, (length, experts), 1)
    ).astype(F32)
    probs = packed[:, 8:]
    upstream = cotangent[...].astype(F32)
    residual = residual_ref[...]
    grad_gate = jnp.sum(upstream * picked, axis=1, keepdims=True) * kept
    grad_logits = ((grad_gate * gate) * (mask - probs)).astype(BF)
    grad_two = back[:, width:] + mm(grad_logits, w_router[...])
    scale_two = rms_scale(residual)
    weighted = grad_two * as_row(gain_ffn)
    grad_residual = (
        upstream
        + scale_two * weighted
        - residual * (scale_two**3 * jnp.mean(weighted * residual, axis=1, keepdims=True))
    )
    layer_output[...] = (residual + gate * kept * picked).astype(BF)
    layer_output.send()
    small[...] = jnp.zeros_like(small)
    small[1:2, :] = jnp.sum(grad_two * residual * scale_two, axis=0, keepdims=True)
    grad_attn = grad_residual.astype(BF)
    grad_mixed_out[...] = mm_nt(grad_attn, w_output[...]).astype(BF)
    small[2 : 2 + experts, :] = mm_tn(grad_logits, normed_two[...])
    pair = 2 * width // heads
    masks = half_masks(length, pair)
    sums = []
    for p in range(heads // 2):
        at = slice(p * pair, (p + 1) * pair)
        q2, k2, v2, g2 = query[:, at], key[:, at], value[:, at], grad_mixed_out[:, at]
        attn = probs_ref[2 * p], probs_ref[2 * p + 1]
        grads = []
        for half in (0, 1):
            e = attn[half].astype(F32)
            grad_probs = mm_nt(g2, v2 * masks[half])
            gs = e * (grad_probs - jnp.sum(e * grad_probs, axis=-1, keepdims=True))
            sums.append(diagonal_sums(gs))
            grads.append(gs.astype(BF))
        grad_v = mm_tn(
            jnp.concatenate(attn, axis=0),
            jnp.concatenate([g2 * masks[0], g2 * masks[1]], axis=0),
        )
        grad_q = mm(
            jnp.concatenate(grads, axis=1),
            jnp.concatenate([k2 * masks[0], k2 * masks[1]], axis=0),
        )
        grad_k = mm_tn(
            jnp.concatenate(grads, axis=0),
            jnp.concatenate([q2 * masks[0], q2 * masks[1]], axis=0),
        )
        grad_value[:, at] = grad_v.astype(BF)
        grad_query[:, at] = (grad_q * scale).astype(BF)
        grad_key[:, at] = (grad_k * scale).astype(BF)
    half = width // 2
    for h in (0, 1):
        at = slice(h * half, (h + 1) * half)
        left = mm_tn(mixed[:, at], grad_attn).astype(BF)
        right = mm_tn(normed_one[:, at], grad_value[...]).astype(BF)
        store_halves(core, h, left, right, keep_1, send_1)
    for h in (0, 1):
        at = slice(h * half, (h + 1) * half)
        left = mm_tn(normed_one[:, at], grad_query[...]).astype(BF)
        right = mm_tn(normed_one[:, at], grad_key[...]).astype(BF)
        store_halves(core, h, left, right, keep_2, send_2)
    send_2.send()
    keep_2.send()
    grad_one = mm_nt(grad_value[...], w_value[...])
    grad_one = grad_one + mm_nt(grad_query[...], w_query[...])
    grad_one = grad_one + mm_nt(grad_key[...], w_key[...])
    inputs = tokens[...].astype(F32)
    scale_one = rms_scale(inputs)
    small[0:1, :] = jnp.sum(grad_one * inputs * scale_one, axis=0, keepdims=True)
    weighted = grad_one * as_row(gain_attn)
    input_grad[...] = (
        grad_residual
        + scale_one * weighted
        - inputs * (scale_one**3 * jnp.mean(weighted * inputs, axis=1, keepdims=True))
    ).astype(BF)
    input_grad.send()
    total = jnp.concatenate(sums, axis=0)
    row = lax.broadcasted_iota(jnp.int32, total.shape, 0) % 8
    for bit in (1, 2, 4):
        total = jnp.where((row & bit) != 0, pltpu.roll(total, 2 * length - bit, 1), total)
    by_offset = jnp.sum(total.reshape(heads, 8, 2 * length), axis=1)
    small[2 + experts : 2 + experts + heads, :buckets_n] = lax.dot_general(
        by_offset,
        bucket_mask(buckets_n, buckets),
        (((1,), (1,)), ((), ())),
        precision=lax.Precision.HIGHEST,
        preferred_element_type=F32,
    )
    if ride:
        top, count = keep_2.shape[0], small.shape[0] // 2
        for out in (keep_1, send_1):
            out[top:, :width] = small[:count].astype(BF)
            out[top:, width:] = small[count:].astype(BF)
    else:
        small_out[...] = small[...]


def both(left, right, rows, columns):
    return left[rows, columns].astype(F32) + right[rows, columns].astype(F32)


def small_kernel(rows, own, got, gain_attn, gain_ffn, router, table, small):
    small[...] = both(own, got, slice(rows, None), slice(None))
    experts = router.shape[0]
    heads, buckets_n = table.shape
    gain_attn[...] = small[0:1, :].reshape(gain_attn.shape)
    gain_ffn[...] = small[1:2, :].reshape(gain_ffn.shape)
    router[...] = small[2 : 2 + experts, :]
    table[...] = small[2 + experts : 2 + experts + heads, :buckets_n]


def side_by_side(rows):
    half = rows.shape[0] // 2
    return jnp.concatenate([rows[:half], rows[half:]], axis=1)


def one_over_other(rows):
    half = rows.shape[1] // 2
    return jnp.concatenate([rows[:, :half], rows[:, half:]], axis=0)


def first_kernel(place_ref, own, got, keep_a, send_a, keep_b, send_b):
    half, columns = keep_b.shape
    for i, (bit, keep, send) in enumerate(((1, keep_a, send_a), (2, keep_b, send_b))):
        at = slice(i * columns, (i + 1) * columns)
        for out, side in ((keep, place_ref[bit]), (send, 1 - place_ref[bit])):
            rows = pl.ds(pl.multiple_of(side * half, half), half)
            out[:half, :] = both(own, got, rows, at).astype(BF)
    if own.shape[0] > 2 * half:
        tail = both(own, got, slice(2 * half, None), slice(None))
        for out in (keep_a, send_a):
            out[half:, :] = one_over_other(tail).astype(BF)


def second_kernel(place_ref, own_a, got_a, own_b, got_b, keep_a, send_a, keep_b, send_b):
    half = keep_b.shape[0]
    for bit, own, got, keep, send in (
        (2, own_a, got_a, keep_a, send_a),
        (1, own_b, got_b, keep_b, send_b),
    ):
        for out, side in ((keep, place_ref[bit]), (send, 1 - place_ref[bit])):
            rows = pl.ds(pl.multiple_of(side * half, half), half)
            out[:half, :] = both(own, got, rows, slice(None)).astype(BF)
    if own_a.shape[0] > 2 * half:
        tail = both(own_a, got_a, slice(2 * half, None), slice(None))
        for out in (keep_a, send_a):
            out[half:, :] = tail.astype(BF)


def rows_kernel(place_ref, own, got, keep, send):
    half = keep.shape[0]
    for out, side in ((keep, place_ref[3]), (send, 1 - place_ref[3])):
        rows = pl.ds(pl.multiple_of(side * half, half), half)
        out[...] = both(own, got, rows, slice(None)).astype(BF)


def pick_kernel(place_ref, own_a, got_a, own_b, got_b, keep, send):
    left = both(own_a, got_a, slice(None), slice(None)).astype(BF)
    right = both(own_b, got_b, slice(None), slice(None)).astype(BF)

    @pl.when(place_ref[4] == 0)
    def _():
        keep[...] = left
        send[...] = right

    @pl.when(place_ref[4] != 0)
    def _():
        keep[...] = right
        send[...] = left


def join_kernel(place_ref, own_a, got_a, own_b, got_b, keep, send):
    rows, columns = own_b.shape
    half = rows // 2
    for out, side in ((keep, place_ref[3]), (send, 1 - place_ref[3])):
        at = pl.ds(pl.multiple_of(side * half, half), half)
        out[:half, :columns] = both(own_a, got_a, at, slice(None)).astype(BF)
        out[:half, columns:] = both(own_b, got_b, at, slice(None)).astype(BF)
    if own_a.shape[0] > rows:
        tail = both(own_a, got_a, slice(rows, None), slice(None))
        for out in (keep, send):
            out[half:, :] = side_by_side(tail).astype(BF)


def columns_kernel(rows, place_ref, own, got, keep, send):
    columns = keep.shape[1]
    for out, side in ((keep, place_ref[4]), (send, 1 - place_ref[4])):
        at = pl.ds(pl.multiple_of(side * columns, columns), columns)
        out[:rows, :] = both(own, got, slice(0, rows), at).astype(BF)
    if own.shape[0] > rows:
        tail = both(own, got, slice(rows, None), slice(None))
        for out in (keep, send):
            out[rows:, :] = one_over_other(tail).astype(BF)


def beside_kernel(bit, place_ref, own, far, out):
    columns = own.shape[1]
    for source, side in ((own, place_ref[bit]), (far, 1 - place_ref[bit])):
        out[:, pl.ds(pl.multiple_of(side * columns, columns), columns)] = source[...]


def stack_kernel(bit, place_ref, own, far, out_a, out_b):
    rows, columns = own.shape[0], out_a.shape[1]
    for source, side in ((own, place_ref[bit]), (far, 1 - place_ref[bit])):
        at = pl.ds(pl.multiple_of(side * rows, rows), rows)
        out_a[at, :] = source[:, :columns]
        out_b[at, :] = source[:, columns:]


def double_kernel(own_a, far_a, own_b, far_b, out_a, out_b):
    rows = own_a.shape[0]
    for source, at, out in ((own_a, 0, out_a), (far_a, 1, out_a), (own_b, 0, out_b), (far_b, 1, out_b)):
        out[at * rows : (at + 1) * rows, :] = source[...]


def half_kernel(parts, place_ref, own_a, far_a, own_b, far_b, out):
    block, columns = own_a.shape[0] // 2, own_a.shape[1]
    rows = block // parts
    sources = ((own_a, 0, 0, 1, 2), (far_a, 0, 1, 1, 2), (own_b, 1, 0, 2, 1), (far_b, 1, 1, 2, 1))
    for source, side, far, bit_1, bit_2 in sources:
        for i in (0, 1):
            at = ((place_ref[bit_1] ^ far) * 2 + (place_ref[bit_2] ^ i)) * rows
            for part in range(parts):
                out[
                    pl.ds(pl.multiple_of(at + part * 4 * rows, rows), rows),
                    side * columns : (side + 1) * columns,
                ] = source[i * block + part * rows : i * block + (part + 1) * rows, :]


def finish_kernel(other, count, place_ref, *refs):
    sources, outs, (buffer, semaphores) = refs[:count], refs[-2 - 2 * count : -2], refs[-2:]
    rows, width = sources[0].shape[0], outs[0].shape[1]
    side = (1 - place_ref[0]) if other else place_ref[0]
    at = pl.ds(pl.multiple_of(side * rows, rows), rows)
    copies = []
    for m, out in enumerate(outs):
        left = m % 2 * width
        buffer[m] = sources[m // 2][:, left : left + width].astype(F32)
        copies.append(pltpu.make_async_copy(buffer.at[m], out.at[at, :], semaphores.at[m]))
        copies[-1].start()
    for copy in copies:
        copy.wait()


def pairs(size, k):
    return [(i, i ^ k) for i in range(size)]


def local(
    n_narrow,
    n_wide,
    tokens,
    cotangent,
    w_query,
    w_key,
    w_value,
    w_output,
    gain_attn,
    gain_ffn,
    w_router,
    bias_table,
    expert_in,
    expert_out,
    choices,
    router_levels,
    buckets,
):
    length, width = tokens.shape
    buckets_n, heads = bias_table.shape
    experts = w_router.shape[1]
    cap = (5 * length + 4 * experts - 1) // (4 * experts)
    flat_slots = experts * cap
    direct = n_wide <= 8
    slot_counts = [cap] * (n_wide // 2) + [flat_slots // 2] if direct else [flat_slots]
    narrow_at, wide_at = lax.axis_index("narrow"), lax.axis_index("wide")
    core_ref = (wide_at % 2).reshape(1)
    shift_ref = (wide_at if direct else jnp.zeros((), jnp.int32)).reshape(1)
    w_router = w_router.T
    rows_bf = shaped((length, width))
    attn_flops = 4 * length * length * width

    def across(x, k):
        return lax.ppermute(x, "narrow", pairs(n_narrow, k))

    def along(x, k):
        return lax.ppermute(x, "wide", pairs(n_wide, k))

    (
        normed_one,
        query,
        key,
        value,
        probs,
        mixed,
        residual,
        normed_two,
        packed,
        *slots,
    ) = call(
        functools.partial(front_kernel, heads, cap),
        [
            rows_bf,
            rows_bf,
            rows_bf,
            rows_bf,
            shaped((heads, length, length)),
            rows_bf,
            shaped((length, width), F32),
            rows_bf,
            shaped((8 + experts, length), F32),
        ]
        + [shaped((n, 2 * width)) for n in slot_counts],
        shift_ref,
        tokens,
        w_query,
        w_key,
        w_value,
        w_output,
        cotangent,
        gain_attn,
        gain_ffn,
        w_router,
        bias_table.T,
        buckets,
        choices.reshape(1, length),
        router_levels,
        smem=1,
        early=2,
        flops=8 * length * width * width + attn_flops,
        transcendentals=heads * length * length,
    )

    quarter = flat_slots // 4
    order = (0, 2, 1, 3)
    if direct:
        per = n_wide // 4
        near = jnp.split(along(slots[-1], 1), n_wide // 2)
        parts = [jnp.concatenate([slots[i], near[i]], axis=0) for i in order]
        parts = [[along(p, 2 * i) if i else p] for i, p in zip(order, parts)]
    else:
        moved = lax.all_to_all(slots[0], "wide", split_axis=0, concat_axis=0, tiled=True)
        parts = [[moved[i * quarter : (i + 1) * quarter]] for i in range(4)]

    def gather(a, b):
        a1, b2 = across(a, 1), across(b, 2)
        a2, b1 = across(a, 2), across(b, 1)
        a3, b3 = across(a1, 2), across(b2, 1)
        return [a, b, a1, b1, a2, b2, a3, b3]

    quarters = [jnp.concatenate(part, axis=0) for part in parts]

    def hop_one(keep_a0, keep_b0, send_a, send_b, keep_b1, keep_a1):
        got_a, got_b = across(send_a, 1), across(send_b, 2)
        next_a = (keep_a1.astype(F32) + got_a[1].astype(F32)).astype(BF)
        next_b = (keep_b1.astype(F32) + got_b[1].astype(F32)).astype(BF)
        return [keep_a0, keep_b0, got_a, got_b, next_a, next_b]

    def hop_two(keep_a0, keep_b0, got_a, got_b, next_a, next_b):
        last_a, last_b = across(next_a, 2), across(next_b, 1)
        sum_a = keep_a0.astype(F32) + got_a[0].astype(F32) + last_a.astype(F32)
        sum_b = keep_b0.astype(F32) + got_b[0].astype(F32) + last_b.astype(F32)
        return [sum_a.astype(BF), sum_b.astype(BF)]

    def reduce(keep_a, send_a, keep_b, send_b):
        got_a, got_b = across(send_a, 1), across(send_b, 2)
        next_a = (keep_a[1].astype(F32) + got_a[1].astype(F32)).astype(BF)
        next_b = (keep_b[1].astype(F32) + got_b[1].astype(F32)).astype(BF)
        last_a, last_b = across(next_a, 2), across(next_b, 1)
        sum_a = keep_a[0].astype(F32) + got_a[0].astype(F32) + last_a.astype(F32)
        sum_b = keep_b[0].astype(F32) + got_b[0].astype(F32) + last_b.astype(F32)
        return sum_a.astype(BF), sum_b.astype(BF)

    w_in = expert_in.reshape(width, -1)
    w_out = expert_out.reshape(-1, width)
    units = w_in.shape[1]
    piece = shaped((2, quarter, 2 * width))
    unit_rows = shaped((4 * quarter, units))
    slot_piece = shaped((quarter, 2 * width))
    expert_flops = 2 * 8 * quarter * width * units
    def experts_of(rows):
        return call(
            expert_kernel,
            [unit_rows] * 4 + [slot_piece, slot_piece, piece, piece, slot_piece, slot_piece],
            w_in,
            *rows[:4],
            w_out,
            *rows[4:],
            early=5,
            flops=4 * expert_flops,
            transcendentals=8 * quarter * units,
        )

    def reduced(keep_a0, keep_b0, send_a, send_b, keep_b1, keep_a1):
        return reduce((keep_a0, keep_a1), send_a, (keep_b0, keep_b1), send_b)

    first = gather(*quarters[:2])
    quarters[2], quarters[3], first[3], first[4] = lax.optimization_barrier(
        (quarters[2], quarters[3], first[3], first[4])
    )
    second = gather(*quarters[2:])
    done_1, done_2 = experts_of(first), experts_of(second)
    groups = [first, second]
    kept = done_1[:4] + done_2[:4]
    h1 = hop_one(*done_1[4:])
    done_2, h1 = lax.optimization_barrier((done_2, h1))
    h2 = hop_one(*done_2[4:])
    sums = hop_two(*h1) + hop_two(*h2)
    if direct:
        sums = [sums[order.index(i)] for i in range(4)]
        returned = [sums[k // per][k % per * cap : (k % per + 1) * cap] for k in range(n_wide)]
        returned = [returned[0]] + [along(returned[k], k) for k in range(1, n_wide)]
        returned = returned[::2] + returned[1::2]
    else:
        returned = jnp.concatenate(sums, axis=0)
        returned = [lax.all_to_all(returned, "wide", split_axis=0, concat_axis=0, tiled=True)]
    grad_expert_in, grad_expert_out = call(
        expert_weights_kernel,
        [shaped(expert_in.shape, F32), shaped(expert_out.shape, F32)],
        *groups[0],
        *groups[1],
        *kept,
        flops=4 * expert_flops,
    )
    returned, grad_expert_in, grad_expert_out = lax.optimization_barrier(
        (returned, grad_expert_in, grad_expert_out)
    )

    half = width // 2
    small_rows = -(-(2 + experts + heads) // 32) * 32
    ride = small_rows if direct else 0
    layer_output, input_grad, keep_1, send_1, keep_2, send_2, small = call(
        functools.partial(backward_kernel, heads, buckets_n),
        [rows_bf, rows_bf]
        + [shaped((half + ride // 2, 2 * width))] * 2
        + [shaped((half, 2 * width))] * 2
        + [shaped((8, 128) if direct else (small_rows, width), F32)],
        core_ref,
        packed,
        gain_ffn,
        w_router,
        buckets,
        cotangent,
        residual,
        w_output,
        value,
        probs,
        normed_two,
        key,
        query,
        mixed,
        normed_one,
        w_value,
        w_query,
        w_key,
        tokens,
        gain_attn,
        *returned,
        smem=1,
        early=4,
        scratch=[pltpu.VMEM((small_rows, width), F32)] + [pltpu.VMEM((length, width), BF)] * 4,
        flops=16 * length * width * width + 3 * attn_flops,
    )

    place = jnp.stack(
        [wide_at % 2, narrow_at % 2, narrow_at // 2, wide_at // 2 % 2, wide_at // 4 % 2]
    ).astype(jnp.int32)
    deeper = [2**i for i in range(3, 20) if 2**i < n_wide]

    def hop(kernel, shapes, *args):
        return call(kernel, [shaped(x) for x in shapes], place, *args, smem=1, stream=False)

    def scatter(keep, send, tail):
        own_a, send_a, own_b, send_b = hop(
            first_kernel,
            [(half // 2 + tail, width)] * 2 + [(half // 2, width)] * 2,
            keep,
            along(send, 1),
        )
        own_a, send_a, own_b, send_b = hop(
            second_kernel,
            [(half // 4 + tail, width)] * 2 + [(half // 4, width)] * 2,
            own_a,
            across(send_a, 1),
            own_b,
            across(send_b, 2),
        )
        rows = half // 8
        own, other = hop(
            join_kernel,
            [(rows + tail // 2, 2 * width)] * 2,
            own_a,
            across(send_a, 2),
            own_b,
            across(send_b, 1),
        )
        own, other = hop(
            functools.partial(columns_kernel, rows),
            [(rows + tail, width)] * 2,
            own,
            along(other, 2),
        )
        return own, along(other, 4)

    def scatter_deep(keep, send):
        own, other = hop(rows_kernel, [(half // 2, 2 * width)] * 2, keep, along(send, 1))
        own_a, send_a, own_b, send_b = hop(
            first_kernel, [(half // 4, width)] * 4, own, along(other, 2)
        )
        own_a, send_a, own_b, send_b = hop(
            second_kernel,
            [(half // 8, width)] * 4,
            own_a,
            across(send_a, 1),
            own_b,
            across(send_b, 2),
        )
        own, other = hop(
            pick_kernel,
            [(half // 8, width)] * 2,
            own_a,
            across(send_a, 2),
            own_b,
            across(send_b, 1),
        )
        return own, along(other, 4)

    def last_sum(own, got):
        rows = half // 8
        x = (own[:rows].astype(F32) + got[:rows].astype(F32)).astype(BF)
        for k in deeper:
            bit, size = wide_at // k % 2, x.shape[0] // 2
            other = lax.dynamic_slice_in_dim(x, (1 - bit) * size, size, 0)
            mine = lax.dynamic_slice_in_dim(x, bit * size, size, 0)
            x = (mine.astype(F32) + along(other, k).astype(F32)).astype(BF)
        return x

    def spread_out(x, parts):
        step = functools.partial
        for k in reversed(deeper):
            bit, far = wide_at // k % 2, along(x, k)
            x = jnp.concatenate([jnp.where(bit == 0, x, far), jnp.where(bit == 0, far, x)], axis=0)
        (x,) = hop(step(beside_kernel, 4), [(half // 8, 2 * width)], x, along(x, 4))
        a, b = hop(step(stack_kernel, 3), [(half // 4, width)] * 2, x, along(x, 2))
        a, b = call(
            double_kernel,
            [shaped((half // 2, width))] * 2,
            a,
            across(a, 2),
            b,
            across(b, 1),
            stream=False,
        )
        kernel = step(half_kernel, parts)
        (x,) = hop(kernel, [(half, 2 * width)], a, across(a, 1), b, across(b, 2))
        return x

    def finish(sources, outs=()):
        count = 2 * len(sources)
        return pl.pallas_call(
            functools.partial(finish_kernel, bool(outs), len(sources)),
            out_shape=(shaped((width, width), F32),) * count,
            in_specs=[pl.BlockSpec(memory_space=pltpu.SMEM)]
            + [pl.BlockSpec(memory_space=pltpu.VMEM)] * len(sources)
            + [pl.BlockSpec(memory_space=pl.ANY)] * len(outs),
            out_specs=(pl.BlockSpec(memory_space=pl.ANY),) * count,
            scratch_shapes=[
                pltpu.VMEM((count, half, width), F32),
                pltpu.SemaphoreType.DMA((count,)),
            ],
            input_output_aliases={1 + len(sources) + i: i for i in range(len(outs))},
            compiler_params=pltpu.CompilerParams(vmem_limit_bytes=LOW),
        )(place, *sources, *outs)

    own, got = scatter(keep_1, send_1, ride)
    part_1, part_2 = last_sum(own, got), last_sum(*scatter_deep(keep_2, send_2))
    if not direct:
        own = lax.psum(small, ("narrow", "wide"))
        got = jnp.zeros_like(own)
    small = call(
        functools.partial(small_kernel, half // 8 if direct else 0),
        [
            shaped((width,), F32),
            shaped((width,), F32),
            shaped((experts, width), F32),
            shaped((heads, buckets_n), F32),
        ],
        own,
        got,
        scratch=[pltpu.VMEM((small_rows, width), F32)],
        stream=False,
    )
    part_1, part_2 = spread_out(part_1, 1), spread_out(part_2, 2)
    far_1, far_2 = along(part_1, 1), along(part_2, 1)
    near = finish((part_1, part_2))
    far_1, far_2, near, small = lax.optimization_barrier((far_1, far_2, near, small))
    grad_w_output, grad_w_value, grad_w_query, grad_w_key = finish((far_1, far_2), near)
    return (
        layer_output,
        input_grad,
        grad_w_query,
        grad_w_key,
        grad_w_value,
        grad_w_output,
        small[0],
        small[1],
        small[2].T,
        small[3].T,
        grad_expert_in,
        grad_expert_out,
    )


def solution(mesh):
    tokens_spec = P(("narrow", "wide"), None)
    experts_in_spec = P("wide", None, "narrow")
    experts_out_spec = P("wide", "narrow", None)
    in_specs = (
        (tokens_spec, tokens_spec)
        + (P(),) * 8
        + (experts_in_spec, experts_out_spec, tokens_spec, P(), P())
    )
    out_specs = (tokens_spec, tokens_spec) + (P(),) * 8 + (experts_in_spec, experts_out_spec)
    body = functools.partial(local, mesh.shape["narrow"], mesh.shape["wide"])
    return jax.shard_map(body, mesh=mesh, in_specs=in_specs, out_specs=out_specs, check_vma=False)
```

```python
import functools

import jax
import jax.numpy as jnp
from jax import lax
from jax.experimental import pallas as pl
from jax.experimental.pallas import tpu as pltpu
from jax.sharding import PartitionSpec as P

epsilon = 1e-06
BF = jnp.bfloat16
F32 = jnp.float32
HIGH = 60 * 2**20
LOW = 12 * 2**20


def mm(a, b):
    return lax.dot_general(a, b, (((1,), (0,)), ((), ())), preferred_element_type=F32)


def mm_nt(a, b):
    return lax.dot_general(a, b, (((1,), (1,)), ((), ())), preferred_element_type=F32)


def mm_tn(a, b):
    return lax.dot_general(a, b, (((0,), (0,)), ((), ())), preferred_element_type=F32)


def rms_scale(rows):
    return lax.rsqrt(jnp.mean(rows * rows, axis=-1, keepdims=True) + epsilon)


def half_masks(rows, width):
    lane = lax.broadcasted_iota(jnp.int32, (rows, width), 1)
    low = (lane < width // 2).astype(F32)
    return low.astype(BF), (1.0 - low).astype(BF)


def as_row(ref):
    return ref[...].reshape(1, -1)


def as_column(ref):
    return ref[...].reshape(-1, 1)


def bucket_mask(count, buckets):
    span = buckets.shape[0] + 1
    row = jnp.concatenate([buckets[...].reshape(1, -1), jnp.zeros((1, 1), jnp.int32)], axis=1)
    rows = pltpu.roll(jnp.broadcast_to(row, (8, span)), span // 2 + 1, 1)
    index = lax.broadcasted_iota(jnp.int32, (count, span), 0)
    return (index == rows[:1]).astype(F32)


class Fetched:
    def __init__(self, source, buffer, semaphore, later):
        self.buffer, self.copy = buffer, pltpu.make_async_copy(source, buffer, semaphore)
        self.later, self.waiting = later, True

    @property
    def shape(self):
        return self.buffer.shape

    def wait(self):
        if self.waiting:
            self.copy.wait()
            self.waiting = False
            while self.later:
                self.later.pop(0).copy.start()

    def __getitem__(self, index):
        self.wait()
        return self.buffer[index]


class Stored:
    def __init__(self, target, buffer, semaphores):
        self.target, self.buffer, self.semaphores = target, buffer, semaphores
        self.copies, self.sent, self.dtype = [], 0, buffer.dtype

    @property
    def shape(self):
        return self.buffer.shape

    def __getitem__(self, index):
        return self.buffer[index]

    def __setitem__(self, index, value):
        self.buffer[index] = value

    def send(self, end=None):
        end = self.shape[0] if end is None else end
        if end > self.sent:
            rows = pl.ds(self.sent, end - self.sent)
            copy = pltpu.make_async_copy(
                self.buffer.at[rows], self.target.at[rows], self.semaphores.at[len(self.copies)]
            )
            copy.start()
            self.copies.append(copy)
            self.sent = end


def large(x):
    return (
        len(x.shape) >= 2
        and x.shape[-2] % 16 == 0
        and x.shape[-1] % 128 == 0
        and x.size * x.dtype.itemsize >= 2**16
    )


def call(kernel, outs, *args, flops=0, transcendentals=0, scratch=(), smem=0, stream=True, early=99):
    out_bytes = sum(o.size * o.dtype.itemsize for o in outs)
    in_bytes = sum(a.size * a.dtype.itemsize for a in args)
    large_in = [stream and i >= smem and large(x) for i, x in enumerate(args)]
    large_out = [stream and large(x) for x in outs]
    moved = [x for x, flag in zip(args + tuple(outs), large_in + large_out) if flag]

    def body(*refs):
        operands, results = refs[: len(args)], refs[len(args) : len(args) + len(outs)]
        rest = refs[len(args) + len(outs) :]
        buffers = iter(rest[: len(moved)])
        semaphores = rest[len(moved)] if moved else None
        count = iter(range(len(moved)))
        later = []
        operands = [
            Fetched(ref, next(buffers), semaphores.at[next(count), 0], later) if flag else ref
            for ref, flag in zip(operands, large_in)
        ]
        fetched = [x for x in operands if isinstance(x, Fetched)]
        later += fetched[early:]
        for x in fetched[:early]:
            x.copy.start()
        results = [
            Stored(ref, next(buffers), semaphores.at[next(count)]) if flag else ref
            for ref, flag in zip(results, large_out)
        ]
        kernel(*operands, *results, *rest[len(moved) + bool(moved) :])
        for x in operands:
            if isinstance(x, Fetched):
                x.wait()
        for x in results:
            if isinstance(x, Stored):
                x.send()
        for x in results:
            if isinstance(x, Stored):
                for copy in x.copies:
                    copy.wait()

    def spec(flag):
        return pl.BlockSpec(memory_space=pl.ANY if flag else pltpu.VMEM)

    scratches = [pltpu.VMEM(x.shape, x.dtype) for x in moved]
    if moved:
        scratches.append(pltpu.SemaphoreType.DMA((len(moved), 2)))
    return pl.pallas_call(
        body,
        out_shape=tuple(outs),
        in_specs=[
            pl.BlockSpec(memory_space=pltpu.SMEM) if i < smem else spec(flag)
            for i, flag in enumerate(large_in)
        ],
        out_specs=tuple(spec(flag) for flag in large_out),
        scratch_shapes=scratches + list(scratch),
        compiler_params=pltpu.CompilerParams(vmem_limit_bytes=HIGH if stream else LOW),
        cost_estimate=pl.CostEstimate(
            flops=flops, transcendentals=transcendentals, bytes_accessed=in_bytes + out_bytes
        ),
    )(*args)


def shaped(shape, dtype=BF):
    return jax.ShapeDtypeStruct(shape, dtype)


def spread_diagonals(rows, length):
    while rows.shape[0] < length // 2:
        rows = jnp.concatenate([rows, pltpu.roll(rows, rows.shape[0], 1)], axis=0)
    half = length // 2
    high = jnp.concatenate([rows[:, 3 * half :], rows[:, :half]], axis=1)
    return jnp.concatenate([rows[:, :length], high], axis=0)


def front_kernel(
    heads,
    cap,
    shift_ref,
    tokens,
    w_query,
    w_key,
    w_value,
    w_output,
    cotangent,
    gain_attn,
    gain_ffn,
    w_router,
    table,
    buckets,
    choices,
    levels,
    normed_one_out,
    query_out,
    key_out,
    value_out,
    probs_out,
    mixed_out,
    residual_out,
    normed_two_out,
    packed_out,
    *slots_out,
):
    length, width = tokens.shape
    scale = (width // heads) ** (-0.5)
    experts = w_router.shape[0]
    flat_slots = sum(out.shape[0] for out in slots_out)
    inputs = tokens[...].astype(F32)
    normed = (inputs * rms_scale(inputs) * as_row(gain_attn)).astype(BF)
    normed_one_out[...] = normed
    normed_one_out.send()
    query_out[...] = mm(normed, w_query[...]).astype(BF)
    key_out[...] = mm(normed, w_key[...]).astype(BF)
    value_out[...] = mm(normed, w_value[...]).astype(BF)
    for out in (query_out, key_out, value_out):
        out.send()
    by_offset = lax.dot_general(
        table[...],
        bucket_mask(table.shape[1], buckets),
        (((1,), (0,)), ((), ())),
        precision=lax.Precision.HIGHEST,
        preferred_element_type=F32,
    )
    rolled = jnp.broadcast_to(by_offset[:, None, :], (heads, 8, 2 * length))
    rolled = rolled.reshape(8 * heads, 2 * length)
    row = lax.broadcasted_iota(jnp.int32, rolled.shape, 0) % 8
    for bit in (1, 2, 4):
        rolled = jnp.where((row & bit) != 0, pltpu.roll(rolled, bit, 1), rolled)
    pair = 2 * width // heads
    masks = half_masks(length, pair)
    for p in range(heads // 2):
        at = slice(p * pair, (p + 1) * pair)
        q2, k2, v2 = query_out[:, at], key_out[:, at], value_out[:, at]
        probs = []
        for half in (0, 1):
            h = 2 * p + half
            bias = spread_diagonals(rolled[8 * h : 8 * h + 8], length)
            scores = mm_nt(q2, k2 * masks[half]) * scale + bias
            e = jnp.exp(scores - jnp.max(scores, axis=-1, keepdims=True))
            e = (e * (1.0 / jnp.sum(e, axis=-1, keepdims=True))).astype(BF)
            probs_out[h] = e
            probs.append(e)
        mixed_out[:, at] = mm(
            jnp.concatenate(probs, axis=1),
            jnp.concatenate([v2 * masks[0], v2 * masks[1]], axis=0),
        ).astype(BF)
    probs_out.send()
    mixed_out.send()
    residual = inputs + mm(mixed_out[...], w_output[...])
    residual_out[...] = residual
    residual_out.send()
    normed_two = (residual * rms_scale(residual) * as_row(gain_ffn)).astype(BF)
    normed_two_out[...] = normed_two
    normed_two_out.send()
    logits = mm_nt(w_router[...], normed_two) + 0.25 * as_column(levels).astype(F32)
    logit_exp = jnp.exp(logits - jnp.max(logits, axis=0, keepdims=True))
    router = logit_exp / jnp.sum(logit_exp, axis=0, keepdims=True)
    chosen = choices[...]
    mask = (chosen == lax.broadcasted_iota(jnp.int32, (experts, length), 0)).astype(F32)
    earlier = (
        lax.broadcasted_iota(jnp.int32, (length, length), 0)
        < lax.broadcasted_iota(jnp.int32, (length, length), 1)
    ).astype(F32)
    counts = mm(mask.astype(BF), earlier.astype(BF))
    position = jnp.sum(mask * counts, axis=0, keepdims=True).astype(jnp.int32)
    slot = chosen ^ shift_ref[0]
    if len(slots_out) > 1:
        slot = (slot & 1) * (experts // 2) + (slot >> 1)
    target = jnp.where(position < cap, slot * cap + position, -1)
    gate = jnp.sum(mask * router, axis=0, keepdims=True)
    row = lax.broadcasted_iota(jnp.int32, (8, length), 0)
    packed = jnp.where(
        row == 0, gate, jnp.where(row == 1, target.astype(F32), chosen.astype(F32))
    )
    packed_out[:8, :] = packed
    packed_out[8:, :] = router
    place = (target == lax.broadcasted_iota(jnp.int32, (flat_slots, length), 0)).astype(F32)
    place = place.astype(BF)
    sent = (packed.T[:, :1] * cotangent[...].astype(F32)).astype(BF)
    normed_slots, grad_slots = mm(place, normed_two), mm(place, sent)
    first = 0
    for out in slots_out:
        rows = slice(first, first + out.shape[0])
        first += out.shape[0]
        out[:, :width] = normed_slots[rows].astype(BF)
        out[:, width:] = grad_slots[rows].astype(BF)


def expert_kernel(*refs):
    w_in, first, w_out, second = refs[0], refs[1:5], refs[5], refs[6:10]
    hidden, grad_pre = refs[10:12], refs[12:14]
    keep_a0, keep_b0, send_a, send_b, keep_b1, keep_a1 = refs[14:]
    rows, double = first[0].shape
    width = double // 2
    c = 0.7978845608028654
    places = (
        ((keep_a0, ()), (keep_b0, ()), (send_a, (0,)), (keep_b1, ())),
        ((keep_a1, ()), (send_b, (0,)), (send_a, (1,)), (send_b, (1,))),
    )
    for i, (pieces, outs) in enumerate(zip((first, second), places)):
        both = jnp.concatenate([p[...] for p in pieces], axis=0)
        pre = mm(both[:, :width], w_in[...])
        square = pre * pre
        t = jnp.tanh(c * pre * (1.0 + 0.044715 * square))
        act = (0.5 * pre * (1.0 + t)).astype(BF)
        slope = 0.5 * (1.0 + t) + 0.5 * c * pre * (1.0 - t * t) * (1.0 + 3 * 0.044715 * square)
        grad = (mm_nt(both[:, width:], w_out[...]) * slope).astype(BF)
        hidden[i][...] = act
        hidden[i].send()
        grad_pre[i][...] = grad
        grad_pre[i].send()
        result = mm(act, w_out[...]).astype(BF)
        back = mm_nt(grad, w_in[...]).astype(BF)
        for j, (out, slot) in enumerate(outs):
            out[(*slot, slice(None), slice(0, width))] = result[j * rows : (j + 1) * rows]
            out[(*slot, slice(None), slice(width, double))] = back[j * rows : (j + 1) * rows]
            if slot != (0,):
                out.send()


def expert_weights_kernel(*refs):
    pieces, units, (grad_in, grad_out) = refs[:16], refs[16:24], refs[24:]
    width = grad_in.shape[1]
    both = jnp.concatenate([p[...] for p in pieces], axis=0)
    act = jnp.concatenate([units[i][...] for i in (0, 1, 4, 5)], axis=0)
    pre = jnp.concatenate([units[i][...] for i in (2, 3, 6, 7)], axis=0)
    step = 256
    for i in range(width // step):
        grad_in[0, i * step : (i + 1) * step, :] = mm_tn(both[:, i * step : (i + 1) * step], pre)
    grad_in.send()
    for i in range(act.shape[1] // step):
        grad_out[0, i * step : (i + 1) * step, :] = mm_tn(
            act[:, i * step : (i + 1) * step], both[:, width:]
        )


def store_halves(core, h, left, right, keep, send):
    columns = left.shape[1]

    rows = slice(0, left.shape[0])

    @pl.when(core == h)
    def _():
        keep[rows, :columns] = left
        keep[rows, columns:] = right

    @pl.when(core != h)
    def _():
        send[rows, :columns] = left
        send[rows, columns:] = right


def diagonal_sums(scores):
    length = scores.shape[0]
    half = length // 2
    low, high = scores[:half], scores[half:]
    total = jnp.concatenate(
        [low[:, :half] + high[:, half:], low[:, half:], jnp.zeros_like(low[:, :half]), high[:, :half]],
        axis=1,
    )
    while total.shape[0] > 8:
        half = total.shape[0] // 2
        total = total[:half] + pltpu.roll(total[half:], 2 * length - half, 1)
    return total


def backward_kernel(
    heads,
    buckets_n,
    core_ref,
    packed_ref,
    gain_ffn,
    w_router,
    buckets,
    cotangent,
    residual_ref,
    w_output,
    value,
    probs_ref,
    normed_two,
    key,
    query,
    mixed,
    normed_one,
    w_value,
    w_query,
    w_key,
    tokens,
    gain_attn,
    *refs,
):
    returned, outs = refs[:-10], refs[-10:]
    layer_output, input_grad, keep_1, send_1, keep_2, send_2, small_out = outs[:7]
    ride = keep_1.shape[0] > keep_2.shape[0]
    small, grad_mixed_out, grad_all = outs[7:]
    core = core_ref[0]
    length, width = residual_ref.shape
    scale = (width // heads) ** (-0.5)
    experts = packed_ref.shape[0] - 8
    slot_rows = returned[0].shape[0]
    packed = packed_ref[...].T
    gate, goal, chosen = packed[:, 0:1], packed[:, 1:2], packed[:, 2:3]
    if len(returned) > 1:
        back = jnp.concatenate([r[...].astype(F32) for r in returned], axis=0).astype(BF)
    else:
        back = returned[0][...]
    place = (
        goal.astype(jnp.int32)
        == lax.broadcasted_iota(jnp.int32, (length, slot_rows * len(returned)), 1)
    ).astype(F32)
    back = mm(place.astype(BF), back)
    picked = back[:, :width]
    kept = (goal >= 0).astype(F32)
    mask = (
        chosen.astype(jnp.int32) == lax.broadcasted_iota(jnp.int32, (length, experts), 1)
    ).astype(F32)
    probs = packed[:, 8:]
    upstream = cotangent[...].astype(F32)
    residual = residual_ref[...]
    grad_gate = jnp.sum(upstream * picked, axis=1, keepdims=True) * kept
    grad_logits = ((grad_gate * gate) * (mask - probs)).astype(BF)
    grad_two = back[:, width:] + mm(grad_logits, w_router[...])
    scale_two = rms_scale(residual)
    weighted = grad_two * as_row(gain_ffn)
    grad_residual = (
        upstream
        + scale_two * weighted
        - residual * (scale_two**3 * jnp.mean(weighted * residual, axis=1, keepdims=True))
    )
    layer_output[...] = (residual + gate * kept * picked).astype(BF)
    layer_output.send()
    small[...] = jnp.zeros_like(small)
    small[1:2, :] = jnp.sum(grad_two * residual * scale_two, axis=0, keepdims=True)
    grad_attn = grad_residual.astype(BF)
    grad_mixed_out[...] = mm_nt(grad_attn, w_output[...]).astype(BF)
    small[2 : 2 + experts, :] = mm_tn(grad_logits, normed_two[...])
    pair = 2 * width // heads
    masks = half_masks(length, pair)
    sums = []
    for p in range(heads // 2):
        at = slice(p * pair, (p + 1) * pair)
        q2, k2, v2, g2 = query[:, at], key[:, at], value[:, at], grad_mixed_out[:, at]
        attn = probs_ref[2 * p], probs_ref[2 * p + 1]
        grads = []
        for half in (0, 1):
            e = attn[half].astype(F32)
            grad_probs = mm_nt(g2, v2 * masks[half])
            gs = e * (grad_probs - jnp.sum(e * grad_probs, axis=-1, keepdims=True))
            sums.append(diagonal_sums(gs))
            grads.append(gs.astype(BF))
        grad_v = mm_tn(
            jnp.concatenate(attn, axis=0),
            jnp.concatenate([g2 * masks[0], g2 * masks[1]], axis=0),
        )
        grad_q = mm(
            jnp.concatenate(grads, axis=1),
            jnp.concatenate([k2 * masks[0], k2 * masks[1]], axis=0),
        )
        grad_k = mm_tn(
            jnp.concatenate(grads, axis=0),
            jnp.concatenate([q2 * masks[0], q2 * masks[1]], axis=0),
        )
        for i, grad in enumerate((grad_v, grad_q * scale, grad_k * scale)):
            grad_all[:, i * width + at.start : i * width + at.stop] = grad.astype(BF)
    half = width // 2
    for h in (0, 1):
        at = slice(h * half, (h + 1) * half)
        left = mm_tn(mixed[:, at], grad_attn).astype(BF)
        right = mm_tn(normed_one[:, at], grad_all[...]).astype(BF)
        store_halves(core, h, left, right[:, :width], keep_1, send_1)
        store_halves(core, h, right[:, width : 2 * width], right[:, 2 * width :], keep_2, send_2)
    for out in (send_1, keep_1, send_2, keep_2):
        out.send(half)
    grad_one = mm_nt(grad_all[:, :width], w_value[...])
    grad_one = grad_one + mm_nt(grad_all[:, width : 2 * width], w_query[...])
    grad_one = grad_one + mm_nt(grad_all[:, 2 * width :], w_key[...])
    inputs = tokens[...].astype(F32)
    scale_one = rms_scale(inputs)
    small[0:1, :] = jnp.sum(grad_one * inputs * scale_one, axis=0, keepdims=True)
    weighted = grad_one * as_row(gain_attn)
    input_grad[...] = (
        grad_residual
        + scale_one * weighted
        - inputs * (scale_one**3 * jnp.mean(weighted * inputs, axis=1, keepdims=True))
    ).astype(BF)
    input_grad.send()
    total = jnp.concatenate(sums, axis=0)
    row = lax.broadcasted_iota(jnp.int32, total.shape, 0) % 8
    for bit in (1, 2, 4):
        total = jnp.where((row & bit) != 0, pltpu.roll(total, 2 * length - bit, 1), total)
    by_offset = jnp.sum(total.reshape(heads, 8, 2 * length), axis=1)
    small[2 + experts : 2 + experts + heads, :buckets_n] = lax.dot_general(
        by_offset,
        bucket_mask(buckets_n, buckets),
        (((1,), (1,)), ((), ())),
        precision=lax.Precision.HIGHEST,
        preferred_element_type=F32,
    )
    if ride:
        top, count = keep_2.shape[0], small.shape[0] // 2
        for out in (keep_1, send_1):
            out[top:, :width] = small[:count].astype(BF)
            out[top:, width:] = small[count:].astype(BF)
    else:
        small_out[...] = small[...]


def both(left, right, rows, columns):
    return left[rows, columns].astype(F32) + right[rows, columns].astype(F32)


def small_kernel(rows, own, got, gain_attn, gain_ffn, router, table, small):
    small[...] = both(own, got, slice(rows, None), slice(None))
    experts = router.shape[0]
    heads, buckets_n = table.shape
    gain_attn[...] = small[0:1, :].reshape(gain_attn.shape)
    gain_ffn[...] = small[1:2, :].reshape(gain_ffn.shape)
    router[...] = small[2 : 2 + experts, :]
    table[...] = small[2 + experts : 2 + experts + heads, :buckets_n]


def side_by_side(rows):
    half = rows.shape[0] // 2
    return jnp.concatenate([rows[:half], rows[half:]], axis=1)


def one_over_other(rows):
    half = rows.shape[1] // 2
    return jnp.concatenate([rows[:, :half], rows[:, half:]], axis=0)


def first_kernel(place_ref, own, got, keep_a, send_a, keep_b, send_b):
    half, columns = keep_b.shape
    for i, (bit, keep, send) in enumerate(((1, keep_a, send_a), (2, keep_b, send_b))):
        at = slice(i * columns, (i + 1) * columns)
        for out, side in ((keep, place_ref[bit]), (send, 1 - place_ref[bit])):
            rows = pl.ds(pl.multiple_of(side * half, half), half)
            out[:half, :] = both(own, got, rows, at).astype(BF)
    if own.shape[0] > 2 * half:
        tail = both(own, got, slice(2 * half, None), slice(None))
        for out in (keep_a, send_a):
            out[half:, :] = one_over_other(tail).astype(BF)


def second_kernel(place_ref, own_a, got_a, own_b, got_b, keep_a, send_a, keep_b, send_b):
    half = keep_b.shape[0]
    for bit, own, got, keep, send in (
        (2, own_a, got_a, keep_a, send_a),
        (1, own_b, got_b, keep_b, send_b),
    ):
        for out, side in ((keep, place_ref[bit]), (send, 1 - place_ref[bit])):
            rows = pl.ds(pl.multiple_of(side * half, half), half)
            out[:half, :] = both(own, got, rows, slice(None)).astype(BF)
    if own_a.shape[0] > 2 * half:
        tail = both(own_a, got_a, slice(2 * half, None), slice(None))
        for out in (keep_a, send_a):
            out[half:, :] = tail.astype(BF)


def rows_kernel(place_ref, own, got, keep, send):
    half = keep.shape[0]
    for out, side in ((keep, place_ref[3]), (send, 1 - place_ref[3])):
        rows = pl.ds(pl.multiple_of(side * half, half), half)
        out[...] = both(own, got, rows, slice(None)).astype(BF)


def pick_kernel(place_ref, own_a, got_a, own_b, got_b, keep, send):
    left = both(own_a, got_a, slice(None), slice(None)).astype(BF)
    right = both(own_b, got_b, slice(None), slice(None)).astype(BF)

    @pl.when(place_ref[4] == 0)
    def _():
        keep[...] = left
        send[...] = right

    @pl.when(place_ref[4] != 0)
    def _():
        keep[...] = right
        send[...] = left


def join_kernel(place_ref, own_a, got_a, own_b, got_b, keep, send):
    rows, columns = own_b.shape
    half = rows // 2
    for out, side in ((keep, place_ref[3]), (send, 1 - place_ref[3])):
        at = pl.ds(pl.multiple_of(side * half, half), half)
        out[:half, :columns] = both(own_a, got_a, at, slice(None)).astype(BF)
        out[:half, columns:] = both(own_b, got_b, at, slice(None)).astype(BF)
    if own_a.shape[0] > rows:
        tail = both(own_a, got_a, slice(rows, None), slice(None))
        for out in (keep, send):
            out[half:, :] = side_by_side(tail).astype(BF)


def columns_kernel(rows, place_ref, own, got, keep, send):
    columns = keep.shape[1]
    for out, side in ((keep, place_ref[4]), (send, 1 - place_ref[4])):
        at = pl.ds(pl.multiple_of(side * columns, columns), columns)
        out[:rows, :] = both(own, got, slice(0, rows), at).astype(BF)
    if own.shape[0] > rows:
        tail = both(own, got, slice(rows, None), slice(None))
        for out in (keep, send):
            out[rows:, :] = one_over_other(tail).astype(BF)


def beside_kernel(bit, place_ref, own, far, out):
    columns = own.shape[1]
    for source, side in ((own, place_ref[bit]), (far, 1 - place_ref[bit])):
        out[:, pl.ds(pl.multiple_of(side * columns, columns), columns)] = source[...]


def stack_kernel(bit, place_ref, own, far, out_a, out_b):
    rows, columns = own.shape[0], out_a.shape[1]
    for source, side in ((own, place_ref[bit]), (far, 1 - place_ref[bit])):
        at = pl.ds(pl.multiple_of(side * rows, rows), rows)
        out_a[at, :] = source[:, :columns]
        out_b[at, :] = source[:, columns:]


def double_kernel(own_a, far_a, own_b, far_b, out_a, out_b):
    rows = own_a.shape[0]
    for source, at, out in ((own_a, 0, out_a), (far_a, 1, out_a), (own_b, 0, out_b), (far_b, 1, out_b)):
        out[at * rows : (at + 1) * rows, :] = source[...]


def half_kernel(parts, place_ref, own_a, far_a, own_b, far_b, out):
    block, columns = own_a.shape[0] // 2, own_a.shape[1]
    rows = block // parts
    sources = ((own_a, 0, 0, 1, 2), (far_a, 0, 1, 1, 2), (own_b, 1, 0, 2, 1), (far_b, 1, 1, 2, 1))
    for source, side, far, bit_1, bit_2 in sources:
        for i in (0, 1):
            at = ((place_ref[bit_1] ^ far) * 2 + (place_ref[bit_2] ^ i)) * rows
            for part in range(parts):
                out[
                    pl.ds(pl.multiple_of(at + part * 4 * rows, rows), rows),
                    side * columns : (side + 1) * columns,
                ] = source[i * block + part * rows : i * block + (part + 1) * rows, :]


def finish_kernel(other, count, place_ref, *refs):
    sources, outs, (buffer, semaphores) = refs[:count], refs[-2 - 2 * count : -2], refs[-2:]
    rows, width = sources[0].shape[0], outs[0].shape[1]
    side = (1 - place_ref[0]) if other else place_ref[0]
    at = pl.ds(pl.multiple_of(side * rows, rows), rows)
    copies = []
    for m, out in enumerate(outs):
        left = m % 2 * width
        buffer[m] = sources[m // 2][:, left : left + width].astype(F32)
        copies.append(pltpu.make_async_copy(buffer.at[m], out.at[at, :], semaphores.at[m]))
        copies[-1].start()
    for copy in copies:
        copy.wait()


def pairs(size, k):
    return [(i, i ^ k) for i in range(size)]


def local(
    n_narrow,
    n_wide,
    tokens,
    cotangent,
    w_query,
    w_key,
    w_value,
    w_output,
    gain_attn,
    gain_ffn,
    w_router,
    bias_table,
    expert_in,
    expert_out,
    choices,
    router_levels,
    buckets,
):
    length, width = tokens.shape
    buckets_n, heads = bias_table.shape
    experts = w_router.shape[1]
    cap = (5 * length + 4 * experts - 1) // (4 * experts)
    flat_slots = experts * cap
    direct = n_wide <= 8
    slot_counts = [cap] * (n_wide // 2) + [flat_slots // 2] if direct else [flat_slots]
    narrow_at, wide_at = lax.axis_index("narrow"), lax.axis_index("wide")
    core_ref = (wide_at % 2).reshape(1)
    shift_ref = (wide_at if direct else jnp.zeros((), jnp.int32)).reshape(1)
    w_router = w_router.T
    rows_bf = shaped((length, width))
    attn_flops = 4 * length * length * width

    def across(x, k):
        return lax.ppermute(x, "narrow", pairs(n_narrow, k))

    def along(x, k):
        return lax.ppermute(x, "wide", pairs(n_wide, k))

    (
        normed_one,
        query,
        key,
        value,
        probs,
        mixed,
        residual,
        normed_two,
        packed,
        *slots,
    ) = call(
        functools.partial(front_kernel, heads, cap),
        [
            rows_bf,
            rows_bf,
            rows_bf,
            rows_bf,
            shaped((heads, length, length)),
            rows_bf,
            shaped((length, width), F32),
            rows_bf,
            shaped((8 + experts, length), F32),
        ]
        + [shaped((n, 2 * width)) for n in slot_counts],
        shift_ref,
        tokens,
        w_query,
        w_key,
        w_value,
        w_output,
        cotangent,
        gain_attn,
        gain_ffn,
        w_router,
        bias_table.T,
        buckets,
        choices.reshape(1, length),
        router_levels,
        smem=1,
        early=2,
        flops=8 * length * width * width + attn_flops,
        transcendentals=heads * length * length,
    )

    quarter = flat_slots // 4
    order = (0, 2, 1, 3)
    if direct:
        per = n_wide // 4
        near = jnp.split(along(slots[-1], 1), n_wide // 2)
        parts = [jnp.concatenate([slots[i], near[i]], axis=0) for i in order]
        parts = [[along(p, 2 * i) if i else p] for i, p in zip(order, parts)]
    else:
        moved = lax.all_to_all(slots[0], "wide", split_axis=0, concat_axis=0, tiled=True)
        parts = [[moved[i * quarter : (i + 1) * quarter]] for i in range(4)]

    def gather(a, b):
        a1, b2 = across(a, 1), across(b, 2)
        a2, b1 = across(a, 2), across(b, 1)
        a3, b3 = across(a1, 2), across(b2, 1)
        return [a, b, a1, b1, a2, b2, a3, b3]

    quarters = [jnp.concatenate(part, axis=0) for part in parts]

    def hop_one(keep_a0, keep_b0, send_a, send_b, keep_b1, keep_a1):
        got_a, got_b = across(send_a, 1), across(send_b, 2)
        next_a = (keep_a1.astype(F32) + got_a[1].astype(F32)).astype(BF)
        next_b = (keep_b1.astype(F32) + got_b[1].astype(F32)).astype(BF)
        return [keep_a0, keep_b0, got_a, got_b, next_a, next_b]

    def hop_two(keep_a0, keep_b0, got_a, got_b, next_a, next_b):
        last_a, last_b = across(next_a, 2), across(next_b, 1)
        sum_a = keep_a0.astype(F32) + got_a[0].astype(F32) + last_a.astype(F32)
        sum_b = keep_b0.astype(F32) + got_b[0].astype(F32) + last_b.astype(F32)
        return [sum_a.astype(BF), sum_b.astype(BF)]

    def reduce(keep_a, send_a, keep_b, send_b):
        got_a, got_b = across(send_a, 1), across(send_b, 2)
        next_a = (keep_a[1].astype(F32) + got_a[1].astype(F32)).astype(BF)
        next_b = (keep_b[1].astype(F32) + got_b[1].astype(F32)).astype(BF)
        last_a, last_b = across(next_a, 2), across(next_b, 1)
        sum_a = keep_a[0].astype(F32) + got_a[0].astype(F32) + last_a.astype(F32)
        sum_b = keep_b[0].astype(F32) + got_b[0].astype(F32) + last_b.astype(F32)
        return sum_a.astype(BF), sum_b.astype(BF)

    w_in = expert_in.reshape(width, -1)
    w_out = expert_out.reshape(-1, width)
    units = w_in.shape[1]
    piece = shaped((2, quarter, 2 * width))
    unit_rows = shaped((4 * quarter, units))
    slot_piece = shaped((quarter, 2 * width))
    expert_flops = 2 * 8 * quarter * width * units
    def experts_of(rows):
        return call(
            expert_kernel,
            [unit_rows] * 4 + [slot_piece, slot_piece, piece, piece, slot_piece, slot_piece],
            w_in,
            *rows[:4],
            w_out,
            *rows[4:],
            early=5,
            flops=4 * expert_flops,
            transcendentals=8 * quarter * units,
        )

    def reduced(keep_a0, keep_b0, send_a, send_b, keep_b1, keep_a1):
        return reduce((keep_a0, keep_a1), send_a, (keep_b0, keep_b1), send_b)

    first = gather(*quarters[:2])
    quarters[2], quarters[3], first[3], first[4] = lax.optimization_barrier(
        (quarters[2], quarters[3], first[3], first[4])
    )
    second = gather(*quarters[2:])
    done_1, done_2 = experts_of(first), experts_of(second)
    groups = [first, second]
    kept = done_1[:4] + done_2[:4]
    h1 = hop_one(*done_1[4:])
    done_2, h1 = lax.optimization_barrier((done_2, h1))
    h2 = hop_one(*done_2[4:])
    sums = hop_two(*h1) + hop_two(*h2)
    if direct:
        sums = [sums[order.index(i)] for i in range(4)]
        returned = [sums[k // per][k % per * cap : (k % per + 1) * cap] for k in range(n_wide)]
        returned = [returned[0]] + [along(returned[k], k) for k in range(1, n_wide)]
        returned = returned[::2] + returned[1::2]
    else:
        returned = jnp.concatenate(sums, axis=0)
        returned = [lax.all_to_all(returned, "wide", split_axis=0, concat_axis=0, tiled=True)]
    grad_expert_in, grad_expert_out = call(
        expert_weights_kernel,
        [shaped(expert_in.shape, F32), shaped(expert_out.shape, F32)],
        *groups[0],
        *groups[1],
        *kept,
        flops=4 * expert_flops,
    )
    returned, grad_expert_in, grad_expert_out = lax.optimization_barrier(
        (returned, grad_expert_in, grad_expert_out)
    )

    half = width // 2
    small_rows = -(-(2 + experts + heads) // 32) * 32
    ride = small_rows if direct else 0
    layer_output, input_grad, keep_1, send_1, keep_2, send_2, small = call(
        functools.partial(backward_kernel, heads, buckets_n),
        [rows_bf, rows_bf]
        + [shaped((half + ride // 2, 2 * width))] * 2
        + [shaped((half, 2 * width))] * 2
        + [shaped((8, 128) if direct else (small_rows, width), F32)],
        core_ref,
        packed,
        gain_ffn,
        w_router,
        buckets,
        cotangent,
        residual,
        w_output,
        value,
        probs,
        normed_two,
        key,
        query,
        mixed,
        normed_one,
        w_value,
        w_query,
        w_key,
        tokens,
        gain_attn,
        *returned,
        smem=1,
        early=4,
        scratch=[pltpu.VMEM((small_rows, width), F32)] + [pltpu.VMEM((length, width), BF), pltpu.VMEM((length, 3 * width), BF)],
        flops=16 * length * width * width + 3 * attn_flops,
    )

    place = jnp.stack(
        [wide_at % 2, narrow_at % 2, narrow_at // 2, wide_at // 2 % 2, wide_at // 4 % 2]
    ).astype(jnp.int32)
    deeper = [2**i for i in range(3, 20) if 2**i < n_wide]

    def hop(kernel, shapes, *args):
        return call(kernel, [shaped(x) for x in shapes], place, *args, smem=1, stream=False)

    def scatter(keep, send, tail):
        own_a, send_a, own_b, send_b = hop(
            first_kernel,
            [(half // 2 + tail, width)] * 2 + [(half // 2, width)] * 2,
            keep,
            along(send, 1),
        )
        own_a, send_a, own_b, send_b = hop(
            second_kernel,
            [(half // 4 + tail, width)] * 2 + [(half // 4, width)] * 2,
            own_a,
            across(send_a, 1),
            own_b,
            across(send_b, 2),
        )
        rows = half // 8
        own, other = hop(
            join_kernel,
            [(rows + tail // 2, 2 * width)] * 2,
            own_a,
            across(send_a, 2),
            own_b,
            across(send_b, 1),
        )
        own, other = hop(
            functools.partial(columns_kernel, rows),
            [(rows + tail, width)] * 2,
            own,
            along(other, 2),
        )
        return own, along(other, 4)

    def scatter_deep(keep, send):
        own, other = hop(rows_kernel, [(half // 2, 2 * width)] * 2, keep, along(send, 1))
        own_a, send_a, own_b, send_b = hop(
            first_kernel, [(half // 4, width)] * 4, own, along(other, 2)
        )
        own_a, send_a, own_b, send_b = hop(
            second_kernel,
            [(half // 8, width)] * 4,
            own_a,
            across(send_a, 1),
            own_b,
            across(send_b, 2),
        )
        own, other = hop(
            pick_kernel,
            [(half // 8, width)] * 2,
            own_a,
            across(send_a, 2),
            own_b,
            across(send_b, 1),
        )
        return own, along(other, 4)

    def last_sum(own, got):
        rows = half // 8
        x = (own[:rows].astype(F32) + got[:rows].astype(F32)).astype(BF)
        for k in deeper:
            bit, size = wide_at // k % 2, x.shape[0] // 2
            other = lax.dynamic_slice_in_dim(x, (1 - bit) * size, size, 0)
            mine = lax.dynamic_slice_in_dim(x, bit * size, size, 0)
            x = (mine.astype(F32) + along(other, k).astype(F32)).astype(BF)
        return x

    def spread_out(x, parts):
        step = functools.partial
        for k in reversed(deeper):
            bit, far = wide_at // k % 2, along(x, k)
            x = jnp.concatenate([jnp.where(bit == 0, x, far), jnp.where(bit == 0, far, x)], axis=0)
        (x,) = hop(step(beside_kernel, 4), [(half // 8, 2 * width)], x, along(x, 4))
        a, b = hop(step(stack_kernel, 3), [(half // 4, width)] * 2, x, along(x, 2))
        a, b = call(
            double_kernel,
            [shaped((half // 2, width))] * 2,
            a,
            across(a, 2),
            b,
            across(b, 1),
            stream=False,
        )
        kernel = step(half_kernel, parts)
        (x,) = hop(kernel, [(half, 2 * width)], a, across(a, 1), b, across(b, 2))
        return x

    def finish(sources, outs=()):
        count = 2 * len(sources)
        return pl.pallas_call(
            functools.partial(finish_kernel, bool(outs), len(sources)),
            out_shape=(shaped((width, width), F32),) * count,
            in_specs=[pl.BlockSpec(memory_space=pltpu.SMEM)]
            + [pl.BlockSpec(memory_space=pltpu.VMEM)] * len(sources)
            + [pl.BlockSpec(memory_space=pl.ANY)] * len(outs),
            out_specs=(pl.BlockSpec(memory_space=pl.ANY),) * count,
            scratch_shapes=[
                pltpu.VMEM((count, half, width), F32),
                pltpu.SemaphoreType.DMA((count,)),
            ],
            input_output_aliases={1 + len(sources) + i: i for i in range(len(outs))},
            compiler_params=pltpu.CompilerParams(vmem_limit_bytes=LOW),
        )(place, *sources, *outs)

    own, got = scatter(keep_1, send_1, ride)
    part_1, part_2 = last_sum(own, got), last_sum(*scatter_deep(keep_2, send_2))
    if not direct:
        own = lax.psum(small, ("narrow", "wide"))
        got = jnp.zeros_like(own)
    small = call(
        functools.partial(small_kernel, half // 8 if direct else 0),
        [
            shaped((width,), F32),
            shaped((width,), F32),
            shaped((experts, width), F32),
            shaped((heads, buckets_n), F32),
        ],
        own,
        got,
        scratch=[pltpu.VMEM((small_rows, width), F32)],
        stream=False,
    )
    part_1, part_2 = spread_out(part_1, 1), spread_out(part_2, 2)
    far_1, far_2 = along(part_1, 1), along(part_2, 1)
    near = finish((part_1, part_2))
    far_1, far_2, near, small = lax.optimization_barrier((far_1, far_2, near, small))
    grad_w_output, grad_w_value, grad_w_query, grad_w_key = finish((far_1, far_2), near)
    return (
        layer_output,
        input_grad,
        grad_w_query,
        grad_w_key,
        grad_w_value,
        grad_w_output,
        small[0],
        small[1],
        small[2].T,
        small[3].T,
        grad_expert_in,
        grad_expert_out,
    )


def solution(mesh):
    tokens_spec = P(("narrow", "wide"), None)
    experts_in_spec = P("wide", None, "narrow")
    experts_out_spec = P("wide", "narrow", None)
    in_specs = (
        (tokens_spec, tokens_spec)
        + (P(),) * 8
        + (experts_in_spec, experts_out_spec, tokens_spec, P(), P())
    )
    out_specs = (tokens_spec, tokens_spec) + (P(),) * 8 + (experts_in_spec, experts_out_spec)
    body = functools.partial(local, mesh.shape["narrow"], mesh.shape["wide"])
    return jax.shard_map(body, mesh=mesh, in_specs=in_specs, out_specs=out_specs, check_vma=False)
```

```python
import functools

import jax
import jax.numpy as jnp
from jax import lax
from jax.experimental import pallas as pl
from jax.experimental.pallas import tpu as pltpu
from jax.sharding import PartitionSpec as P

epsilon = 1e-06
BF = jnp.bfloat16
F32 = jnp.float32
HIGH = 60 * 2**20
LOW = 12 * 2**20


def mm(a, b):
    return lax.dot_general(a, b, (((1,), (0,)), ((), ())), preferred_element_type=F32)


def mm_nt(a, b):
    return lax.dot_general(a, b, (((1,), (1,)), ((), ())), preferred_element_type=F32)


def mm_tn(a, b):
    return lax.dot_general(a, b, (((0,), (0,)), ((), ())), preferred_element_type=F32)


def rms_scale(rows):
    return lax.rsqrt(jnp.mean(rows * rows, axis=-1, keepdims=True) + epsilon)


def half_masks(rows, width):
    lane = lax.broadcasted_iota(jnp.int32, (rows, width), 1)
    low = (lane < width // 2).astype(F32)
    return low.astype(BF), (1.0 - low).astype(BF)


def as_row(ref):
    return ref[...].reshape(1, -1)


def as_column(ref):
    return ref[...].reshape(-1, 1)


def bucket_mask(count, buckets):
    span = buckets.shape[0] + 1
    row = jnp.concatenate([buckets[...].reshape(1, -1), jnp.zeros((1, 1), jnp.int32)], axis=1)
    rows = pltpu.roll(jnp.broadcast_to(row, (8, span)), span // 2 + 1, 1)
    index = lax.broadcasted_iota(jnp.int32, (count, span), 0)
    return (index == rows[:1]).astype(F32)


class Fetched:
    def __init__(self, source, buffer, semaphore, later):
        self.buffer, self.copy = buffer, pltpu.make_async_copy(source, buffer, semaphore)
        self.later, self.waiting = later, True

    @property
    def shape(self):
        return self.buffer.shape

    def wait(self):
        if self.waiting:
            self.copy.wait()
            self.waiting = False
            while self.later:
                self.later.pop(0).copy.start()

    def __getitem__(self, index):
        self.wait()
        return self.buffer[index]


class Stored:
    def __init__(self, target, buffer, semaphores):
        self.target, self.buffer, self.semaphores = target, buffer, semaphores
        self.copies, self.sent, self.dtype = [], 0, buffer.dtype

    @property
    def shape(self):
        return self.buffer.shape

    def __getitem__(self, index):
        return self.buffer[index]

    def __setitem__(self, index, value):
        self.buffer[index] = value

    def send(self, end=None):
        end = self.shape[0] if end is None else end
        if end > self.sent:
            rows = pl.ds(self.sent, end - self.sent)
            copy = pltpu.make_async_copy(
                self.buffer.at[rows], self.target.at[rows], self.semaphores.at[len(self.copies)]
            )
            copy.start()
            self.copies.append(copy)
            self.sent = end


def large(x):
    return (
        len(x.shape) >= 2
        and x.shape[-2] % 16 == 0
        and x.shape[-1] % 128 == 0
        and x.size * x.dtype.itemsize >= 2**16
    )


def call(kernel, outs, *args, flops=0, transcendentals=0, scratch=(), smem=0, stream=True, early=99):
    out_bytes = sum(o.size * o.dtype.itemsize for o in outs)
    in_bytes = sum(a.size * a.dtype.itemsize for a in args)
    large_in = [stream and i >= smem and large(x) for i, x in enumerate(args)]
    large_out = [stream and large(x) for x in outs]
    moved = [x for x, flag in zip(args + tuple(outs), large_in + large_out) if flag]

    def body(*refs):
        operands, results = refs[: len(args)], refs[len(args) : len(args) + len(outs)]
        rest = refs[len(args) + len(outs) :]
        buffers = iter(rest[: len(moved)])
        semaphores = rest[len(moved)] if moved else None
        count = iter(range(len(moved)))
        later = []
        operands = [
            Fetched(ref, next(buffers), semaphores.at[next(count), 0], later) if flag else ref
            for ref, flag in zip(operands, large_in)
        ]
        fetched = [x for x in operands if isinstance(x, Fetched)]
        later += fetched[early:]
        for x in fetched[:early]:
            x.copy.start()
        results = [
            Stored(ref, next(buffers), semaphores.at[next(count)]) if flag else ref
            for ref, flag in zip(results, large_out)
        ]
        kernel(*operands, *results, *rest[len(moved) + bool(moved) :])
        for x in operands:
            if isinstance(x, Fetched):
                x.wait()
        for x in results:
            if isinstance(x, Stored):
                x.send()
        for x in results:
            if isinstance(x, Stored):
                for copy in x.copies:
                    copy.wait()

    def spec(flag):
        return pl.BlockSpec(memory_space=pl.ANY if flag else pltpu.VMEM)

    scratches = [pltpu.VMEM(x.shape, x.dtype) for x in moved]
    if moved:
        scratches.append(pltpu.SemaphoreType.DMA((len(moved), 2)))
    return pl.pallas_call(
        body,
        out_shape=tuple(outs),
        in_specs=[
            pl.BlockSpec(memory_space=pltpu.SMEM) if i < smem else spec(flag)
            for i, flag in enumerate(large_in)
        ],
        out_specs=tuple(spec(flag) for flag in large_out),
        scratch_shapes=scratches + list(scratch),
        compiler_params=pltpu.CompilerParams(vmem_limit_bytes=HIGH if stream else LOW),
        cost_estimate=pl.CostEstimate(
            flops=flops, transcendentals=transcendentals, bytes_accessed=in_bytes + out_bytes
        ),
    )(*args)


def shaped(shape, dtype=BF):
    return jax.ShapeDtypeStruct(shape, dtype)


def spread_diagonals(rows, length):
    while rows.shape[0] < length // 2:
        rows = jnp.concatenate([rows, pltpu.roll(rows, rows.shape[0], 1)], axis=0)
    half = length // 2
    high = jnp.concatenate([rows[:, 3 * half :], rows[:, :half]], axis=1)
    return jnp.concatenate([rows[:, :length], high], axis=0)


def front_kernel(
    heads,
    cap,
    shift_ref,
    tokens,
    w_query,
    w_key,
    w_value,
    w_output,
    cotangent,
    gain_attn,
    gain_ffn,
    w_router,
    table,
    buckets,
    choices,
    levels,
    query_out,
    key_out,
    value_out,
    probs_out,
    mixed_out,
    residual_out,
    packed_out,
    *slots_out,
):
    length, width = tokens.shape
    scale = (width // heads) ** (-0.5)
    experts = w_router.shape[0]
    flat_slots = sum(out.shape[0] for out in slots_out)
    inputs = tokens[...].astype(F32)
    normed = (inputs * rms_scale(inputs) * as_row(gain_attn)).astype(BF)
    query_out[...] = mm(normed, w_query[...]).astype(BF)
    key_out[...] = mm(normed, w_key[...]).astype(BF)
    value_out[...] = mm(normed, w_value[...]).astype(BF)
    for out in (query_out, key_out, value_out):
        out.send()
    by_offset = lax.dot_general(
        table[...],
        bucket_mask(table.shape[1], buckets),
        (((1,), (0,)), ((), ())),
        precision=lax.Precision.HIGHEST,
        preferred_element_type=F32,
    )
    rolled = jnp.broadcast_to(by_offset[:, None, :], (heads, 8, 2 * length))
    rolled = rolled.reshape(8 * heads, 2 * length)
    row = lax.broadcasted_iota(jnp.int32, rolled.shape, 0) % 8
    for bit in (1, 2, 4):
        rolled = jnp.where((row & bit) != 0, pltpu.roll(rolled, bit, 1), rolled)
    pair = 2 * width // heads
    masks = half_masks(length, pair)
    for p in range(heads // 2):
        at = slice(p * pair, (p + 1) * pair)
        q2, k2, v2 = query_out[:, at], key_out[:, at], value_out[:, at]
        probs = []
        for half in (0, 1):
            h = 2 * p + half
            bias = spread_diagonals(rolled[8 * h : 8 * h + 8], length)
            scores = mm_nt(q2, k2 * masks[half]) * scale + bias
            e = jnp.exp(scores - jnp.max(scores, axis=-1, keepdims=True))
            e = (e * (1.0 / jnp.sum(e, axis=-1, keepdims=True))).astype(BF)
            probs_out[h] = e
            probs.append(e)
        mixed_out[:, at] = mm(
            jnp.concatenate(probs, axis=1),
            jnp.concatenate([v2 * masks[0], v2 * masks[1]], axis=0),
        ).astype(BF)
    probs_out.send()
    mixed_out.send()
    residual = inputs + mm(mixed_out[...], w_output[...])
    residual_out[...] = residual
    residual_out.send()
    normed_two = (residual * rms_scale(residual) * as_row(gain_ffn)).astype(BF)
    logits = mm_nt(w_router[...], normed_two) + 0.25 * as_column(levels).astype(F32)
    logit_exp = jnp.exp(logits - jnp.max(logits, axis=0, keepdims=True))
    router = logit_exp / jnp.sum(logit_exp, axis=0, keepdims=True)
    chosen = choices[...]
    mask = (chosen == lax.broadcasted_iota(jnp.int32, (experts, length), 0)).astype(F32)
    earlier = (
        lax.broadcasted_iota(jnp.int32, (length, length), 0)
        < lax.broadcasted_iota(jnp.int32, (length, length), 1)
    ).astype(F32)
    counts = mm(mask.astype(BF), earlier.astype(BF))
    position = jnp.sum(mask * counts, axis=0, keepdims=True).astype(jnp.int32)
    slot = chosen ^ shift_ref[0]
    if len(slots_out) > 1:
        slot = (slot & 1) * (experts // 2) + (slot >> 1)
    target = jnp.where(position < cap, slot * cap + position, -1)
    gate = jnp.sum(mask * router, axis=0, keepdims=True)
    row = lax.broadcasted_iota(jnp.int32, (8, length), 0)
    packed = jnp.where(
        row == 0, gate, jnp.where(row == 1, target.astype(F32), chosen.astype(F32))
    )
    packed_out[:8, :] = packed
    packed_out[8:, :] = router
    place = (target == lax.broadcasted_iota(jnp.int32, (flat_slots, length), 0)).astype(F32)
    place = place.astype(BF)
    sent = (packed.T[:, :1] * cotangent[...].astype(F32)).astype(BF)
    normed_slots, grad_slots = mm(place, normed_two), mm(place, sent)
    first = 0
    for out in slots_out:
        rows = slice(first, first + out.shape[0])
        first += out.shape[0]
        out[:, :width] = normed_slots[rows].astype(BF)
        out[:, width:] = grad_slots[rows].astype(BF)


def expert_kernel(*refs):
    w_in, first, w_out, second = refs[0], refs[1:5], refs[5], refs[6:10]
    hidden, grad_pre = refs[10:12], refs[12:14]
    keep_a0, keep_b0, send_a, send_b, keep_b1, keep_a1 = refs[14:]
    rows, double = first[0].shape
    width = double // 2
    c = 0.7978845608028654
    places = (
        ((keep_a0, ()), (keep_b0, ()), (send_a, (0,)), (keep_b1, ())),
        ((keep_a1, ()), (send_b, (0,)), (send_a, (1,)), (send_b, (1,))),
    )
    for i, (pieces, outs) in enumerate(zip((first, second), places)):
        both = jnp.concatenate([p[...] for p in pieces], axis=0)
        pre = mm(both[:, :width], w_in[...])
        square = pre * pre
        t = jnp.tanh(c * pre * (1.0 + 0.044715 * square))
        act = (0.5 * pre * (1.0 + t)).astype(BF)
        slope = 0.5 * (1.0 + t) + 0.5 * c * pre * (1.0 - t * t) * (1.0 + 3 * 0.044715 * square)
        grad = (mm_nt(both[:, width:], w_out[...]) * slope).astype(BF)
        hidden[i][...] = act
        hidden[i].send()
        grad_pre[i][...] = grad
        grad_pre[i].send()
        result = mm(act, w_out[...]).astype(BF)
        back = mm_nt(grad, w_in[...]).astype(BF)
        for j, (out, slot) in enumerate(outs):
            out[(*slot, slice(None), slice(0, width))] = result[j * rows : (j + 1) * rows]
            out[(*slot, slice(None), slice(width, double))] = back[j * rows : (j + 1) * rows]
            if slot != (0,):
                out.send()


def expert_weights_kernel(*refs):
    pieces, units, (grad_in, grad_out) = refs[:16], refs[16:24], refs[24:]
    width = grad_in.shape[1]
    both = jnp.concatenate([p[...] for p in pieces], axis=0)
    act = jnp.concatenate([units[i][...] for i in (0, 1, 4, 5)], axis=0)
    pre = jnp.concatenate([units[i][...] for i in (2, 3, 6, 7)], axis=0)
    step = 256
    for i in range(width // step):
        grad_in[0, i * step : (i + 1) * step, :] = mm_tn(both[:, i * step : (i + 1) * step], pre)
    grad_in.send()
    for i in range(act.shape[1] // step):
        grad_out[0, i * step : (i + 1) * step, :] = mm_tn(
            act[:, i * step : (i + 1) * step], both[:, width:]
        )


def store_halves(core, h, left, right, keep, send):
    columns = left.shape[1]

    rows = slice(0, left.shape[0])

    @pl.when(core == h)
    def _():
        keep[rows, :columns] = left
        keep[rows, columns:] = right

    @pl.when(core != h)
    def _():
        send[rows, :columns] = left
        send[rows, columns:] = right


def diagonal_sums(scores):
    length = scores.shape[0]
    half = length // 2
    low, high = scores[:half], scores[half:]
    total = jnp.concatenate(
        [low[:, :half] + high[:, half:], low[:, half:], jnp.zeros_like(low[:, :half]), high[:, :half]],
        axis=1,
    )
    while total.shape[0] > 8:
        half = total.shape[0] // 2
        total = total[:half] + pltpu.roll(total[half:], 2 * length - half, 1)
    return total


def backward_kernel(
    heads,
    buckets_n,
    core_ref,
    packed_ref,
    gain_ffn,
    w_router,
    buckets,
    cotangent,
    residual_ref,
    w_output,
    value,
    probs_ref,
    key,
    query,
    mixed,
    tokens,
    w_value,
    w_query,
    w_key,
    gain_attn,
    *refs,
):
    returned, outs = refs[:-10], refs[-10:]
    layer_output, input_grad, keep_1, send_1, keep_2, send_2, small_out = outs[:7]
    ride = keep_1.shape[0] > keep_2.shape[0]
    small, grad_mixed_out, grad_all = outs[7:]
    core = core_ref[0]
    length, width = residual_ref.shape
    scale = (width // heads) ** (-0.5)
    experts = packed_ref.shape[0] - 8
    slot_rows = returned[0].shape[0]
    packed = packed_ref[...].T
    gate, goal, chosen = packed[:, 0:1], packed[:, 1:2], packed[:, 2:3]
    if len(returned) > 1:
        back = jnp.concatenate([r[...].astype(F32) for r in returned], axis=0).astype(BF)
    else:
        back = returned[0][...]
    place = (
        goal.astype(jnp.int32)
        == lax.broadcasted_iota(jnp.int32, (length, slot_rows * len(returned)), 1)
    ).astype(F32)
    back = mm(place.astype(BF), back)
    picked = back[:, :width]
    kept = (goal >= 0).astype(F32)
    mask = (
        chosen.astype(jnp.int32) == lax.broadcasted_iota(jnp.int32, (length, experts), 1)
    ).astype(F32)
    probs = packed[:, 8:]
    upstream = cotangent[...].astype(F32)
    residual = residual_ref[...]
    grad_gate = jnp.sum(upstream * picked, axis=1, keepdims=True) * kept
    grad_logits = ((grad_gate * gate) * (mask - probs)).astype(BF)
    grad_two = back[:, width:] + mm(grad_logits, w_router[...])
    scale_two = rms_scale(residual)
    weighted = grad_two * as_row(gain_ffn)
    grad_residual = (
        upstream
        + scale_two * weighted
        - residual * (scale_two**3 * jnp.mean(weighted * residual, axis=1, keepdims=True))
    )
    layer_output[...] = (residual + gate * kept * picked).astype(BF)
    layer_output.send()
    small[...] = jnp.zeros_like(small)
    small[1:2, :] = jnp.sum(grad_two * residual * scale_two, axis=0, keepdims=True)
    grad_attn = grad_residual.astype(BF)
    grad_mixed_out[...] = mm_nt(grad_attn, w_output[...]).astype(BF)
    normed_two = (residual * scale_two * as_row(gain_ffn)).astype(BF)
    small[2 : 2 + experts, :] = mm_tn(grad_logits, normed_two)
    pair = 2 * width // heads
    masks = half_masks(length, pair)
    sums = []
    for p in range(heads // 2):
        at = slice(p * pair, (p + 1) * pair)
        q2, k2, v2, g2 = query[:, at], key[:, at], value[:, at], grad_mixed_out[:, at]
        attn = probs_ref[2 * p], probs_ref[2 * p + 1]
        grads = []
        for half in (0, 1):
            e = attn[half].astype(F32)
            grad_probs = mm_nt(g2, v2 * masks[half])
            gs = e * (grad_probs - jnp.sum(e * grad_probs, axis=-1, keepdims=True))
            sums.append(diagonal_sums(gs))
            grads.append(gs.astype(BF))
        grad_v = mm_tn(
            jnp.concatenate(attn, axis=0),
            jnp.concatenate([g2 * masks[0], g2 * masks[1]], axis=0),
        )
        grad_q = mm(
            jnp.concatenate(grads, axis=1),
            jnp.concatenate([k2 * masks[0], k2 * masks[1]], axis=0),
        )
        grad_k = mm_tn(
            jnp.concatenate(grads, axis=0),
            jnp.concatenate([q2 * masks[0], q2 * masks[1]], axis=0),
        )
        for i, grad in enumerate((grad_v, grad_q * scale, grad_k * scale)):
            grad_all[:, i * width + at.start : i * width + at.stop] = grad.astype(BF)
    inputs = tokens[...].astype(F32)
    scale_one = rms_scale(inputs)
    normed_one = (inputs * scale_one * as_row(gain_attn)).astype(BF)
    half = width // 2
    for h in (0, 1):
        at = slice(h * half, (h + 1) * half)
        left = mm_tn(mixed[:, at], grad_attn).astype(BF)
        right = mm_tn(normed_one[:, at], grad_all[...]).astype(BF)
        store_halves(core, h, left, right[:, :width], keep_1, send_1)
        store_halves(core, h, right[:, width : 2 * width], right[:, 2 * width :], keep_2, send_2)
    for out in (send_1, keep_1, send_2, keep_2):
        out.send(half)
    grad_one = mm_nt(grad_all[:, :width], w_value[...])
    grad_one = grad_one + mm_nt(grad_all[:, width : 2 * width], w_query[...])
    grad_one = grad_one + mm_nt(grad_all[:, 2 * width :], w_key[...])
    small[0:1, :] = jnp.sum(grad_one * inputs * scale_one, axis=0, keepdims=True)
    weighted = grad_one * as_row(gain_attn)
    input_grad[...] = (
        grad_residual
        + scale_one * weighted
        - inputs * (scale_one**3 * jnp.mean(weighted * inputs, axis=1, keepdims=True))
    ).astype(BF)
    input_grad.send()
    total = jnp.concatenate(sums, axis=0)
    row = lax.broadcasted_iota(jnp.int32, total.shape, 0) % 8
    for bit in (1, 2, 4):
        total = jnp.where((row & bit) != 0, pltpu.roll(total, 2 * length - bit, 1), total)
    by_offset = jnp.sum(total.reshape(heads, 8, 2 * length), axis=1)
    small[2 + experts : 2 + experts + heads, :buckets_n] = lax.dot_general(
        by_offset,
        bucket_mask(buckets_n, buckets),
        (((1,), (1,)), ((), ())),
        precision=lax.Precision.HIGHEST,
        preferred_element_type=F32,
    )
    if ride:
        top, count = keep_2.shape[0], small.shape[0] // 2
        for out in (keep_1, send_1):
            out[top:, :width] = small[:count].astype(BF)
            out[top:, width:] = small[count:].astype(BF)
    else:
        small_out[...] = small[...]


def both(left, right, rows, columns):
    return left[rows, columns].astype(F32) + right[rows, columns].astype(F32)


def small_kernel(rows, own, got, gain_attn, gain_ffn, router, table, small):
    small[...] = both(own, got, slice(rows, None), slice(None))
    experts = router.shape[0]
    heads, buckets_n = table.shape
    gain_attn[...] = small[0:1, :].reshape(gain_attn.shape)
    gain_ffn[...] = small[1:2, :].reshape(gain_ffn.shape)
    router[...] = small[2 : 2 + experts, :]
    table[...] = small[2 + experts : 2 + experts + heads, :buckets_n]


def side_by_side(rows):
    half = rows.shape[0] // 2
    return jnp.concatenate([rows[:half], rows[half:]], axis=1)


def one_over_other(rows):
    half = rows.shape[1] // 2
    return jnp.concatenate([rows[:, :half], rows[:, half:]], axis=0)


def first_kernel(place_ref, own, got, keep_a, send_a, keep_b, send_b):
    half, columns = keep_b.shape
    for i, (bit, keep, send) in enumerate(((1, keep_a, send_a), (2, keep_b, send_b))):
        at = slice(i * columns, (i + 1) * columns)
        for out, side in ((keep, place_ref[bit]), (send, 1 - place_ref[bit])):
            rows = pl.ds(pl.multiple_of(side * half, half), half)
            out[:half, :] = both(own, got, rows, at).astype(BF)
    if own.shape[0] > 2 * half:
        tail = both(own, got, slice(2 * half, None), slice(None))
        for out in (keep_a, send_a):
            out[half:, :] = one_over_other(tail).astype(BF)


def second_kernel(place_ref, own_a, got_a, own_b, got_b, keep_a, send_a, keep_b, send_b):
    half = keep_b.shape[0]
    for bit, own, got, keep, send in (
        (2, own_a, got_a, keep_a, send_a),
        (1, own_b, got_b, keep_b, send_b),
    ):
        for out, side in ((keep, place_ref[bit]), (send, 1 - place_ref[bit])):
            rows = pl.ds(pl.multiple_of(side * half, half), half)
            out[:half, :] = both(own, got, rows, slice(None)).astype(BF)
    if own_a.shape[0] > 2 * half:
        tail = both(own_a, got_a, slice(2 * half, None), slice(None))
        for out in (keep_a, send_a):
            out[half:, :] = tail.astype(BF)


def rows_kernel(place_ref, own, got, keep, send):
    half = keep.shape[0]
    for out, side in ((keep, place_ref[3]), (send, 1 - place_ref[3])):
        rows = pl.ds(pl.multiple_of(side * half, half), half)
        out[...] = both(own, got, rows, slice(None)).astype(BF)


def pick_kernel(place_ref, own_a, got_a, own_b, got_b, keep, send):
    left = both(own_a, got_a, slice(None), slice(None)).astype(BF)
    right = both(own_b, got_b, slice(None), slice(None)).astype(BF)

    @pl.when(place_ref[4] == 0)
    def _():
        keep[...] = left
        send[...] = right

    @pl.when(place_ref[4] != 0)
    def _():
        keep[...] = right
        send[...] = left


def join_kernel(place_ref, own_a, got_a, own_b, got_b, keep, send):
    rows, columns = own_b.shape
    half = rows // 2
    for out, side in ((keep, place_ref[3]), (send, 1 - place_ref[3])):
        at = pl.ds(pl.multiple_of(side * half, half), half)
        out[:half, :columns] = both(own_a, got_a, at, slice(None)).astype(BF)
        out[:half, columns:] = both(own_b, got_b, at, slice(None)).astype(BF)
    if own_a.shape[0] > rows:
        tail = both(own_a, got_a, slice(rows, None), slice(None))
        for out in (keep, send):
            out[half:, :] = side_by_side(tail).astype(BF)


def columns_kernel(rows, place_ref, own, got, keep, send):
    columns = keep.shape[1]
    for out, side in ((keep, place_ref[4]), (send, 1 - place_ref[4])):
        at = pl.ds(pl.multiple_of(side * columns, columns), columns)
        out[:rows, :] = both(own, got, slice(0, rows), at).astype(BF)
    if own.shape[0] > rows:
        tail = both(own, got, slice(rows, None), slice(None))
        for out in (keep, send):
            out[rows:, :] = one_over_other(tail).astype(BF)


def beside_kernel(bit, place_ref, own, far, out):
    columns = own.shape[1]
    for source, side in ((own, place_ref[bit]), (far, 1 - place_ref[bit])):
        out[:, pl.ds(pl.multiple_of(side * columns, columns), columns)] = source[...]


def stack_kernel(bit, place_ref, own, far, out_a, out_b):
    rows, columns = own.shape[0], out_a.shape[1]
    for source, side in ((own, place_ref[bit]), (far, 1 - place_ref[bit])):
        at = pl.ds(pl.multiple_of(side * rows, rows), rows)
        out_a[at, :] = source[:, :columns]
        out_b[at, :] = source[:, columns:]


def double_kernel(own_a, far_a, own_b, far_b, out_a, out_b):
    rows = own_a.shape[0]
    for source, at, out in ((own_a, 0, out_a), (far_a, 1, out_a), (own_b, 0, out_b), (far_b, 1, out_b)):
        out[at * rows : (at + 1) * rows, :] = source[...]


def half_kernel(parts, place_ref, own_a, far_a, own_b, far_b, out):
    block, columns = own_a.shape[0] // 2, own_a.shape[1]
    rows = block // parts
    sources = ((own_a, 0, 0, 1, 2), (far_a, 0, 1, 1, 2), (own_b, 1, 0, 2, 1), (far_b, 1, 1, 2, 1))
    for source, side, far, bit_1, bit_2 in sources:
        for i in (0, 1):
            at = ((place_ref[bit_1] ^ far) * 2 + (place_ref[bit_2] ^ i)) * rows
            for part in range(parts):
                out[
                    pl.ds(pl.multiple_of(at + part * 4 * rows, rows), rows),
                    side * columns : (side + 1) * columns,
                ] = source[i * block + part * rows : i * block + (part + 1) * rows, :]


def finish_kernel(other, count, place_ref, *refs):
    sources, outs, (buffer, semaphores) = refs[:count], refs[-2 - 2 * count : -2], refs[-2:]
    rows, width = sources[0].shape[0], outs[0].shape[1]
    side = (1 - place_ref[0]) if other else place_ref[0]
    at = pl.ds(pl.multiple_of(side * rows, rows), rows)
    copies = []
    for m, out in enumerate(outs):
        left = m % 2 * width
        buffer[m] = sources[m // 2][:, left : left + width].astype(F32)
        copies.append(pltpu.make_async_copy(buffer.at[m], out.at[at, :], semaphores.at[m]))
        copies[-1].start()
    for copy in copies:
        copy.wait()


def pairs(size, k):
    return [(i, i ^ k) for i in range(size)]


def local(
    n_narrow,
    n_wide,
    tokens,
    cotangent,
    w_query,
    w_key,
    w_value,
    w_output,
    gain_attn,
    gain_ffn,
    w_router,
    bias_table,
    expert_in,
    expert_out,
    choices,
    router_levels,
    buckets,
):
    length, width = tokens.shape
    buckets_n, heads = bias_table.shape
    experts = w_router.shape[1]
    cap = (5 * length + 4 * experts - 1) // (4 * experts)
    flat_slots = experts * cap
    direct = n_wide <= 8
    slot_counts = [cap] * (n_wide // 2) + [flat_slots // 2] if direct else [flat_slots]
    narrow_at, wide_at = lax.axis_index("narrow"), lax.axis_index("wide")
    core_ref = (wide_at % 2).reshape(1)
    shift_ref = (wide_at if direct else jnp.zeros((), jnp.int32)).reshape(1)
    w_router = w_router.T
    rows_bf = shaped((length, width))
    attn_flops = 4 * length * length * width

    def across(x, k):
        return lax.ppermute(x, "narrow", pairs(n_narrow, k))

    def along(x, k):
        return lax.ppermute(x, "wide", pairs(n_wide, k))

    (
        query,
        key,
        value,
        probs,
        mixed,
        residual,
        packed,
        *slots,
    ) = call(
        functools.partial(front_kernel, heads, cap),
        [
            rows_bf,
            rows_bf,
            rows_bf,
            shaped((heads, length, length)),
            rows_bf,
            shaped((length, width), F32),
            shaped((8 + experts, length), F32),
        ]
        + [shaped((n, 2 * width)) for n in slot_counts],
        shift_ref,
        tokens,
        w_query,
        w_key,
        w_value,
        w_output,
        cotangent,
        gain_attn,
        gain_ffn,
        w_router,
        bias_table.T,
        buckets,
        choices.reshape(1, length),
        router_levels,
        smem=1,
        early=2,
        flops=8 * length * width * width + attn_flops,
        transcendentals=heads * length * length,
    )

    quarter = flat_slots // 4
    order = (0, 2, 1, 3)
    if direct:
        per = n_wide // 4
        near = jnp.split(along(slots[-1], 1), n_wide // 2)
        parts = [jnp.concatenate([slots[i], near[i]], axis=0) for i in order]
        parts = [[along(p, 2 * i) if i else p] for i, p in zip(order, parts)]
    else:
        moved = lax.all_to_all(slots[0], "wide", split_axis=0, concat_axis=0, tiled=True)
        parts = [[moved[i * quarter : (i + 1) * quarter]] for i in range(4)]

    def gather(a, b):
        a1, b2 = across(a, 1), across(b, 2)
        a2, b1 = across(a, 2), across(b, 1)
        a3, b3 = across(a1, 2), across(b2, 1)
        return [a, b, a1, b1, a2, b2, a3, b3]

    quarters = [jnp.concatenate(part, axis=0) for part in parts]

    def hop_one(keep_a0, keep_b0, send_a, send_b, keep_b1, keep_a1):
        got_a, got_b = across(send_a, 1), across(send_b, 2)
        next_a = (keep_a1.astype(F32) + got_a[1].astype(F32)).astype(BF)
        next_b = (keep_b1.astype(F32) + got_b[1].astype(F32)).astype(BF)
        return [keep_a0, keep_b0, got_a, got_b, next_a, next_b]

    def hop_two(keep_a0, keep_b0, got_a, got_b, next_a, next_b):
        last_a, last_b = across(next_a, 2), across(next_b, 1)
        sum_a = keep_a0.astype(F32) + got_a[0].astype(F32) + last_a.astype(F32)
        sum_b = keep_b0.astype(F32) + got_b[0].astype(F32) + last_b.astype(F32)
        return [sum_a.astype(BF), sum_b.astype(BF)]

    def reduce(keep_a, send_a, keep_b, send_b):
        got_a, got_b = across(send_a, 1), across(send_b, 2)
        next_a = (keep_a[1].astype(F32) + got_a[1].astype(F32)).astype(BF)
        next_b = (keep_b[1].astype(F32) + got_b[1].astype(F32)).astype(BF)
        last_a, last_b = across(next_a, 2), across(next_b, 1)
        sum_a = keep_a[0].astype(F32) + got_a[0].astype(F32) + last_a.astype(F32)
        sum_b = keep_b[0].astype(F32) + got_b[0].astype(F32) + last_b.astype(F32)
        return sum_a.astype(BF), sum_b.astype(BF)

    w_in = expert_in.reshape(width, -1)
    w_out = expert_out.reshape(-1, width)
    units = w_in.shape[1]
    piece = shaped((2, quarter, 2 * width))
    unit_rows = shaped((4 * quarter, units))
    slot_piece = shaped((quarter, 2 * width))
    expert_flops = 2 * 8 * quarter * width * units
    def experts_of(rows):
        return call(
            expert_kernel,
            [unit_rows] * 4 + [slot_piece, slot_piece, piece, piece, slot_piece, slot_piece],
            w_in,
            *rows[:4],
            w_out,
            *rows[4:],
            early=5,
            flops=4 * expert_flops,
            transcendentals=8 * quarter * units,
        )

    def reduced(keep_a0, keep_b0, send_a, send_b, keep_b1, keep_a1):
        return reduce((keep_a0, keep_a1), send_a, (keep_b0, keep_b1), send_b)

    first = gather(*quarters[:2])
    quarters[2], quarters[3], first[3], first[4] = lax.optimization_barrier(
        (quarters[2], quarters[3], first[3], first[4])
    )
    second = gather(*quarters[2:])
    done_1, done_2 = experts_of(first), experts_of(second)
    groups = [first, second]
    kept = done_1[:4] + done_2[:4]
    h1 = hop_one(*done_1[4:])
    done_2, h1 = lax.optimization_barrier((done_2, h1))
    h2 = hop_one(*done_2[4:])
    sums = hop_two(*h1) + hop_two(*h2)
    if direct:
        sums = [sums[order.index(i)] for i in range(4)]
        returned = [sums[k // per][k % per * cap : (k % per + 1) * cap] for k in range(n_wide)]
        returned = [returned[0]] + [along(returned[k], k) for k in range(1, n_wide)]
        returned = returned[::2] + returned[1::2]
    else:
        returned = jnp.concatenate(sums, axis=0)
        returned = [lax.all_to_all(returned, "wide", split_axis=0, concat_axis=0, tiled=True)]
    grad_expert_in, grad_expert_out = call(
        expert_weights_kernel,
        [shaped(expert_in.shape, F32), shaped(expert_out.shape, F32)],
        *groups[0],
        *groups[1],
        *kept,
        flops=4 * expert_flops,
    )
    returned, grad_expert_in, grad_expert_out = lax.optimization_barrier(
        (returned, grad_expert_in, grad_expert_out)
    )

    half = width // 2
    small_rows = -(-(2 + experts + heads) // 32) * 32
    ride = small_rows if direct else 0
    layer_output, input_grad, keep_1, send_1, keep_2, send_2, small = call(
        functools.partial(backward_kernel, heads, buckets_n),
        [rows_bf, rows_bf]
        + [shaped((half + ride // 2, 2 * width))] * 2
        + [shaped((half, 2 * width))] * 2
        + [shaped((8, 128) if direct else (small_rows, width), F32)],
        core_ref,
        packed,
        gain_ffn,
        w_router,
        buckets,
        cotangent,
        residual,
        w_output,
        value,
        probs,
        key,
        query,
        mixed,
        tokens,
        w_value,
        w_query,
        w_key,
        gain_attn,
        *returned,
        smem=1,
        early=4,
        scratch=[pltpu.VMEM((small_rows, width), F32)] + [pltpu.VMEM((length, width), BF), pltpu.VMEM((length, 3 * width), BF)],
        flops=16 * length * width * width + 3 * attn_flops,
    )

    place = jnp.stack(
        [wide_at % 2, narrow_at % 2, narrow_at // 2, wide_at // 2 % 2, wide_at // 4 % 2]
    ).astype(jnp.int32)
    deeper = [2**i for i in range(3, 20) if 2**i < n_wide]

    def hop(kernel, shapes, *args):
        return call(kernel, [shaped(x) for x in shapes], place, *args, smem=1, stream=False)

    def scatter(keep, send, tail):
        own_a, send_a, own_b, send_b = hop(
            first_kernel,
            [(half // 2 + tail, width)] * 2 + [(half // 2, width)] * 2,
            keep,
            along(send, 1),
        )
        own_a, send_a, own_b, send_b = hop(
            second_kernel,
            [(half // 4 + tail, width)] * 2 + [(half // 4, width)] * 2,
            own_a,
            across(send_a, 1),
            own_b,
            across(send_b, 2),
        )
        rows = half // 8
        own, other = hop(
            join_kernel,
            [(rows + tail // 2, 2 * width)] * 2,
            own_a,
            across(send_a, 2),
            own_b,
            across(send_b, 1),
        )
        own, other = hop(
            functools.partial(columns_kernel, rows),
            [(rows + tail, width)] * 2,
            own,
            along(other, 2),
        )
        return own, along(other, 4)

    def scatter_deep(keep, send):
        own, other = hop(rows_kernel, [(half // 2, 2 * width)] * 2, keep, along(send, 1))
        own_a, send_a, own_b, send_b = hop(
            first_kernel, [(half // 4, width)] * 4, own, along(other, 2)
        )
        own_a, send_a, own_b, send_b = hop(
            second_kernel,
            [(half // 8, width)] * 4,
            own_a,
            across(send_a, 1),
            own_b,
            across(send_b, 2),
        )
        own, other = hop(
            pick_kernel,
            [(half // 8, width)] * 2,
            own_a,
            across(send_a, 2),
            own_b,
            across(send_b, 1),
        )
        return own, along(other, 4)

    def last_sum(own, got):
        rows = half // 8
        x = (own[:rows].astype(F32) + got[:rows].astype(F32)).astype(BF)
        for k in deeper:
            bit, size = wide_at // k % 2, x.shape[0] // 2
            other = lax.dynamic_slice_in_dim(x, (1 - bit) * size, size, 0)
            mine = lax.dynamic_slice_in_dim(x, bit * size, size, 0)
            x = (mine.astype(F32) + along(other, k).astype(F32)).astype(BF)
        return x

    def spread_out(x, parts):
        step = functools.partial
        for k in reversed(deeper):
            bit, far = wide_at // k % 2, along(x, k)
            x = jnp.concatenate([jnp.where(bit == 0, x, far), jnp.where(bit == 0, far, x)], axis=0)
        (x,) = hop(step(beside_kernel, 4), [(half // 8, 2 * width)], x, along(x, 4))
        a, b = hop(step(stack_kernel, 3), [(half // 4, width)] * 2, x, along(x, 2))
        a, b = call(
            double_kernel,
            [shaped((half // 2, width))] * 2,
            a,
            across(a, 2),
            b,
            across(b, 1),
            stream=False,
        )
        kernel = step(half_kernel, parts)
        (x,) = hop(kernel, [(half, 2 * width)], a, across(a, 1), b, across(b, 2))
        return x

    def finish(sources, outs=()):
        count = 2 * len(sources)
        return pl.pallas_call(
            functools.partial(finish_kernel, bool(outs), len(sources)),
            out_shape=(shaped((width, width), F32),) * count,
            in_specs=[pl.BlockSpec(memory_space=pltpu.SMEM)]
            + [pl.BlockSpec(memory_space=pltpu.VMEM)] * len(sources)
            + [pl.BlockSpec(memory_space=pl.ANY)] * len(outs),
            out_specs=(pl.BlockSpec(memory_space=pl.ANY),) * count,
            scratch_shapes=[
                pltpu.VMEM((count, half, width), F32),
                pltpu.SemaphoreType.DMA((count,)),
            ],
            input_output_aliases={1 + len(sources) + i: i for i in range(len(outs))},
            compiler_params=pltpu.CompilerParams(vmem_limit_bytes=LOW),
        )(place, *sources, *outs)

    own, got = scatter(keep_1, send_1, ride)
    part_1, part_2 = last_sum(own, got), last_sum(*scatter_deep(keep_2, send_2))
    if not direct:
        own = lax.psum(small, ("narrow", "wide"))
        got = jnp.zeros_like(own)
    small = call(
        functools.partial(small_kernel, half // 8 if direct else 0),
        [
            shaped((width,), F32),
            shaped((width,), F32),
            shaped((experts, width), F32),
            shaped((heads, buckets_n), F32),
        ],
        own,
        got,
        scratch=[pltpu.VMEM((small_rows, width), F32)],
        stream=False,
    )
    part_2, small = lax.optimization_barrier((part_2, small))
    part_1, part_2 = spread_out(part_1, 1), spread_out(part_2, 2)
    far_1, far_2 = along(part_1, 1), along(part_2, 1)
    near = finish((part_1, part_2))
    far_1, far_2, near = lax.optimization_barrier((far_1, far_2, near))
    grad_w_output, grad_w_value, grad_w_query, grad_w_key = finish((far_1, far_2), near)
    return (
        layer_output,
        input_grad,
        grad_w_query,
        grad_w_key,
        grad_w_value,
        grad_w_output,
        small[0],
        small[1],
        small[2].T,
        small[3].T,
        grad_expert_in,
        grad_expert_out,
    )


def solution(mesh):
    tokens_spec = P(("narrow", "wide"), None)
    experts_in_spec = P("wide", None, "narrow")
    experts_out_spec = P("wide", "narrow", None)
    in_specs = (
        (tokens_spec, tokens_spec)
        + (P(),) * 8
        + (experts_in_spec, experts_out_spec, tokens_spec, P(), P())
    )
    out_specs = (tokens_spec, tokens_spec) + (P(),) * 8 + (experts_in_spec, experts_out_spec)
    body = functools.partial(local, mesh.shape["narrow"], mesh.shape["wide"])
    return jax.shard_map(body, mesh=mesh, in_specs=in_specs, out_specs=out_specs, check_vma=False)
```
